32 devices in a mesh: rep: 8 (over z, y), shard: 4 (over x, core).
Axes of the slice: x: 2, y: 2, z: 4, core: 2. Of those that a mesh axis runs over, the one named last changes fastest.
Arguments:
- tokens: bfloat16 [2, 16384, 1280], P(None, ('rep', 'shard')), may hold values from -6 to 6
- cotangent: bfloat16 [2, 16384, 1280], P(None, ('rep', 'shard')), may hold values from -6 to 6
- block_map: int32 [2, 8, 4], P(None, 'rep'), may hold values from 0 to 3, each once within a row
- query_weight: bfloat16 [1280, 1280], P('shard'), may hold values from -0.15625 to 0.15625
- key_weight: bfloat16 [1280, 320], P('shard'), may hold values from -0.15625 to 0.15625
- value_weight: bfloat16 [1280, 320], P('shard'), may hold values from -0.15625 to 0.15625
- output_weight: bfloat16 [1280, 1280], P('shard'), may hold values from -1.5 to 1.5
- attention_gain: bfloat16 [1280], P('shard'), may hold values from 0.099609375 to 1.8984375
- gate_weight: bfloat16 [1280, 3584], P('shard'), may hold values from -0.15625 to 0.15625
- up_weight: bfloat16 [1280, 3584], P('shard'), may hold values from -0.15625 to 0.15625
- down_weight: bfloat16 [3584, 1280], P(None, 'shard'), may hold values from -0.09375 to 0.09375
- feed_gain: bfloat16 [1280], P('shard'), may hold values from 0.099609375 to 1.8984375
Outputs:
- layer_out: bfloat16 [2, 16384, 1280], P(None, ('rep', 'shard'))
- grad_tokens: bfloat16 [2, 16384, 1280], P(None, ('rep', 'shard'))
- grad_query: float32 [1280, 1280], P('shard')
- grad_key: float32 [1280, 320], P('shard')
- grad_value: float32 [1280, 320], P('shard')
- grad_output: float32 [1280, 1280], P('shard')
- grad_attention_gain: float32 [1280], P('shard')
- grad_gate: float32 [1280, 3584], P('shard')
- grad_up: float32 [1280, 3584], P('shard')
- grad_down: float32 [3584, 1280], P(None, 'shard')
- grad_feed_gain: float32 [1280], P('shard')
The draws below stay inside these ranges and needn't reach their ends.
Inputs may be any that keep to these rules, and one draw needn't show every extreme that they name: block_map[m, r] names each block of group r's prompt once: entry s is the block that device s of the group holds.
All inputs are finite; a program needn't handle non-finite values.
Results may differ from the reference program's by a relative error of at most 0.023.
Values may be sent and summed in bfloat16 or wider, within the bound.
No kernel may reach another device: no remote copies, remote signals or barrier semaphores. Data moves between devices by JAX's collectives and lax.ppermute only.
A program may use at most 320 MiB of HBM per device.

```python
import jax
import jax.numpy as jnp
from jax import lax

D = 1280
HEADS = 20
KV_HEADS = 5
HEAD_DIM = 64
FF = 3584
PDEV = 256
MICRO = 2
TOK_DEV = 512
PROMPT = 1024
TOKENS = 16384
N_REP = 8
N_SHARD = 4


def steps_of(rng, dims, split, least, top_value):
    loudness, own = 1.0, jax.random.fold_in(rng, 6)
    for position, blocks in split:
        steps = jnp.exp(jax.random.uniform(jax.random.fold_in(own, position), (blocks,), jnp.float32, least / len(split), top_value / len(split)))
        loudness = loudness * jnp.repeat(steps, dims[position] // blocks).reshape([-1 if axis == position else 1 for axis in range(len(dims))])
    return loudness


def centred(own_key, extent, width, most, pieces=(), held_as=jnp.bfloat16):
    loudness = steps_of(own_key, extent, pieces, -0.22, 0.18) if pieces else 1.0
    values = jax.random.normal(own_key, extent, jnp.float32) * width * loudness
    return jnp.minimum(jnp.maximum(values, -most), most).astype(held_as)


def setup_inputs(seed: int = 0) -> dict:
    seeds = jax.random.split(jax.random.key(seed), 13)
    return {
        "tokens": centred(seeds[0], (MICRO, TOKENS, D), 1.0, 6.0, ((1, 32),)),
        "cotangent": centred(seeds[1], (MICRO, TOKENS, D), 1.0, 6.0, ((1, 32),)),
        "block_map": jax.vmap(lambda own: jax.random.permutation(own, N_SHARD))(jax.random.split(seeds[2], MICRO * N_REP)).reshape((MICRO, N_REP, N_SHARD)).astype(jnp.int32),
        "query_weight": centred(seeds[3], (D, HEADS * HEAD_DIM), D ** -0.5, 0.15625, ((0, 4),)),
        "key_weight": centred(seeds[4], (D, KV_HEADS * HEAD_DIM), D ** -0.5, 0.15625, ((0, 4),)),
        "value_weight": centred(seeds[5], (D, KV_HEADS * HEAD_DIM), D ** -0.5, 0.15625, ((0, 4),)),
        "output_weight": centred(seeds[6], (HEADS * HEAD_DIM, D), 16 ** -0.5, 1.5, ((0, 4),)),
        "attention_gain": jnp.clip(1.0 + 0.18 * jax.random.normal(seeds[7], (D,), jnp.float32), 0.099609375, 1.8984375).astype(jnp.bfloat16),
        "gate_weight": centred(seeds[8], (D, FF), D ** -0.5, 0.15625, ((0, 4),)),
        "up_weight": centred(seeds[9], (D, FF), D ** -0.5, 0.15625, ((0, 4),)),
        "down_weight": centred(seeds[10], (FF, D), FF ** -0.5, 0.09375, ((1, 4),)),
        "feed_gain": jnp.clip(1.0 + 0.18 * jax.random.normal(seeds[11], (D,), jnp.float32), 0.099609375, 1.8984375).astype(jnp.bfloat16),
    }


EPS = 1e-05
NEG = -1e+30
HIGH = lax.Precision.HIGHEST

@jax.custom_vjp
def low(v):
    return lax.optimization_barrier(v.astype(jnp.bfloat16)).astype(jnp.float32)

@jax.custom_vjp
def low_back(v):
    return v

def low_keep(v):
    return (low(v), None)

def low_pass(kept, grad):
    return (grad,)

def back_keep(v):
    return (v, None)

def back_low(kept, grad):
    return (low(grad),)
low.defvjp(low_keep, low_pass)
low_back.defvjp(back_keep, back_low)

def rms_scale(field, gain):
    return field * lax.rsqrt(lax.optimization_barrier(jnp.mean(field * field, axis=-1, keepdims=True)) + EPS) * gain

def rotate(field, place, sense):
    half = field.shape[-1] // 2
    freq = jnp.exp(jnp.arange(half, dtype=jnp.float32) * (-2.0 * jnp.log(10000.0) / field.shape[-1]))
    angle = place.astype(jnp.float32)[:, None] * freq[None, :] * sense
    cosine = jnp.cos(angle)[:, None, :]
    sine = jnp.sin(angle)[:, None, :]
    first = field[..., :half]
    second = field[..., half:]
    return jnp.concatenate([first * cosine - second * sine, second * cosine + first * sine], axis=-1)

def attention(query, keys, values, place, segment):
    count = query.shape[0]
    size = min(512, count)
    group = HEADS // KV_HEADS
    scale = HEAD_DIM ** (-0.5)

    def block(item):
        part, part_place, part_segment = item
        raw = jnp.einsum('qkgd,tkd->kgqt', part, keys, precision=HIGH)
        logits = low_back(raw) * scale
        allowed = (place[None, :] <= part_place[:, None]) & ((segment[None, :] == 0) | (segment[None, :] == part_segment[:, None]))
        logits = jnp.where(allowed, logits, NEG)
        top = lax.optimization_barrier(jnp.max(logits, axis=-1, keepdims=True))
        terms = jnp.exp(logits - top)
        weights = terms / lax.optimization_barrier(jnp.sum(terms, axis=-1, keepdims=True))
        mixed = jnp.einsum('kgqt,tkd->qkgd', low(weights), values, precision=HIGH)
        return mixed.reshape(part.shape[0], HEADS * HEAD_DIM)
    parts = query.reshape(count // size, size, KV_HEADS, group, HEAD_DIM)
    result = lax.map(jax.checkpoint(block), (parts, place.reshape(-1, size), segment.reshape(-1, size)))
    return result.reshape(count, HEADS * HEAD_DIM)

def group_forward(source, params, place, segment):
    query_weight, key_weight, value_weight, output_weight, attention_gain, gate_weight, up_weight, down_weight, feed_gain = params
    count = source.shape[0]
    normed_one = low(rms_scale(source, attention_gain))
    query = low_back(jnp.dot(normed_one, query_weight, precision=HIGH)).reshape(count, HEADS, HEAD_DIM)
    query = low(rotate(query, place, 1.0)).reshape(count, KV_HEADS, HEADS // KV_HEADS, HEAD_DIM)
    keys = low_back(jnp.dot(normed_one, key_weight, precision=HIGH)).reshape(count, KV_HEADS, HEAD_DIM)
    keys = low(rotate(keys, place, 1.0))
    values = low(low_back(jnp.dot(normed_one, value_weight, precision=HIGH))).reshape(count, KV_HEADS, HEAD_DIM)
    mixed = low(low_back(attention(query, keys, values, place, segment)))
    middle = source + low_back(jnp.dot(mixed, output_weight, precision=HIGH))
    normed_two = low(rms_scale(middle, feed_gain))
    gate = low_back(jnp.dot(normed_two, gate_weight, precision=HIGH))
    upper = low_back(jnp.dot(normed_two, up_weight, precision=HIGH))
    hidden = low(jax.nn.silu(gate) * upper)
    return middle + low_back(jnp.dot(hidden, down_weight, precision=HIGH))

def layout(block_map):
    groups = MICRO * N_REP
    blocks = block_map.reshape(groups, N_SHARD)
    within = jnp.arange(TOK_DEV, dtype=jnp.int32)
    is_prompt = within < PDEV
    prompt_place = blocks[:, :, None] * PDEV + within[None, None, :]
    later_place = jnp.broadcast_to((PROMPT - PDEV + within)[None, None, :], prompt_place.shape)
    place = jnp.where(is_prompt[None, None, :], prompt_place, later_place)
    device = jnp.arange(N_SHARD, dtype=jnp.int32)
    segment = jnp.where(is_prompt[None, None, :], jnp.zeros_like(prompt_place), jnp.broadcast_to(device[None, :, None] + 1, prompt_place.shape))
    return (place.reshape(groups, N_SHARD * TOK_DEV), segment.reshape(groups, N_SHARD * TOK_DEV))

def whole_forward(sources, params, places, segments):

    def visit(carry, item):
        return (carry, group_forward(item[0], params, item[1], item[2]))
    _, result = lax.scan(jax.checkpoint(visit), None, (sources, places, segments))
    return result

def reference(tokens, cotangent, block_map, query_weight, key_weight, value_weight, output_weight, attention_gain, gate_weight, up_weight, down_weight, feed_gain):
    groups = MICRO * N_REP
    span = N_SHARD * TOK_DEV
    sources = tokens.astype(jnp.float32).reshape(groups, span, D)
    places, segments = layout(block_map)
    params = (query_weight.astype(jnp.float32), key_weight.astype(jnp.float32), value_weight.astype(jnp.float32), output_weight.astype(jnp.float32), attention_gain.astype(jnp.float32), gate_weight.astype(jnp.float32), up_weight.astype(jnp.float32), down_weight.astype(jnp.float32), feed_gain.astype(jnp.float32))
    result, pull = jax.vjp(lambda s, p: whole_forward(s, p, places, segments), sources, params)
    grad_source, grads = pull(cotangent.astype(jnp.float32).reshape(groups, span, D))
    return (result.reshape(MICRO, TOKENS, D).astype(jnp.bfloat16), grad_source.reshape(MICRO, TOKENS, D).astype(jnp.bfloat16), grads[0], grads[1], grads[2], grads[3], grads[4], grads[5], grads[6], grads[7], grads[8])
```

```python
import jax
import jax.numpy as jnp
from jax import lax
from jax.experimental import pallas as pl
from jax.experimental.pallas import tpu as pltpu
from jax.sharding import PartitionSpec as P

HEADS = 20
KV_HEADS = 5
HEAD_DIM = 64
GROUP = HEADS // KV_HEADS
EPS = 1e-05
NEG = -1e30
F32 = jnp.float32
BF = jnp.bfloat16
VMEM_BYTES = 62 * 1024 * 1024


def mm(left, right):
    return jnp.dot(left, right, preferred_element_type=F32)


def ein(spec, left, right):
    return jnp.einsum(spec, left, right, preferred_element_type=F32)

def attend_kernel(gap_ref, q_ref, *refs, m, blocks):
    k_ref, v_ref, refs = refs[:blocks], refs[blocks : 2 * blocks], refs[2 * blocks :]
    kl_ref, vl_ref, a_ref, lse_ref = refs
    dim, blk = kl_ref.shape
    keys = jnp.concatenate([k_ref[j][...].T for j in range(blocks)] + [kl_ref[...].T], axis=0)
    ones = jnp.ones((16, (blocks+1)*blk), BF)
    vals = jnp.concatenate([jnp.concatenate([v_ref[j][...] for j in range(blocks)] + [vl_ref[...]], axis=1), ones], axis=0)
    diff = lax.broadcasted_iota(jnp.int32,(blk,blk),0) - lax.broadcasted_iota(jnp.int32,(blk,blk),1)
    n = blocks*blk
    for g in range(GROUP):
        for half in (0,1):
            q = q_ref[g*dim:(g+1)*dim, half*blk:(half+1)*blk]
            if half == 0:
                s = mm(keys[:n], q)
                s = jnp.concatenate([jnp.where(diff <= gap_ref[m, j], s[j*blk:(j+1)*blk], NEG) for j in range(blocks)], axis=0)
                vv = vals[:, :n]
            else:
                s = mm(keys, q)
                s = jnp.concatenate([s[:n], jnp.where(diff <= 0, s[n:], NEG)], axis=0)
                vv = vals
            top = jnp.max(s, axis=0, keepdims=True)
            p = jnp.exp(s - top).astype(BF)
            o = mm(vv, p)
            total = o[dim:dim+1]
            a_ref[g*dim:(g+1)*dim, half*blk:(half+1)*blk] = (o[:dim] / total).astype(BF)
            lse_ref[0, g:g+1, half*blk:(half+1)*blk] = top + jnp.log(total)

def attend(gap, qT, pairs, ownT, micro, m):
    blocks, blk = len(pairs), pairs[0].shape[1]
    rows = qT.shape[1] // micro
    return pl.pallas_call(
        lambda *refs: attend_kernel(*refs, m=m, blocks=blocks),
        grid=(KV_HEADS,),
        in_specs=[
            pl.BlockSpec(memory_space=pltpu.SMEM),
            pl.BlockSpec((GROUP * HEAD_DIM, rows), lambda h: (h, m)),
        ]
        + [pl.BlockSpec((HEAD_DIM, blk), lambda h: (h, 0))] * blocks
        + [pl.BlockSpec((HEAD_DIM, blk), lambda h: (KV_HEADS + h, 0))] * blocks
        + [
            pl.BlockSpec((HEAD_DIM, blk), lambda h: (h, 2 * m + 1)),
            pl.BlockSpec((HEAD_DIM, blk), lambda h: (KV_HEADS + h, 2 * m + 1)),
        ],
        out_specs=[
            pl.BlockSpec((GROUP * HEAD_DIM, rows), lambda h: (h, 0)),
            pl.BlockSpec((1, GROUP, rows), lambda h: (h, 0, 0)),
        ],
        out_shape=[
            jax.ShapeDtypeStruct((qT.shape[0], rows), BF),
            jax.ShapeDtypeStruct((KV_HEADS, GROUP, rows), F32),
        ],
        compiler_params=pltpu.CompilerParams(vmem_limit_bytes=VMEM_BYTES),
        cost_estimate=pl.CostEstimate(flops=3 * 10**10, bytes_accessed=5 * 10**6, transcendentals=12 * 10**6),
        name="attend",
    )(gap, qT, *pairs, *pairs, ownT, ownT)


def back_kernel(gap_ref, cos_ref, sin_ref, kcos_ref, ksin_ref, q_ref, a_ref, da_ref, lse_ref, *refs, m, blocks):
    k_ref, v_ref, refs = refs[:blocks], refs[blocks : 2 * blocks], refs[2 * blocks :]
    kl_ref, vl_ref, dq_ref, terms_ref, own_ref, p_scr, ds_scr = refs
    dim, blk = kl_ref.shape
    n = blocks*blk
    keysT = jnp.concatenate([k_ref[j][...] for j in range(blocks)] + [kl_ref[...]], axis=1)
    keys = jnp.concatenate([k_ref[j][...].T for j in range(blocks)] + [kl_ref[...].T], axis=0)
    vals = jnp.concatenate([v_ref[j][...].T for j in range(blocks)] + [vl_ref[...].T], axis=0)
    diff = lax.broadcasted_iota(jnp.int32,(blk,blk),0) - lax.broadcasted_iota(jnp.int32,(blk,blk),1)
    dk = None; dv = None
    for half in (0,1):
        span = n if half == 0 else n + blk
        cols = slice(half*blk, (half+1)*blk)
        qn = []; dan = []
        for g in range(GROUP):
            rows = slice(g*dim, (g+1)*dim)
            q = q_ref[rows, cols]; da = da_ref[rows, cols]
            qn.append(q.T); dan.append(da.T)
            delta = jnp.sum(da.astype(F32) * a_ref[rows, cols].astype(F32), axis=0, keepdims=True)
            lse = lse_ref[0, g:g+1, cols]
            s = mm(keys[:span], q)
            if half == 0:
                s = jnp.concatenate([jnp.where(diff <= gap_ref[m, j], s[j*blk:(j+1)*blk], NEG) for j in range(blocks)], axis=0)
            else:
                s = jnp.concatenate([s[:n], jnp.where(diff <= 0, s[n:], NEG)], axis=0)
            p = jnp.exp(s - lse)
            dp = mm(vals[:span], da)
            ds = (p * (dp - delta)).astype(BF)
            p_scr[:span, g*blk:(g+1)*blk] = p.astype(BF)
            ds_scr[:span, g*blk:(g+1)*blk] = ds
            dq = mm(keysT[:, :span], ds) * (HEAD_DIM ** -0.5)
            c = cos_ref[:, cols]; sn = sin_ref[:, cols]
            first = dq[:dim//2]; second = dq[dim//2:]
            dq_ref[rows, cols] = jnp.concatenate([first*c + second*sn, second*c - first*sn], axis=0).astype(BF)
        qn = jnp.concatenate(qn, axis=0); dan = jnp.concatenate(dan, axis=0)
        dkh = mm(ds_scr[:span], qn); dvh = mm(p_scr[:span], dan)
        if half == 0:
            dk, dv = dkh, dvh
        else:
            dk = jnp.concatenate([dk + dkh[:n], dkh[n:]], axis=0)
            dv = jnp.concatenate([dv + dvh[:n], dvh[n:]], axis=0)
    half = dim // 2
    for j in range(blocks + 1):
        cols = slice(j * blk, (j + 1) * blk)
        turned = dk[cols].T
        first, second = turned[:half], turned[half:]
        c, sn = kcos_ref[:, cols], ksin_ref[:, cols]
        turned = jnp.concatenate([first * c + second * sn, second * c - first * sn], axis=0).astype(BF)
        value = dv[cols].T.astype(BF)
        if j < blocks:
            terms_ref[j, 0, 0], terms_ref[j, 1, 0] = turned, value
        else:
            own_ref[0, 0], own_ref[1, 0] = turned, value


def attend_back(gap, cosT, sinT, kcos, ksin, qT, aT, daT, lse, pairs, ownT, micro, m, low, high):
    blocks, blk = len(pairs), pairs[0].shape[1]
    rows = qT.shape[1] // micro
    count = high - low
    query = pl.BlockSpec((GROUP * HEAD_DIM, rows), lambda h: (low + h, m))
    part = pl.BlockSpec((GROUP * HEAD_DIM, rows), lambda h: (low + h, 0))
    table = pl.BlockSpec((HEAD_DIM // 2, rows), lambda h: (0, m))
    keys = pl.BlockSpec((HEAD_DIM // 2, (blocks + 1) * blk), lambda h: (0, m))
    return pl.pallas_call(
        lambda *refs: back_kernel(*refs, m=m, blocks=blocks),
        grid=(count,),
        in_specs=[
            pl.BlockSpec(memory_space=pltpu.SMEM),
            table,
            table,
            keys,
            keys,
            query,
            part,
            part,
            pl.BlockSpec((1, GROUP, rows), lambda h: (low + h, 0, 0)),
        ]
        + [pl.BlockSpec((HEAD_DIM, blk), lambda h: (low + h, 0))] * blocks
        + [pl.BlockSpec((HEAD_DIM, blk), lambda h: (KV_HEADS + low + h, 0))] * blocks
        + [
            pl.BlockSpec((HEAD_DIM, blk), lambda h: (low + h, 2 * m + 1)),
            pl.BlockSpec((HEAD_DIM, blk), lambda h: (KV_HEADS + low + h, 2 * m + 1)),
        ],
        out_specs=[
            pl.BlockSpec((GROUP * HEAD_DIM, rows), lambda h: (h, 0)),
            pl.BlockSpec((blocks, 2, 1, HEAD_DIM, blk), lambda h: (0, 0, h, 0, 0)),
            pl.BlockSpec((2, 1, HEAD_DIM, blk), lambda h: (0, h, 0, 0)),
        ],
        out_shape=[
            jax.ShapeDtypeStruct((count * GROUP * HEAD_DIM, rows), BF),
            jax.ShapeDtypeStruct((blocks, 2, count, HEAD_DIM, blk), BF),
            jax.ShapeDtypeStruct((2, count, HEAD_DIM, blk), BF),
        ],
        scratch_shapes=[pltpu.VMEM(((blocks + 1) * blk, GROUP * blk), BF)] * 2,
        compiler_params=pltpu.CompilerParams(vmem_limit_bytes=VMEM_BYTES),
        cost_estimate=pl.CostEstimate(flops=8 * 10**9 * count, bytes_accessed=10**6 * count, transcendentals=0),
        name="attend_back",
    )(gap, cosT, sinT, kcos, ksin, qT, aT, daT, lse, *pairs, *pairs, ownT, ownT)


def nt(left, right):
    return lax.dot_general(left, right, (((1,), (1,)), ((), ())), preferred_element_type=F32)


def tn(left, right):
    return lax.dot_general(left, right, (((0,), (0,)), ((), ())), preferred_element_type=F32)


def project_kernel(row_ref, ht_ref, cos_ref, sin_ref, *refs, pieces, turned, scale):
    parts, (out_ref, whole_ref) = refs[:pieces], refs[pieces:]
    for i, part in enumerate(parts):
        whole_ref[pl.ds(pl.multiple_of(row_ref[i], 16), part.shape[0]), :] = part[...]
    raw = tn(whole_ref[...], ht_ref[...])
    half = HEAD_DIM // 2
    for head in range(raw.shape[0] // HEAD_DIM):
        at = head * HEAD_DIM
        if head < turned:
            first, second = raw[at : at + half], raw[at + half : at + HEAD_DIM]
            cosine, sine = cos_ref[...], sin_ref[...]
            out_ref[at : at + half] = (first * cosine - second * sine).astype(BF) * BF(scale)
            out_ref[at + half : at + HEAD_DIM] = (second * cosine + first * sine).astype(BF) * BF(scale)
        else:
            out_ref[at : at + HEAD_DIM] = raw[at : at + HEAD_DIM].astype(BF)


def project(starts, ht, cosine, sine, pieces, tile, turned, scale):
    width, tokens = ht.shape
    count = pieces[0].shape[1]
    table = pl.BlockSpec(cosine.shape, lambda i: (0, 0))
    return pl.pallas_call(
        lambda *refs: project_kernel(*refs, pieces=len(pieces), turned=turned, scale=scale),
        grid=(count // tile,),
        in_specs=[
            pl.BlockSpec(memory_space=pltpu.SMEM),
            pl.BlockSpec((width, tokens), lambda i: (0, 0)),
            table,
            table,
        ]
        + [pl.BlockSpec((piece.shape[0], tile), lambda i: (0, i)) for piece in pieces],
        out_specs=[
            pl.BlockSpec((tile, tokens), lambda i: (i, 0)),
            pl.BlockSpec((width, tile), lambda i: (0, i)),
        ],
        out_shape=[
            jax.ShapeDtypeStruct((count, tokens), BF),
            jax.ShapeDtypeStruct((width, count), BF),
        ],
        compiler_params=pltpu.CompilerParams(vmem_limit_bytes=VMEM_BYTES),
        cost_estimate=pl.CostEstimate(
            flops=2 * tokens * width * count, bytes_accessed=6 * width * count, transcendentals=0
        ),
        name="project",
    )(starts, ht, cosine, sine, *pieces)


def feed_kernel(row_ref, left_ref, *refs, sets, pieces, groups, split, step):
    hs, cs, refs = refs[:sets], refs[sets : 2 * sets], refs[2 * sets :]
    parts, refs = refs[:pieces], refs[pieces:]
    count = groups * len(split)
    grads, refs = refs[:count], refs[count:]
    backs, refs = refs[:sets], refs[sets:]
    hid_ref, down_ref, ht_ref, ct_ref, gate_ref, up_ref, dg_ref, dw_ref, acc_ref = refs
    tokens, width = hs[0].shape
    at = pl.program_id(0)

    @pl.when(at == 0)
    def _():
        for i in range(sets):
            ht_ref[:, i * tokens : (i + 1) * tokens] = hs[i][...].T
            ct_ref[:, i * tokens : (i + 1) * tokens] = cs[i][...].T
        acc_ref[...] = jnp.zeros_like(acc_ref)

    for k, whole in enumerate((gate_ref, up_ref, down_ref)):
        for i, part in enumerate(parts):
            whole[pl.ds(pl.multiple_of(row_ref[i], 16), part.shape[1]), :] = part[k]
    for i in range(sets):
        for b in range(0, tokens, step):
            rows, to = pl.ds(b, step), pl.ds(i * tokens + b, step)
            gate = mm(hs[i][rows, :], gate_ref[...])
            upper = mm(hs[i][rows, :], up_ref[...])
            grad = mm(cs[i][rows, :], down_ref[...])
            sigma = jax.nn.sigmoid(gate)
            silu = gate * sigma
            hid_ref[to, :] = (silu * upper).astype(BF)
            dg_ref[to, :] = (grad * upper * (sigma + silu * (1.0 - sigma))).astype(BF)
            dw_ref[to, :] = (grad * silu).astype(BF)
    times = ((ht_ref, dg_ref), (ht_ref, dw_ref), (ct_ref, hid_ref))
    for i in range(groups):
        for j, names in enumerate(split):
            out = grads[i * len(split) + j]
            rows = pl.ds(pl.multiple_of(left_ref[i], 16), out.shape[1])
            for at_name, name in enumerate(names):
                left, right = times[name]
                out[at_name] = mm(left[rows, :], right[...]).astype(BF)
    for b in range(0, sets * tokens, step):
        rows = pl.ds(b, step)
        acc_ref[rows, :] += nt(dg_ref[rows, :], gate_ref[...]) + nt(dw_ref[rows, :], up_ref[...])

    @pl.when(at == pl.num_programs(0) - 1)
    def _():
        for i, back in enumerate(backs):
            back[...] = acc_ref[pl.ds(i * tokens, tokens), :].astype(BF)


def feed(starts, left_starts, hs, cs, parts, sizes, rows, split=((0, 1, 2),), tile=256, step=256):
    sets = len(hs)
    tokens, width = rows, hs[0][0].shape[1]
    hidden = parts[0].shape[2]
    one = pl.Buffered(1)
    back = pl.BlockSpec((tokens, width), lambda i: (0, 0), pipeline_mode=one)
    toks = [pl.BlockSpec((tokens, width), lambda i, at=at: (at, 0), pipeline_mode=one) for _, at in hs + cs]
    smem = pl.BlockSpec(memory_space=pltpu.SMEM)
    counts = [(len(names), size) for size in sizes for names in split]
    grad_specs = [pl.BlockSpec((count, size, tile), lambda i: (0, 0, i)) for count, size in counts]
    grad_shapes = [jax.ShapeDtypeStruct((count, size, hidden), BF) for count, size in counts]
    results = pl.pallas_call(
        lambda *refs: feed_kernel(*refs, sets=sets, pieces=len(parts), groups=len(sizes), split=split, step=step),
        grid=(hidden // tile,),
        in_specs=[smem, smem]
        + toks
        + [pl.BlockSpec((3, part.shape[1], tile), lambda i: (0, 0, i)) for part in parts],
        out_specs=grad_specs
        + [back] * sets
        + [pl.BlockSpec((sets * tokens, tile), lambda i: (0, i)), pl.BlockSpec((width, tile), lambda i: (0, i))],
        out_shape=grad_shapes
        + [jax.ShapeDtypeStruct((tokens, width), BF)] * sets
        + [jax.ShapeDtypeStruct((sets * tokens, hidden), BF), jax.ShapeDtypeStruct((width, hidden), BF)],
        scratch_shapes=[pltpu.VMEM((width, sets * tokens), BF)] * 2
        + [pltpu.VMEM((width, tile), BF)] * 2
        + [pltpu.VMEM((sets * tokens, tile), BF)] * 2
        + [pltpu.VMEM((sets * tokens, width), F32)],
        compiler_params=pltpu.CompilerParams(vmem_limit_bytes=VMEM_BYTES),
        cost_estimate=pl.CostEstimate(
            flops=16 * sets * tokens * width * hidden,
            bytes_accessed=14 * width * hidden + 12 * sets * tokens * width,
            transcendentals=sets * tokens * hidden,
        ),
        name="feed",
    )(starts, left_starts, *[h for h, _ in hs], *[c for c, _ in cs], *parts)
    count = len(grad_specs)
    return results[:count], results[count : count + sets], results[-2], results[-1]


def prepare_kernel(x_ref, gain_ref, ht_ref):
    source = x_ref[...].astype(F32)
    scale = lax.rsqrt(jnp.mean(source * source, axis=-1, keepdims=True) + EPS)
    ht_ref[...] = (source * scale * gain_ref[...]).astype(BF).T


def prepare(x, gain, tile=256):
    tokens, width = x.shape
    return pl.pallas_call(
        prepare_kernel,
        grid=(tokens // tile,),
        in_specs=[pl.BlockSpec((tile, width), lambda i: (i, 0)), pl.BlockSpec((1, width), lambda i: (0, 0))],
        out_specs=pl.BlockSpec((width, tile), lambda i: (0, i)),
        out_shape=jax.ShapeDtypeStruct((width, tokens), BF),
        compiler_params=pltpu.CompilerParams(vmem_limit_bytes=VMEM_BYTES),
        cost_estimate=pl.CostEstimate(flops=0, bytes_accessed=6 * 10**6, transcendentals=0),
        name="prepare",
    )(x, gain)


def merge_kernel(row_ref, at_ref, x_ref, gain_ref, *refs, pieces):
    if pieces == 1:
        whole_ref, mid_ref, h_ref = refs
    else:
        parts, (mid_ref, h_ref, whole_ref) = refs[:pieces], refs[pieces:]
        for i, part in enumerate(parts):
            whole_ref[pl.ds(pl.multiple_of(row_ref[i], 16), part.shape[0]), :] = part[...]
    middle = x_ref[...].astype(F32) + tn(at_ref[...], whole_ref[...])
    scale = lax.rsqrt(jnp.mean(middle * middle, axis=-1, keepdims=True) + EPS)
    mid_ref[...] = middle
    h_ref[...] = (middle * scale * gain_ref[...]).astype(BF)


def merge(starts, at, x, gain, pieces):
    head_width, tokens = at.shape
    width = x.shape[1]
    row = pl.BlockSpec((tokens, width), lambda i: (0, 0))
    outs = [row, row]
    shapes = [jax.ShapeDtypeStruct((tokens, width), F32), jax.ShapeDtypeStruct((tokens, width), BF)]
    if len(pieces) > 1:
        outs.append(pl.BlockSpec((head_width, width), lambda i: (0, 0)))
        shapes.append(jax.ShapeDtypeStruct((head_width, width), BF))
    return pl.pallas_call(
        lambda *refs: merge_kernel(*refs, pieces=len(pieces)),
        grid=(1,),
        in_specs=[
            pl.BlockSpec(memory_space=pltpu.SMEM),
            pl.BlockSpec((head_width, tokens), lambda i: (0, 0)),
            row,
            pl.BlockSpec((1, width), lambda i: (0, 0)),
        ]
        + [pl.BlockSpec(piece.shape, lambda i: (0, 0)) for piece in pieces],
        out_specs=outs,
        out_shape=shapes,
        compiler_params=pltpu.CompilerParams(vmem_limit_bytes=VMEM_BYTES),
        cost_estimate=pl.CostEstimate(
            flops=2 * tokens * width * head_width, bytes_accessed=16 * 10**6, transcendentals=0
        ),
        name="merge",
    )(starts, at, x, gain, *pieces)


def unmerge_kernel(mid_ref, c_ref, gain_ref, whole_ref, *refs):
    backs, (dmid_ref, da_ref) = refs[:-2], refs[-2:]
    middle = mid_ref[...]
    scale = lax.rsqrt(jnp.mean(middle * middle, axis=-1, keepdims=True) + EPS)
    unit = middle * scale
    grad = backs[0][...].astype(F32)
    for back in backs[1:]:
        grad = grad + back[...].astype(F32)
    weighted = grad * gain_ref[...]
    mean = jnp.mean(weighted * unit, axis=-1, keepdims=True)
    dmid = (c_ref[...].astype(F32) + scale * (weighted - unit * mean)).astype(BF)
    dmid_ref[...] = dmid
    da_ref[...] = nt(whole_ref[...], dmid).astype(BF)


def unmerge(mid, c, gain, whole, backs, tile=256):
    tokens, width = mid.shape
    head_width = whole.shape[0]
    row = pl.BlockSpec((tile, width), lambda i: (i, 0))
    return pl.pallas_call(
        unmerge_kernel,
        grid=(tokens // tile,),
        in_specs=[
            row,
            row,
            pl.BlockSpec((1, width), lambda i: (0, 0)),
            pl.BlockSpec((head_width, width), lambda i: (0, 0)),
        ]
        + [row] * len(backs),
        out_specs=[row, pl.BlockSpec((head_width, tile), lambda i: (0, i))],
        out_shape=[
            jax.ShapeDtypeStruct((tokens, width), BF),
            jax.ShapeDtypeStruct((head_width, tokens), BF),
        ],
        compiler_params=pltpu.CompilerParams(vmem_limit_bytes=VMEM_BYTES),
        cost_estimate=pl.CostEstimate(
            flops=2 * tokens * width * head_width, bytes_accessed=16 * 10**6, transcendentals=0
        ),
        name="unmerge",
    )(mid, c, gain, whole, *backs)


def terms_kernel(left_ref, *refs, count, turned):
    lefts, rights, outs = refs[:count], refs[count : 2 * count], refs[2 * count :]
    times = nt if turned else mm
    for i, out in enumerate(outs):
        rows = pl.ds(pl.multiple_of(left_ref[i], 16), out.shape[0])
        total = times(lefts[0][rows, :], rights[0][...])
        for left, right in zip(lefts[1:], rights[1:]):
            total = total + times(left[rows, :], right[...])
        out[...] = total.astype(BF)


def grad_terms(left_starts, lefts, rights, turned, size, tile):
    columns = rights[0].shape[0 if turned else 1]
    span = rights[0].shape[1 if turned else 0]
    count = left_starts.shape[0]
    if turned:
        right_specs = [pl.BlockSpec((tile, span), lambda i: (i, 0)) for _ in rights]
    else:
        right_specs = [pl.BlockSpec((span, tile), lambda i: (0, i)) for _ in rights]
    left_specs = [pl.BlockSpec((left.shape[0], span), lambda i, at=at: (0, at)) for left, at in lefts]
    return pl.pallas_call(
        lambda *refs: terms_kernel(*refs, count=len(lefts), turned=turned),
        grid=(columns // tile,),
        in_specs=[pl.BlockSpec(memory_space=pltpu.SMEM)] + left_specs + right_specs,
        out_specs=[pl.BlockSpec((size, tile), lambda i: (0, i))] * count,
        out_shape=[jax.ShapeDtypeStruct((size, columns), BF)] * count,
        compiler_params=pltpu.CompilerParams(vmem_limit_bytes=VMEM_BYTES),
        cost_estimate=pl.CostEstimate(
            flops=2 * len(lefts) * span * columns * size * count, bytes_accessed=8 * 10**6, transcendentals=0
        ),
        name="grad_terms",
    )(left_starts, *[left for left, _ in lefts], *rights)


def joint_kernel(left_ref, *refs, plan, sizes, outs):
    refs, outs = refs[:-outs], refs[-outs:]
    for i, out in enumerate(outs):
        rows = pl.ds(pl.multiple_of(left_ref[i], 16), out.shape[0])
        column = 0
        for steps, count in zip(plan, sizes):
            total = 0.0
            for left, at, right, index in steps:
                value = refs[right][...] if index is None else refs[right][index]
                total = total + nt(refs[left][rows, at : at + value.shape[1]], value)
            out[:, column : column + count] = total.astype(BF)
            column += count


def joint_terms(left_starts, arrays, plan, sizes, size):
    whole = [pl.BlockSpec(array.shape, lambda i, n=array.ndim: (0,) * n) for array in arrays]
    outs = left_starts.shape[0]
    return pl.pallas_call(
        lambda *refs: joint_kernel(*refs, plan=plan, sizes=sizes, outs=outs),
        grid=(1,),
        in_specs=[pl.BlockSpec(memory_space=pltpu.SMEM)] + whole,
        out_specs=[pl.BlockSpec((size, sum(sizes)), lambda i: (0, 0))] * outs,
        out_shape=[jax.ShapeDtypeStruct((size, sum(sizes)), BF)] * outs,
        compiler_params=pltpu.CompilerParams(vmem_limit_bytes=VMEM_BYTES),
        cost_estimate=pl.CostEstimate(flops=6 * 10**9, bytes_accessed=14 * 10**6, transcendentals=0),
        name="joint_terms",
    )(left_starts, *arrays)


def output_kernel(*refs, parts, added):
    hids, downs, adds, out_ref = refs[:parts], refs[parts : 2 * parts], refs[2 * parts : -1], refs[-1]
    total = nt(hids[0][...], downs[0][...])
    for hid, down in zip(hids[1:], downs[1:]):
        total = total + nt(hid[...], down[...])
    for add in adds:
        total = total + add[...].astype(F32)
    out_ref[...] = total.astype(BF)


def output(hids, downs, adds, first, tokens, tile=512):
    width = downs[0].shape[0]
    row = pl.BlockSpec((tile, width), lambda i: (i, 0))
    skip = first // tile
    return pl.pallas_call(
        lambda *refs: output_kernel(*refs, parts=len(hids), added=len(adds)),
        grid=(tokens // tile,),
        in_specs=[pl.BlockSpec((tile, hid.shape[1]), lambda i: (skip + i, 0)) for hid in hids]
        + [pl.BlockSpec(down.shape, lambda i: (0, 0)) for down in downs]
        + [row] * len(adds),
        out_specs=row,
        out_shape=jax.ShapeDtypeStruct((tokens, width), BF),
        compiler_params=pltpu.CompilerParams(vmem_limit_bytes=VMEM_BYTES),
        cost_estimate=pl.CostEstimate(
            flops=2 * tokens * width * sum(hid.shape[1] for hid in hids), bytes_accessed=16 * 10**6, transcendentals=0
        ),
        name="output",
    )(*hids, *downs, *adds)


def finish_kernel(x_ref, gain_ref, dmid_ref, dq_ref, dp_ref, query_ref, pair_ref, out_ref):
    source = x_ref[...].astype(F32)
    scale = lax.rsqrt(jnp.mean(source * source, axis=-1, keepdims=True) + EPS)
    unit = source * scale
    grad = (mm(query_ref[...], dq_ref[...]) + mm(pair_ref[...], dp_ref[...])).T
    weighted = grad * gain_ref[...]
    mean = jnp.mean(weighted * unit, axis=-1, keepdims=True)
    out_ref[...] = (dmid_ref[...].astype(F32) + scale * (weighted - unit * mean)).astype(BF)


def finish(x, gain, dmid, dq, dp, query, pair, tile=256):
    tokens, width = x.shape
    row = pl.BlockSpec((tile, width), lambda i: (i, 0))
    return pl.pallas_call(
        finish_kernel,
        grid=(tokens // tile,),
        in_specs=[
            row,
            pl.BlockSpec((1, width), lambda i: (0, 0)),
            row,
            pl.BlockSpec((dq.shape[0], tile), lambda i: (0, i)),
            pl.BlockSpec((dp.shape[0], tile), lambda i: (0, i)),
            pl.BlockSpec(query.shape, lambda i: (0, 0)),
            pl.BlockSpec(pair.shape, lambda i: (0, 0)),
        ],
        out_specs=row,
        out_shape=jax.ShapeDtypeStruct((tokens, width), BF),
        compiler_params=pltpu.CompilerParams(vmem_limit_bytes=VMEM_BYTES),
        cost_estimate=pl.CostEstimate(
            flops=2 * tokens * width * (dq.shape[0] + dp.shape[0]), bytes_accessed=12 * 10**6, transcendentals=0
        ),
        name="finish",
    )(x, gain, dmid, dq, dp, query, pair)


def widen_kernel(core_ref, *refs, parts, counts):
    mine, theirs, refs = refs[:parts], refs[parts : 2 * parts], refs[2 * parts :]
    gate_ref, up_ref, gate_grad, up_grad, down_grad, sums_ref = refs
    step = pl.program_id(0)
    tiles = sum(counts)
    at = step % tiles
    picked = None
    low = 0
    for part, other, count in zip(mine, theirs, counts):
        here = jnp.where(step < tiles, part[...], other[...])
        picked = here if picked is None else jnp.where(at < low, picked, here)
        low += count
    picked = picked.astype(F32)
    gate_grad[...] = picked[0]
    up_grad[...] = picked[1]
    down_grad[...] = picked[2]

    @pl.when(step == 0)
    def _():
        sums_ref[...] = jnp.zeros_like(sums_ref)

    terms = gate_ref[...].astype(F32) * picked[0] + up_ref[...].astype(F32) * picked[1]
    sums_ref[...] += jnp.sum(terms, axis=1, keepdims=True)


def widen(core, mine, theirs, gate, up, tile=256):
    rows, hidden = gate.shape
    counts = [part.shape[2] // tile for part in mine]
    tiles = sum(counts)
    lows = [sum(counts[:i]) for i in range(len(counts))]

    def place(step, core):
        return (core[0] ^ (step // tiles)) * tiles + step % tiles

    def inside(step, low, count):
        return jnp.minimum(jnp.maximum(step - low, 0), count - 1)

    mine_specs = [
        pl.BlockSpec((3, rows, tile), lambda i, core, low=low, count=count: (0, 0, inside(i, low, count)))
        for low, count in zip(lows, counts)
    ]
    their_specs = [
        pl.BlockSpec((3, rows, tile), lambda i, core, low=low, count=count: (0, 0, inside(i - tiles, low, count)))
        for low, count in zip(lows, counts)
    ]
    wide = pl.BlockSpec((rows, tile), lambda i, core: (0, place(i, core)))
    return pl.pallas_call(
        lambda *refs: widen_kernel(*refs, parts=len(mine), counts=counts),
        grid_spec=pltpu.PrefetchScalarGridSpec(
            num_scalar_prefetch=1,
            grid=(2 * tiles,),
            in_specs=mine_specs + their_specs + [wide, wide],
            out_specs=[wide, wide, wide, pl.BlockSpec((rows, 1), lambda i, core: (0, 0))],
        ),
        out_shape=[
            jax.ShapeDtypeStruct((rows, hidden), F32),
            jax.ShapeDtypeStruct((rows, hidden), F32),
            jax.ShapeDtypeStruct((rows, hidden), F32),
            jax.ShapeDtypeStruct((rows, 1), F32),
        ],
        compiler_params=pltpu.CompilerParams(vmem_limit_bytes=VMEM_BYTES),
        cost_estimate=pl.CostEstimate(flops=0, bytes_accessed=26 * 10**6, transcendentals=0),
        name="widen",
    )(core, *mine, *theirs, gate, up)


def partner(value, axis, size, bit):
    return lax.ppermute(value, axis, [(i, i ^ bit) for i in range(size)])


def after(value, *others):
    return lax.optimization_barrier((value,) + others)[0]


def pick(value, index, axis):
    return lax.dynamic_index_in_dim(value, index, axis, keepdims=False)


def pair_up(mine, other, index, axis):
    first = jnp.where(index == 0, mine, other)
    second = jnp.where(index == 0, other, mine)
    return jnp.stack([first, second], axis=axis)


class Fast:
    chip = 2

    def __init__(self, rows):
        self.rows = rows
        member, rep = lax.axis_index("shard"), lax.axis_index("rep")
        self.member, self.rep_index = member, rep
        self.c, self.y, self.z, self.far = member % 2, rep % 2, (rep // 2) % 2, rep // 4
        self.order = [member, member ^ 2, member ^ 1, member ^ 3]
        across = member // 2
        self.feed_starts = jnp.stack([across * 2 * rows, (1 - across) * 2 * rows]).astype(jnp.int32)
        self.feed_sizes = (2 * rows, 2 * rows)
        self.starts = jnp.stack([which * rows for which in self.order]).astype(jnp.int32)
        self.left_starts = self.feed_starts

    def x(self, value):
        return partner(value, "shard", 4, 2)

    def core(self, value):
        return partner(value, "shard", 4, 1)

    def rep(self, value, bit):
        return partner(value, "rep", 8, bit)

    def pieces(self, value, behind=None):
        across = self.x(value)
        return [value, across, self.core(value), self.core(across)]


    def feed_columns(self, columns):
        return self.c * (columns // 2), columns // 2

    def feed_core(self, shards, low, high, columns):
        half = columns // 2

        def cut(which):
            return jnp.stack([lax.dynamic_slice_in_dim(s, which * half + low, high - low, 1) for s in shards])

        mine, theirs = cut(self.c), cut(1 - self.c)
        both = pair_up(mine, self.core(theirs), self.c, 1)
        return both.reshape(3, 2 * self.rows, high - low)

    def feed_eighth(self, both):
        flat = both.reshape(-1, both.shape[2])
        eighth = flat.shape[0] // 8
        return self.x(lax.dynamic_slice_in_dim(flat, self.rep_index * eighth, eighth, 0))

    def feed_parts(self, both, eighth):
        return [both, self.spread(eighth).reshape(both.shape)]

    def gather_pairs(self, sent):
        both = jnp.stack([sent, self.x(sent)])
        return jnp.concatenate([both, self.core(both)], axis=0)

    def spread(self, eighth):
        return lax.all_gather(eighth, "rep", axis=0, tiled=True)

    def z_sum(self, value, order=(0, 1)):
        lines = [[at for at in range(8) if at % 2 == y] for y in order]
        return lax.psum(value, "rep", axis_index_groups=lines)

    def deal(self, held):
        first, second = [], []
        for at in range(32):
            rep, member = at // 4, at % 4
            y, c = rep % 2, member % 2
            here, there = rep * 4 + member - c + y, (rep ^ 1) * 4 + member - c + y
            if c == y:
                first.append((at, there))
            else:
                first.append((at, here))
                second.append((at, there))
        return [lax.ppermute(held, ("rep", "shard"), pairs) for pairs in (first, second)]

    def dealt(self, held, got):
        stay = self.c == self.y
        return jnp.where(stay, held, got[0]), jnp.where(stay, got[0], got[1])


class Chain:
    def __init__(self, net, kept, outward, count=1):
        self.net, self.stage, self.got = net, 0, None
        self.shape = (count, 2, kept.shape[0] // (2 * count), kept.shape[1])
        self.parts, self.out = [kept], outward

    def total(self):
        return sum(part.astype(F32) for part in self.parts + [self.got]).astype(BF)

    def ready(self):
        if self.stage == 1:
            parts = [part.reshape(self.shape) for part in self.parts + [self.got]]
            y = self.net.y
            self.out = sum(pick(part, 1 - y, 1).astype(F32) for part in parts).astype(BF)
            self.parts = [pick(part, y, 1) for part in parts]
        elif self.stage > 1:
            self.out = self.total()
            self.parts = [self.out]
        return self.out

    def move(self):
        if self.stage == 0:
            self.got = self.net.x(self.out)
        else:
            self.got = self.net.rep(self.out, (1, 2, 4)[self.stage - 1])
        self.stage += 1


def settle(chains, *others):
    values = lax.optimization_barrier(tuple(chain.got for chain in chains) + others)
    for chain, value in zip(chains, values):
        chain.got = value
    return values[len(chains) :]


def advance(chains, *others):
    outs = [chain.ready() for chain in chains]
    values = lax.optimization_barrier(tuple(outs) + others)
    for chain, value in zip(chains, values):
        chain.out = value
        chain.move()
    return values[len(chains) :]


class General:
    chip = 1

    def __init__(self, rows):
        shards = lax.axis_size("shard")
        self.rows, self.shards = rows, shards
        self.member = lax.axis_index("shard")
        self.order = [jnp.int32(i) for i in range(shards)]
        self.starts = jnp.arange(shards, dtype=jnp.int32) * rows
        self.feed_starts = self.starts
        self.left_starts = jnp.zeros((1,), jnp.int32)
        self.feed_sizes = (shards * rows,)

    def pieces(self, value):
        whole = lax.all_gather(value, "shard", axis=0)
        return [whole[i] for i in range(self.shards)]

    def feed_core(self, shards, low, high, columns):
        return jnp.stack([shard[:, low:high] for shard in shards])

    def gather_pairs(self, sent):
        return lax.all_gather(sent, "shard", axis=0)

    def sum_pairs(self, terms):
        return lax.psum_scatter(terms, "shard", scatter_dimension=0, tiled=False).astype(F32)

    def whole_sum(self, terms, axis):
        owned = lax.psum_scatter(terms, "shard", scatter_dimension=axis, tiled=True)
        return lax.psum(owned, "rep").astype(F32)


def on_device(
    tokens,
    cotangent,
    block_map,
    query_weight,
    key_weight,
    value_weight,
    output_weight,
    attention_gain,
    gate_weight,
    up_weight,
    down_weight,
    feed_gain,
):
    shards = lax.axis_size("shard")
    fast = shards == 4 and lax.axis_size("rep") == 8
    micro, rows, width = tokens.shape
    block = rows // 2
    total = micro * rows
    shard_rows = query_weight.shape[0]
    net = Fast(shard_rows) if fast else General(shard_rows)
    head_width = HEADS * HEAD_DIM
    pair_width = KV_HEADS * HEAD_DIM
    hidden_width = gate_weight.shape[1]
    batches = range(micro)

    gain_pieces = net.pieces(jnp.stack([attention_gain, feed_gain], axis=1))
    gains = jnp.zeros((width, 2), BF)
    for i, piece in enumerate(gain_pieces):
        gains = lax.dynamic_update_slice_in_dim(gains, piece, net.starts[i], 0)
    gain_one = gains[:, 0].astype(F32)[None, :]
    gain_two = gains[:, 1].astype(F32)[None, :]
    pair_pieces = net.pieces(jnp.concatenate([key_weight, value_weight], axis=1))
    feed_shards = [gate_weight, up_weight, down_weight.T]
    columns = hidden_width // net.chip
    cuts = [0, 512, 1280, columns] if fast else [0, columns]

    blocks_here = block_map[:, 0]
    own_block = lax.dynamic_index_in_dim(blocks_here, net.member, axis=1, keepdims=False)
    others = jnp.stack(
        [lax.dynamic_index_in_dim(blocks_here, which, axis=1, keepdims=False) for which in net.order],
        axis=1,
    )
    gap = ((own_block[:, None] - others) * block).astype(jnp.int32)
    inside = jnp.arange(block, dtype=jnp.int32)
    place = jnp.concatenate(
        [
            own_block[:, None] * block + inside[None, :],
            jnp.broadcast_to(block * shards + inside[None, :], (micro, block)),
        ],
        axis=1,
    ).reshape(total)
    half = HEAD_DIM // 2
    freq = jnp.exp(jnp.arange(half, dtype=F32) * (-2.0 * jnp.log(10000.0) / HEAD_DIM))
    angle = freq[:, None] * place.astype(F32)[None, :]
    cosine, sine = jnp.cos(angle), jnp.sin(angle)

    key_place = jnp.concatenate(
        [
            (others[:, :, None] * block + inside).reshape(micro, -1),
            jnp.broadcast_to(block * shards + inside[None, :], (micro, block)),
        ],
        axis=1,
    ).reshape(-1)
    key_angle = freq[:, None] * key_place.astype(F32)[None, :]
    key_cosine, key_sine = jnp.cos(key_angle), jnp.sin(key_angle)

    source = tokens.reshape(total, width)
    turned_one = prepare(source, gain_one)
    upstream = [cotangent[m] for m in batches]
    if fast:
        bind = lax.optimization_barrier

        def core_of(part, *others):
            shards_after = [after(shard, *others) if others else shard for shard in feed_shards]
            return net.feed_core(shards_after, cuts[part], cuts[part + 1], hidden_width)

        feed_cores = [core_of(0), core_of(1)]
        query_across = net.x(after(query_weight, pair_pieces[1]))
        pair_across = after(pair_pieces[1], turned_one)
        pair_pieces = [pair_pieces[0], pair_across, pair_pieces[2], net.core(pair_across)]
        own_pairs, pair_full = project(net.starts, turned_one, cosine, sine, pair_pieces, 640, KV_HEADS, 1.0)
        sent = [own_pairs[:, m * rows : m * rows + block] for m in batches]
        across = [net.x(part) for part in sent]
        query_across = after(query_across, own_pairs)
        query_pieces = [query_weight, query_across, net.core(query_weight), net.core(query_across)]
        query, query_full = project(net.starts, turned_one, cosine, sine, query_pieces, 640, HEADS, HEAD_DIM**-0.5)
        across_0, across_1, query = bind((*across, query))
        pairs = [
            [mine, theirs, net.core(mine), net.core(theirs)] for mine, theirs in zip(sent, (across_0, across_1))
        ]
        eighths = [net.feed_eighth(after(part, query)) for part in feed_cores]
        moved = net.core(after(cotangent, query)).reshape(total, width)
        upstream_all = [(value, 0) for value in upstream] + [(moved, m) for m in batches]
        turned_other = net.core(after(turned_one, query))
        output_across = net.x(after(output_weight, query))
        eighth_0, pairs[0][3] = bind((eighths[0], pairs[0][3]))
        feed_parts = [net.feed_parts(feed_cores[0], eighth_0)]
        mixed_0, log_0 = attend(gap, query, pairs[0], own_pairs, micro, 0)
        mixed_0, output_across, eighth_1 = bind((mixed_0, output_across, eighths[1]))
        feed_parts.append(net.feed_parts(feed_cores[1], eighth_1))
        feed_cores.append(core_of(2, mixed_0))
        eighth_2 = net.feed_eighth(feed_cores[2])
        output_pieces = [output_weight, output_across, net.core(output_weight), net.core(output_across)]
        mixed_1, log_1 = attend(after(gap, mixed_0), query, pairs[1], own_pairs, micro, 1)
        mixed_1, eighth_2 = bind((mixed_1, eighth_2))
        feed_parts.append(net.feed_parts(feed_cores[2], eighth_2))
        mixed, log_total = [mixed_0, mixed_1], [log_0, log_1]
        mixed_all = mixed + [net.core(value) for value in mixed]
        middle_0, normed_0, output_full = merge(
            net.starts, after(mixed_0, mixed_1), tokens[0], gain_two, output_pieces
        )
        middle_1, normed_1 = merge(net.starts, mixed_1, tokens[1], gain_two, [output_full])
        middle, normed_two = [middle_0, middle_1], [normed_0, normed_1]
        normed_all = [(value, 0) for value in normed_two] + [(net.core(value), 0) for value in normed_two]
    else:
        own_pairs, pair_full = project(net.starts, turned_one, cosine, sine, pair_pieces, 640, KV_HEADS, 1.0)
        pairs = [list(net.gather_pairs(own_pairs[:, m * rows : m * rows + block])) for m in batches]
        query_pieces = net.pieces(query_weight)
        query, query_full = project(net.starts, turned_one, cosine, sine, query_pieces, 640, HEADS, HEAD_DIM**-0.5)
        feed_parts = [net.pieces(jnp.stack(feed_shards))]
        output_pieces = net.pieces(output_weight)
        mixed, log_total, middle, normed_two = [], [], [], []
        for m in batches:
            mixed_m, log_m = attend(gap, query, pairs[m], own_pairs, micro, m)
            middle_m, normed_m, output_full = merge(net.starts, mixed_m, tokens[m], gain_two, output_pieces)
            mixed.append(mixed_m)
            log_total.append(log_m)
            middle.append(middle_m)
            normed_two.append(normed_m)
        normed_all = [(value, 0) for value in normed_two]
        upstream_all = [(value, 0) for value in upstream]

    backs = [[] for _ in batches]
    hids, downs, feed_terms, ones = [], [], [], []
    starts = net.feed_starts
    for k, parts in enumerate(feed_parts):
        split = ((0, 1), (2,)) if fast and k == 1 else ((0, 1, 2),)
        grads, backs_here, hid, down = feed(
            starts, net.left_starts, normed_all, upstream_all, parts, net.feed_sizes, rows, split
        )
        feed_terms.append(grads)
        if fast and k == 2:
            settled = settle(ones[:2], *backs_here, hid)
            backs_here, hid = settled[:-1], settled[-1]
        for m in batches:
            backs[m].append(backs_here[m])
            if fast:
                backs[m].append(net.core(backs_here[micro + m]))
        if fast:
            grads = [grad.reshape(-1, grad.shape[-1]) for grad in grads]
            ones += [Chain(net, grads[j], grads[len(split) + j], len(names)) for j, names in enumerate(split)]
        hids.append(hid)
        downs.append(down)
        starts = after(net.feed_starts, hid)
        if fast and k == 0:
            prompt = jnp.concatenate(
                [turned_one[:, m * rows : m * rows + block] for m in batches], axis=1
            )
            prompt_across = net.x(after(prompt, normed_two[-1]))
            starts, prompt_across = bind((starts, prompt_across))
            prompts = [prompt, prompt_across, net.core(prompt), net.core(prompt_across)]
            ones[0].move()
        elif fast and k == 1:
            (starts,) = settle(ones[:1], starts)
            (starts,) = advance(ones[:1], starts)
            ones[1].move()
    size = net.feed_sizes[0]

    def back_of(m, grad_mixed, low, high):
        return attend_back(
            gap, cosine, sine, key_cosine, key_sine, query, mixed[m], grad_mixed, log_total[m], pairs[m], own_pairs, micro, m, low, high
        )

    def pair_grads(summed, own_terms):
        return jnp.concatenate([summed.astype(BF), own_terms], axis=-1).reshape(2 * pair_width, rows)

    def finish_of(m, dmid, grad_query, grad_pairs):
        return finish(tokens[m], gain_one, dmid, grad_query, grad_pairs, query_full, pair_full)

    if fast:
        lefts_one = [(turned_one, 0), (turned_one, 1), (turned_other, 0), (turned_other, 1)]
        lefts_mixed = [(value, 0) for value in mixed_all]
        part_1, part_2, part_3, part_4 = ones

        def split(value, axis):
            size = value.shape[axis] // 2
            return [lax.dynamic_slice_in_dim(value, at * size, size, axis) for at in (net.c, 1 - net.c)]

        middle_0, first = advance([part_2, part_3], after(middle[0], backs[0][-1]), part_1.total())
        first = net.z_sum(first)
        def kind(value, which):
            return lax.dynamic_index_in_dim(value, which, value.ndim - 4, keepdims=False)

        def pairs_out(terms, own):
            extra = jnp.concatenate([kind(terms[:2], 1 - net.c), kind(own, 1 - net.c)[None]], axis=0)
            return net.core(terms[2:]), net.core(extra)

        def pairs_chip(terms, own, away, extra):
            mine = kind(terms, net.c).astype(F32)
            theirs = jnp.concatenate([kind(away, net.c), extra[:2]], axis=0).astype(F32)
            return (mine + theirs).astype(BF).reshape(4, pair_width, block), [
                value.reshape(pair_width, block) for value in (kind(own, net.c), extra[2])
            ]

        dmid_0, mixed_0 = unmerge(middle_0, upstream[0], gain_two, output_full, backs[0])
        theirs = output(hids, [downs[0], downs[1], after(downs[2], mixed_0)], [], total, total)
        mixed_0, theirs = settle([part_2, part_3], mixed_0, theirs)
        theirs = net.core(theirs)
        (mixed_0,) = advance([part_3, part_4], mixed_0)
        query_0, terms_0, own_0 = back_of(0, mixed_0, 0, KV_HEADS)
        query_0, terms_0, theirs, first = settle([part_3], query_0, terms_0, theirs, first)
        away_0, extra_0 = pairs_out(terms_0, own_0)
        second = jnp.concatenate([part_2.total(), part_3.total()], axis=0)
        halves_0 = split(after(dmid_0, query_0), 1)
        second, middle_1 = bind((second, after(middle[1], query_0)))
        second = net.z_sum(second)
        dmid_1, mixed_1 = unmerge(middle_1, upstream[1], gain_two, output_full, backs[1])
        halves_1 = split(dmid_1, 1)
        mixed_1, moved_0, moved_1, away_0, extra_0 = settle(
            [part_4], mixed_1, halves_0[1], halves_1[1], away_0, extra_0
        )
        kept_0 = (terms_0[:2].astype(F32) + away_0.astype(F32)).astype(BF)
        mixed_1, moved_0, moved_1, out_0 = advance([part_4], mixed_1, moved_0, moved_1, kept_0[1])
        got_0 = net.x(out_0)
        dmid_halves = [halves_0[0], halves_1[0], net.core(moved_0), net.core(moved_1)]
        query_1, terms_1, own_1 = back_of(1, mixed_1, 0, 3)
        output_terms = grad_terms(
            net.left_starts, lefts_mixed, [after(value, query_1) for value in dmid_halves], False, size, 640
        )

        query_1, got_0, *output_terms = settle([part_4], query_1, got_0, *output_terms)
        blocks_0, owns_0 = pairs_chip(terms_0, own_0, away_0, extra_0)
        chain_o = Chain(net, *output_terms)
        mixed_1, third, blocks_0 = advance([chain_o], after(mixed_1, query_1), part_4.total(), blocks_0)
        third = net.z_sum(third, (1, 0))
        query_1b, terms_1b, own_1b = back_of(1, mixed_1, 3, KV_HEADS)

        query_1b, second = settle([chain_o], query_1b, second)
        terms_1 = jnp.concatenate([terms_1, terms_1b], axis=2)
        own_1 = jnp.concatenate([own_1, own_1b], axis=1)
        grad_query = [query_0, jnp.concatenate([query_1, query_1b], axis=0)]
        halves = [split(value, 0) for value in grad_query]
        moved_0, moved_1, terms_1 = bind((halves[0][1], halves[1][1], terms_1))
        away_1, extra_1 = pairs_out(terms_1, own_1)
        query_halves = [halves[0][0], halves[1][0], net.core(moved_0), net.core(moved_1)]
        (out_o,) = bind((chain_o.ready(),))
        away_1, extra_1, out_o, *query_halves = bind((away_1, extra_1, out_o, *query_halves))
        kept_1 = (terms_1[:2].astype(F32) + away_1.astype(F32)).astype(BF)
        blocks_1, owns_1 = pairs_chip(terms_1, own_1, away_1, extra_1)
        out_1, blocks_1, chain_o.out = bind((kept_1[1], blocks_1, out_o))
        chain_o.move()
        got_1 = net.x(out_1)
        got_2 = net.deal(after(second, out_1))
        arrays = [turned_one, turned_other, *prompts, *query_halves, blocks_0, *owns_0, blocks_1, *owns_1]
        steps_query = [(m // 2, (m % 2) * rows, 6 + m, None) for m in range(4)]
        steps_pair = []
        for m in batches:
            steps_pair += [(2 + j, m * block, 10 + 3 * m, j) for j in range(4)]
            steps_pair += [(j, m * rows + block, 11 + 3 * m + j, None) for j in range(2)]
        query_terms = joint_terms(
            net.left_starts, arrays, [steps_query, steps_pair], [head_width // 2, pair_width], size
        )
        got_1, *query_terms = settle([chain_o], got_1, *query_terms)
        chain_q = Chain(net, *query_terms)
        (query_0,) = advance([chain_q], query_0)
        chain_o.got = after(chain_o.got, query_0)
        (query_0,) = advance([chain_o], query_0)
        got_1st = net.deal(after(first, query_0))
        grad_pairs = [
            pair_grads(kept[0].astype(F32) + got.astype(F32), own)
            for kept, got, own in ((kept_0, got_0, own_0), (kept_1, after(got_1, query_0), own_1))
        ]
        source_0 = finish_of(0, dmid_0, query_0, grad_pairs[0])
        source_1 = finish_of(1, dmid_1, grad_query[1], grad_pairs[1])
        source_0, source_1, *settled = settle([chain_q, chain_o], source_0, source_1, *got_2, *got_1st)
        got_2, got_1st = settled[:2], settled[2:]
        (theirs,) = advance([chain_q], theirs)
        chain_o.got = after(chain_o.got, theirs)
        (theirs,) = advance([chain_o], theirs)
        layer_out = output(hids, downs, [jnp.concatenate(middle, axis=0), theirs], 0, total)
        (layer_out,) = settle([chain_q, chain_o], layer_out)
        (held_q,) = bind((chain_q.ready(),))
        held_q = net.z_sum(after(held_q, layer_out))
        held_o = after(chain_o.total(), layer_out)
        got_o = net.deal(held_o)
        got_3 = net.deal(after(third, layer_out))
        mine_1, theirs_1 = net.dealt(first, got_1st)
        mine_2, theirs_2 = net.dealt(second, got_2)
        mine_3, theirs_3 = net.dealt(third, got_3)
        gate_grad, up_grad, down_grad, sums = widen(
            net.c[None].astype(jnp.int32),
            [mine_1, mine_2, mine_3],
            [theirs_1, theirs_2, theirs_3],
            gate_weight,
            up_weight,
        )
        held_q, sums, *got_o = bind((held_q, sums, *got_o))
        got_q = net.deal(held_q)
        output_rows = [value[0] for value in net.dealt(held_o, got_o)]
        query_rows = [value[0] for value in net.dealt(held_q, got_q)]
        pair_rows = [value[:, head_width // 2 :] for value in query_rows]
        query_rows = [value[:, : head_width // 2] for value in query_rows]

        def columns_of(rows_of):
            mine, theirs = (value.astype(F32) for value in rows_of)
            return jnp.where(net.c == 0, mine, theirs), jnp.where(net.c == 0, theirs, mine)

        output_grad = jnp.concatenate(columns_of(output_rows), axis=1)
        query_grad = jnp.concatenate(columns_of(query_rows), axis=1)
        key_grad, value_grad = columns_of(pair_rows)
        down_grad = down_grad.T
        feed_gain_grad = sums[:, 0] / feed_gain.astype(F32)
        grad_source = [source_0, source_1]
    else:
        grad_query, grad_pairs, dmids = [], [], []
        for m in batches:
            dmid, grad_mixed = unmerge(middle[m], upstream[m], gain_two, output_full, backs[m])
            query_m, terms, own = back_of(m, grad_mixed, 0, KV_HEADS)
            dmids.append(dmid)
            grad_query.append(query_m)
            grad_pairs.append(pair_grads(net.sum_pairs(terms), own))
        lefts_one = [(turned_one, m) for m in batches]
        lefts_mixed = [(value, 0) for value in mixed]
        terms = [
            grad_terms(net.left_starts, lefts_mixed, dmids, False, size, 640),
            grad_terms(net.left_starts, lefts_one, grad_query, True, size, 640),
            grad_terms(net.left_starts, lefts_one, grad_pairs, True, size, 640),
        ]
        output_grad, query_grad, pair_grad = [net.whole_sum(term[0], 0) for term in terms]
        key_grad, value_grad = pair_grad[:, :pair_width], pair_grad[:, pair_width:]
        feed_grads = net.whole_sum(feed_terms[0][0].reshape(3, width, hidden_width), 1)
        gate_grad, up_grad, down_grad = feed_grads[0], feed_grads[1], feed_grads[2].T
        layer_out = output(hids, downs, [jnp.concatenate(middle, axis=0)], 0, total)
        grad_source = [finish_of(m, dmids[m], grad_query[m], grad_pairs[m]) for m in batches]

    def gain_grad(gain, *both):
        terms = sum(jnp.sum(weight.astype(F32) * grad, axis=1) for weight, grad in both)
        return terms / gain.astype(F32)

    attention_gain_grad = gain_grad(
        attention_gain, (query_weight, query_grad), (key_weight, key_grad), (value_weight, value_grad)
    )
    if not fast:
        feed_gain_grad = gain_grad(feed_gain, (gate_weight, gate_grad), (up_weight, up_grad))
    return (
        layer_out.reshape(tokens.shape),
        jnp.stack(grad_source),
        query_grad,
        key_grad,
        value_grad,
        output_grad,
        attention_gain_grad,
        gate_grad,
        up_grad,
        down_grad,
        feed_gain_grad,
    )


def solution(mesh):
    return jax.shard_map(
        on_device,
        mesh=mesh,
        in_specs=(
            P(None, ("rep", "shard"), None),
            P(None, ("rep", "shard"), None),
            P(None, "rep", None),
            P("shard", None),
            P("shard", None),
            P("shard", None),
            P("shard", None),
            P("shard"),
            P("shard", None),
            P("shard", None),
            P(None, "shard"),
            P("shard"),
        ),
        out_specs=(
            P(None, ("rep", "shard"), None),
            P(None, ("rep", "shard"), None),
            P("shard", None),
            P("shard", None),
            P("shard", None),
            P("shard", None),
            P("shard"),
            P("shard", None),
            P("shard", None),
            P(None, "shard"),
            P("shard"),
        ),
        check_vma=False,
    )
```

```python
import jax
import jax.numpy as jnp
from jax import lax
from jax.experimental import pallas as pl
from jax.experimental.pallas import tpu as pltpu
from jax.sharding import PartitionSpec as P

HEADS = 20
KV_HEADS = 5
HEAD_DIM = 64
GROUP = HEADS // KV_HEADS
EPS = 1e-05
NEG = -1e30
F32 = jnp.float32
BF = jnp.bfloat16
VMEM_BYTES = 62 * 1024 * 1024


def mm(left, right):
    return jnp.dot(left, right, preferred_element_type=F32)


def ein(spec, left, right):
    return jnp.einsum(spec, left, right, preferred_element_type=F32)

def attend_kernel(gap_ref, q_ref, *refs, m, blocks):
    k_ref, v_ref, refs = refs[:blocks], refs[blocks : 2 * blocks], refs[2 * blocks :]
    kl_ref, vl_ref, a_ref, lse_ref = refs
    dim, blk = kl_ref.shape
    keys = jnp.concatenate([k_ref[j][...].T for j in range(blocks)] + [kl_ref[...].T], axis=0)
    ones = jnp.ones((16, (blocks+1)*blk), BF)
    vals = jnp.concatenate([jnp.concatenate([v_ref[j][...] for j in range(blocks)] + [vl_ref[...]], axis=1), ones], axis=0)
    diff = lax.broadcasted_iota(jnp.int32,(blk,blk),0) - lax.broadcasted_iota(jnp.int32,(blk,blk),1)
    n = blocks*blk
    for g in range(GROUP):
        for half in (0,1):
            q = q_ref[g*dim:(g+1)*dim, half*blk:(half+1)*blk]
            if half == 0:
                s = mm(keys[:n], q)
                s = jnp.concatenate([jnp.where(diff <= gap_ref[m, j], s[j*blk:(j+1)*blk], NEG) for j in range(blocks)], axis=0)
                vv = vals[:, :n]
            else:
                s = mm(keys, q)
                s = jnp.concatenate([s[:n], jnp.where(diff <= 0, s[n:], NEG)], axis=0)
                vv = vals
            top = jnp.max(s, axis=0, keepdims=True)
            p = jnp.exp(s - top).astype(BF)
            o = mm(vv, p)
            total = o[dim:dim+1]
            a_ref[g*dim:(g+1)*dim, half*blk:(half+1)*blk] = (o[:dim] / total).astype(BF)
            lse_ref[0, g:g+1, half*blk:(half+1)*blk] = top + jnp.log(total)

def attend(gap, qT, pairs, ownT, micro, m):
    blocks, blk = len(pairs), pairs[0].shape[1]
    rows = qT.shape[1] // micro
    return pl.pallas_call(
        lambda *refs: attend_kernel(*refs, m=m, blocks=blocks),
        grid=(KV_HEADS,),
        in_specs=[
            pl.BlockSpec(memory_space=pltpu.SMEM),
            pl.BlockSpec((GROUP * HEAD_DIM, rows), lambda h: (h, m)),
        ]
        + [pl.BlockSpec((HEAD_DIM, blk), lambda h: (h, 0))] * blocks
        + [pl.BlockSpec((HEAD_DIM, blk), lambda h: (KV_HEADS + h, 0))] * blocks
        + [
            pl.BlockSpec((HEAD_DIM, blk), lambda h: (h, 2 * m + 1)),
            pl.BlockSpec((HEAD_DIM, blk), lambda h: (KV_HEADS + h, 2 * m + 1)),
        ],
        out_specs=[
            pl.BlockSpec((GROUP * HEAD_DIM, rows), lambda h: (h, 0)),
            pl.BlockSpec((1, GROUP, rows), lambda h: (h, 0, 0)),
        ],
        out_shape=[
            jax.ShapeDtypeStruct((qT.shape[0], rows), BF),
            jax.ShapeDtypeStruct((KV_HEADS, GROUP, rows), F32),
        ],
        compiler_params=pltpu.CompilerParams(vmem_limit_bytes=VMEM_BYTES),
        cost_estimate=pl.CostEstimate(flops=3 * 10**10, bytes_accessed=5 * 10**6, transcendentals=12 * 10**6),
        name="attend",
    )(gap, qT, *pairs, *pairs, ownT, ownT)


def back_kernel(gap_ref, cos_ref, sin_ref, kcos_ref, ksin_ref, q_ref, a_ref, da_ref, lse_ref, *refs, m, blocks):
    k_ref, v_ref, refs = refs[:blocks], refs[blocks : 2 * blocks], refs[2 * blocks :]
    kl_ref, vl_ref, dq_ref, terms_ref, own_ref, p_scr, ds_scr = refs
    dim, blk = kl_ref.shape
    n = blocks*blk
    keysT = jnp.concatenate([k_ref[j][...] for j in range(blocks)] + [kl_ref[...]], axis=1)
    keys = jnp.concatenate([k_ref[j][...].T for j in range(blocks)] + [kl_ref[...].T], axis=0)
    vals = jnp.concatenate([v_ref[j][...].T for j in range(blocks)] + [vl_ref[...].T], axis=0)
    diff = lax.broadcasted_iota(jnp.int32,(blk,blk),0) - lax.broadcasted_iota(jnp.int32,(blk,blk),1)
    dk = None; dv = None
    for half in (0,1):
        span = n if half == 0 else n + blk
        cols = slice(half*blk, (half+1)*blk)
        qn = []; dan = []
        for g in range(GROUP):
            rows = slice(g*dim, (g+1)*dim)
            q = q_ref[rows, cols]; da = da_ref[rows, cols]
            qn.append(q.T); dan.append(da.T)
            delta = jnp.sum(da.astype(F32) * a_ref[rows, cols].astype(F32), axis=0, keepdims=True)
            lse = lse_ref[0, g:g+1, cols]
            s = mm(keys[:span], q)
            if half == 0:
                s = jnp.concatenate([jnp.where(diff <= gap_ref[m, j], s[j*blk:(j+1)*blk], NEG) for j in range(blocks)], axis=0)
            else:
                s = jnp.concatenate([s[:n], jnp.where(diff <= 0, s[n:], NEG)], axis=0)
            p = jnp.exp(s - lse)
            dp = mm(vals[:span], da)
            ds = (p * (dp - delta)).astype(BF)
            p_scr[:span, g*blk:(g+1)*blk] = p.astype(BF)
            ds_scr[:span, g*blk:(g+1)*blk] = ds
            dq = mm(keysT[:, :span], ds) * (HEAD_DIM ** -0.5)
            c = cos_ref[:, cols]; sn = sin_ref[:, cols]
            first = dq[:dim//2]; second = dq[dim//2:]
            dq_ref[rows, cols] = jnp.concatenate([first*c + second*sn, second*c - first*sn], axis=0).astype(BF)
        qn = jnp.concatenate(qn, axis=0); dan = jnp.concatenate(dan, axis=0)
        dkh = mm(ds_scr[:span], qn); dvh = mm(p_scr[:span], dan)
        if half == 0:
            dk, dv = dkh, dvh
        else:
            dk = jnp.concatenate([dk + dkh[:n], dkh[n:]], axis=0)
            dv = jnp.concatenate([dv + dvh[:n], dvh[n:]], axis=0)
    half = dim // 2
    for j in range(blocks + 1):
        cols = slice(j * blk, (j + 1) * blk)
        turned = dk[cols].T
        first, second = turned[:half], turned[half:]
        c, sn = kcos_ref[:, cols], ksin_ref[:, cols]
        turned = jnp.concatenate([first * c + second * sn, second * c - first * sn], axis=0).astype(BF)
        value = dv[cols].T.astype(BF)
        if j < blocks:
            terms_ref[j, 0, 0], terms_ref[j, 1, 0] = turned, value
        else:
            own_ref[0, 0], own_ref[1, 0] = turned, value


def attend_back(gap, cosT, sinT, kcos, ksin, qT, aT, daT, lse, pairs, ownT, micro, m, low, high):
    blocks, blk = len(pairs), pairs[0].shape[1]
    rows = qT.shape[1] // micro
    count = high - low
    query = pl.BlockSpec((GROUP * HEAD_DIM, rows), lambda h: (low + h, m))
    part = pl.BlockSpec((GROUP * HEAD_DIM, rows), lambda h: (low + h, 0))
    table = pl.BlockSpec((HEAD_DIM // 2, rows), lambda h: (0, m))
    keys = pl.BlockSpec((HEAD_DIM // 2, (blocks + 1) * blk), lambda h: (0, m))
    return pl.pallas_call(
        lambda *refs: back_kernel(*refs, m=m, blocks=blocks),
        grid=(count,),
        in_specs=[
            pl.BlockSpec(memory_space=pltpu.SMEM),
            table,
            table,
            keys,
            keys,
            query,
            part,
            part,
            pl.BlockSpec((1, GROUP, rows), lambda h: (low + h, 0, 0)),
        ]
        + [pl.BlockSpec((HEAD_DIM, blk), lambda h: (low + h, 0))] * blocks
        + [pl.BlockSpec((HEAD_DIM, blk), lambda h: (KV_HEADS + low + h, 0))] * blocks
        + [
            pl.BlockSpec((HEAD_DIM, blk), lambda h: (low + h, 2 * m + 1)),
            pl.BlockSpec((HEAD_DIM, blk), lambda h: (KV_HEADS + low + h, 2 * m + 1)),
        ],
        out_specs=[
            pl.BlockSpec((GROUP * HEAD_DIM, rows), lambda h: (h, 0)),
            pl.BlockSpec((blocks, 2, 1, HEAD_DIM, blk), lambda h: (0, 0, h, 0, 0)),
            pl.BlockSpec((2, 1, HEAD_DIM, blk), lambda h: (0, h, 0, 0)),
        ],
        out_shape=[
            jax.ShapeDtypeStruct((count * GROUP * HEAD_DIM, rows), BF),
            jax.ShapeDtypeStruct((blocks, 2, count, HEAD_DIM, blk), BF),
            jax.ShapeDtypeStruct((2, count, HEAD_DIM, blk), BF),
        ],
        scratch_shapes=[pltpu.VMEM(((blocks + 1) * blk, GROUP * blk), BF)] * 2,
        compiler_params=pltpu.CompilerParams(vmem_limit_bytes=VMEM_BYTES),
        cost_estimate=pl.CostEstimate(flops=8 * 10**9 * count, bytes_accessed=10**6 * count, transcendentals=0),
        name="attend_back",
    )(gap, cosT, sinT, kcos, ksin, qT, aT, daT, lse, *pairs, *pairs, ownT, ownT)


def nt(left, right):
    return lax.dot_general(left, right, (((1,), (1,)), ((), ())), preferred_element_type=F32)


def tn(left, right):
    return lax.dot_general(left, right, (((0,), (0,)), ((), ())), preferred_element_type=F32)


def project_kernel(row_ref, ht_ref, cos_ref, sin_ref, *refs, pieces, turned, scale):
    parts, (out_ref, whole_ref) = refs[:pieces], refs[pieces:]
    for i, part in enumerate(parts):
        whole_ref[pl.ds(pl.multiple_of(row_ref[i], 16), part.shape[0]), :] = part[...]
    raw = tn(whole_ref[...], ht_ref[...])
    half = HEAD_DIM // 2
    for head in range(raw.shape[0] // HEAD_DIM):
        at = head * HEAD_DIM
        if head < turned:
            first, second = raw[at : at + half], raw[at + half : at + HEAD_DIM]
            cosine, sine = cos_ref[...], sin_ref[...]
            out_ref[at : at + half] = (first * cosine - second * sine).astype(BF) * BF(scale)
            out_ref[at + half : at + HEAD_DIM] = (second * cosine + first * sine).astype(BF) * BF(scale)
        else:
            out_ref[at : at + HEAD_DIM] = raw[at : at + HEAD_DIM].astype(BF)


def project(starts, ht, cosine, sine, pieces, tile, turned, scale):
    width, tokens = ht.shape
    count = pieces[0].shape[1]
    table = pl.BlockSpec(cosine.shape, lambda i: (0, 0))
    return pl.pallas_call(
        lambda *refs: project_kernel(*refs, pieces=len(pieces), turned=turned, scale=scale),
        grid=(count // tile,),
        in_specs=[
            pl.BlockSpec(memory_space=pltpu.SMEM),
            pl.BlockSpec((width, tokens), lambda i: (0, 0)),
            table,
            table,
        ]
        + [pl.BlockSpec((piece.shape[0], tile), lambda i: (0, i)) for piece in pieces],
        out_specs=[
            pl.BlockSpec((tile, tokens), lambda i: (i, 0)),
            pl.BlockSpec((width, tile), lambda i: (0, i)),
        ],
        out_shape=[
            jax.ShapeDtypeStruct((count, tokens), BF),
            jax.ShapeDtypeStruct((width, count), BF),
        ],
        compiler_params=pltpu.CompilerParams(vmem_limit_bytes=VMEM_BYTES),
        cost_estimate=pl.CostEstimate(
            flops=2 * tokens * width * count, bytes_accessed=6 * width * count, transcendentals=0
        ),
        name="project",
    )(starts, ht, cosine, sine, *pieces)


def feed_kernel(row_ref, left_ref, *refs, sets, pieces, groups, split, step):
    hs, cs, refs = refs[:sets], refs[sets : 2 * sets], refs[2 * sets :]
    parts, refs = refs[:pieces], refs[pieces:]
    count = groups * len(split)
    grads, refs = refs[:count], refs[count:]
    backs, refs = refs[:sets], refs[sets:]
    hid_ref, down_ref, ht_ref, ct_ref, gate_ref, up_ref, dg_ref, dw_ref, acc_ref = refs
    tokens, width = hs[0].shape
    at = pl.program_id(0)

    @pl.when(at == 0)
    def _():
        for i in range(sets):
            ht_ref[:, i * tokens : (i + 1) * tokens] = hs[i][...].T
            ct_ref[:, i * tokens : (i + 1) * tokens] = cs[i][...].T
        acc_ref[...] = jnp.zeros_like(acc_ref)

    for k, whole in enumerate((gate_ref, up_ref, down_ref)):
        for i, part in enumerate(parts):
            whole[pl.ds(pl.multiple_of(row_ref[i], 16), part.shape[1]), :] = part[k]
    for i in range(sets):
        for b in range(0, tokens, step):
            rows, to = pl.ds(b, step), pl.ds(i * tokens + b, step)
            gate = mm(hs[i][rows, :], gate_ref[...])
            upper = mm(hs[i][rows, :], up_ref[...])
            grad = mm(cs[i][rows, :], down_ref[...])
            sigma = jax.nn.sigmoid(gate)
            silu = gate * sigma
            hid_ref[to, :] = (silu * upper).astype(BF)
            dg_ref[to, :] = (grad * upper * (sigma + silu * (1.0 - sigma))).astype(BF)
            dw_ref[to, :] = (grad * silu).astype(BF)
    times = ((ht_ref, dg_ref), (ht_ref, dw_ref), (ct_ref, hid_ref))
    for i in range(groups):
        for j, names in enumerate(split):
            out = grads[i * len(split) + j]
            rows = pl.ds(pl.multiple_of(left_ref[i], 16), out.shape[1])
            for at_name, name in enumerate(names):
                left, right = times[name]
                out[at_name] = mm(left[rows, :], right[...]).astype(BF)
    for b in range(0, sets * tokens, step):
        rows = pl.ds(b, step)
        acc_ref[rows, :] += nt(dg_ref[rows, :], gate_ref[...]) + nt(dw_ref[rows, :], up_ref[...])

    @pl.when(at == pl.num_programs(0) - 1)
    def _():
        for i, back in enumerate(backs):
            back[...] = acc_ref[pl.ds(i * tokens, tokens), :].astype(BF)


def feed(starts, left_starts, hs, cs, parts, sizes, rows, split=((0, 1, 2),), tile=256, step=256):
    sets = len(hs)
    tokens, width = rows, hs[0][0].shape[1]
    hidden = parts[0].shape[2]
    one = pl.Buffered(1)
    back = pl.BlockSpec((tokens, width), lambda i: (0, 0), pipeline_mode=one)
    toks = [pl.BlockSpec((tokens, width), lambda i, at=at: (at, 0), pipeline_mode=one) for _, at in hs + cs]
    smem = pl.BlockSpec(memory_space=pltpu.SMEM)
    counts = [(len(names), size) for size in sizes for names in split]
    grad_specs = [pl.BlockSpec((count, size, tile), lambda i: (0, 0, i)) for count, size in counts]
    grad_shapes = [jax.ShapeDtypeStruct((count, size, hidden), BF) for count, size in counts]
    results = pl.pallas_call(
        lambda *refs: feed_kernel(*refs, sets=sets, pieces=len(parts), groups=len(sizes), split=split, step=step),
        grid=(hidden // tile,),
        in_specs=[smem, smem]
        + toks
        + [pl.BlockSpec((3, part.shape[1], tile), lambda i: (0, 0, i)) for part in parts],
        out_specs=grad_specs
        + [back] * sets
        + [pl.BlockSpec((sets * tokens, tile), lambda i: (0, i)), pl.BlockSpec((width, tile), lambda i: (0, i))],
        out_shape=grad_shapes
        + [jax.ShapeDtypeStruct((tokens, width), BF)] * sets
        + [jax.ShapeDtypeStruct((sets * tokens, hidden), BF), jax.ShapeDtypeStruct((width, hidden), BF)],
        scratch_shapes=[pltpu.VMEM((width, sets * tokens), BF)] * 2
        + [pltpu.VMEM((width, tile), BF)] * 2
        + [pltpu.VMEM((sets * tokens, tile), BF)] * 2
        + [pltpu.VMEM((sets * tokens, width), F32)],
        compiler_params=pltpu.CompilerParams(vmem_limit_bytes=VMEM_BYTES),
        cost_estimate=pl.CostEstimate(
            flops=16 * sets * tokens * width * hidden,
            bytes_accessed=14 * width * hidden + 12 * sets * tokens * width,
            transcendentals=sets * tokens * hidden,
        ),
        name="feed",
    )(starts, left_starts, *[h for h, _ in hs], *[c for c, _ in cs], *parts)
    count = len(grad_specs)
    return results[:count], results[count : count + sets], results[-2], results[-1]


def prepare_kernel(x_ref, gain_ref, ht_ref):
    source = x_ref[...].astype(F32)
    scale = lax.rsqrt(jnp.mean(source * source, axis=-1, keepdims=True) + EPS)
    ht_ref[...] = (source * scale * gain_ref[...]).astype(BF).T


def prepare(x, gain, tile=256):
    tokens, width = x.shape
    return pl.pallas_call(
        prepare_kernel,
        grid=(tokens // tile,),
        in_specs=[pl.BlockSpec((tile, width), lambda i: (i, 0)), pl.BlockSpec((1, width), lambda i: (0, 0))],
        out_specs=pl.BlockSpec((width, tile), lambda i: (0, i)),
        out_shape=jax.ShapeDtypeStruct((width, tokens), BF),
        compiler_params=pltpu.CompilerParams(vmem_limit_bytes=VMEM_BYTES),
        cost_estimate=pl.CostEstimate(flops=0, bytes_accessed=6 * 10**6, transcendentals=0),
        name="prepare",
    )(x, gain)


def merge_kernel(row_ref, at_ref, x_ref, gain_ref, *refs, pieces):
    if pieces == 1:
        whole_ref, mid_ref, h_ref = refs
    else:
        parts, (mid_ref, h_ref, whole_ref) = refs[:pieces], refs[pieces:]
        for i, part in enumerate(parts):
            whole_ref[pl.ds(pl.multiple_of(row_ref[i], 16), part.shape[0]), :] = part[...]
    middle = x_ref[...].astype(F32) + tn(at_ref[...], whole_ref[...])
    scale = lax.rsqrt(jnp.mean(middle * middle, axis=-1, keepdims=True) + EPS)
    mid_ref[...] = middle
    h_ref[...] = (middle * scale * gain_ref[...]).astype(BF)


def merge(starts, at, x, m, gain, pieces):
    head_width, tokens = at.shape
    width = x.shape[1]
    row = pl.BlockSpec((tokens, width), lambda i: (0, 0))
    outs = [row, row]
    shapes = [jax.ShapeDtypeStruct((tokens, width), F32), jax.ShapeDtypeStruct((tokens, width), BF)]
    if len(pieces) > 1:
        outs.append(pl.BlockSpec((head_width, width), lambda i: (0, 0)))
        shapes.append(jax.ShapeDtypeStruct((head_width, width), BF))
    return pl.pallas_call(
        lambda *refs: merge_kernel(*refs, pieces=len(pieces)),
        grid=(1,),
        in_specs=[
            pl.BlockSpec(memory_space=pltpu.SMEM),
            pl.BlockSpec((head_width, tokens), lambda i: (0, 0)),
            pl.BlockSpec((tokens, width), lambda i: (m, 0)),
            pl.BlockSpec((1, width), lambda i: (0, 0)),
        ]
        + [pl.BlockSpec(piece.shape, lambda i: (0, 0)) for piece in pieces],
        out_specs=outs,
        out_shape=shapes,
        compiler_params=pltpu.CompilerParams(vmem_limit_bytes=VMEM_BYTES),
        cost_estimate=pl.CostEstimate(
            flops=2 * tokens * width * head_width, bytes_accessed=16 * 10**6, transcendentals=0
        ),
        name="merge",
    )(starts, at, x, gain, *pieces)


def unmerge_kernel(mid_ref, c_ref, gain_ref, whole_ref, *refs):
    backs, (dmid_ref, da_ref) = refs[:-2], refs[-2:]
    middle = mid_ref[...]
    scale = lax.rsqrt(jnp.mean(middle * middle, axis=-1, keepdims=True) + EPS)
    unit = middle * scale
    grad = backs[0][...].astype(F32)
    for back in backs[1:]:
        grad = grad + back[...].astype(F32)
    weighted = grad * gain_ref[...]
    mean = jnp.mean(weighted * unit, axis=-1, keepdims=True)
    dmid = (c_ref[...].astype(F32) + scale * (weighted - unit * mean)).astype(BF)
    dmid_ref[...] = dmid
    da_ref[...] = nt(whole_ref[...], dmid).astype(BF)


def unmerge(mid, c, m, gain, whole, backs, tile=256):
    tokens, width = mid.shape
    head_width = whole.shape[0]
    row = pl.BlockSpec((tile, width), lambda i: (i, 0))
    return pl.pallas_call(
        unmerge_kernel,
        grid=(tokens // tile,),
        in_specs=[
            row,
            pl.BlockSpec((tile, width), lambda i: (m * (tokens // tile) + i, 0)),
            pl.BlockSpec((1, width), lambda i: (0, 0)),
            pl.BlockSpec((head_width, width), lambda i: (0, 0)),
        ]
        + [row] * len(backs),
        out_specs=[row, pl.BlockSpec((head_width, tile), lambda i: (0, i))],
        out_shape=[
            jax.ShapeDtypeStruct((tokens, width), BF),
            jax.ShapeDtypeStruct((head_width, tokens), BF),
        ],
        compiler_params=pltpu.CompilerParams(vmem_limit_bytes=VMEM_BYTES),
        cost_estimate=pl.CostEstimate(
            flops=2 * tokens * width * head_width, bytes_accessed=16 * 10**6, transcendentals=0
        ),
        name="unmerge",
    )(mid, c, gain, whole, *backs)


def terms_kernel(left_ref, *refs, count, turned):
    lefts, rights, outs = refs[:count], refs[count : 2 * count], refs[2 * count :]
    times = nt if turned else mm
    for i, out in enumerate(outs):
        rows = pl.ds(pl.multiple_of(left_ref[i], 16), out.shape[0])
        total = times(lefts[0][rows, :], rights[0][...])
        for left, right in zip(lefts[1:], rights[1:]):
            total = total + times(left[rows, :], right[...])
        out[...] = total.astype(BF)


def grad_terms(left_starts, lefts, rights, turned, size, tile):
    columns = rights[0].shape[0 if turned else 1]
    span = rights[0].shape[1 if turned else 0]
    count = left_starts.shape[0]
    if turned:
        right_specs = [pl.BlockSpec((tile, span), lambda i: (i, 0)) for _ in rights]
    else:
        right_specs = [pl.BlockSpec((span, tile), lambda i: (0, i)) for _ in rights]
    left_specs = [pl.BlockSpec((left.shape[0], span), lambda i, at=at: (0, at)) for left, at in lefts]
    return pl.pallas_call(
        lambda *refs: terms_kernel(*refs, count=len(lefts), turned=turned),
        grid=(columns // tile,),
        in_specs=[pl.BlockSpec(memory_space=pltpu.SMEM)] + left_specs + right_specs,
        out_specs=[pl.BlockSpec((size, tile), lambda i: (0, i))] * count,
        out_shape=[jax.ShapeDtypeStruct((size, columns), BF)] * count,
        compiler_params=pltpu.CompilerParams(vmem_limit_bytes=VMEM_BYTES),
        cost_estimate=pl.CostEstimate(
            flops=2 * len(lefts) * span * columns * size * count, bytes_accessed=8 * 10**6, transcendentals=0
        ),
        name="grad_terms",
    )(left_starts, *[left for left, _ in lefts], *rights)


def joint_kernel(left_ref, *refs, plan, sizes, outs):
    refs, outs = refs[:-outs], refs[-outs:]
    for i, out in enumerate(outs):
        rows = pl.ds(pl.multiple_of(left_ref[i], 16), out.shape[0])
        column = 0
        for steps, count in zip(plan, sizes):
            total = 0.0
            for left, at, right, index in steps:
                value = refs[right][...] if index is None else refs[right][index]
                total = total + nt(refs[left][rows, at : at + value.shape[1]], value)
            out[:, column : column + count] = total.astype(BF)
            column += count


def joint_terms(left_starts, arrays, plan, sizes, size):
    whole = [pl.BlockSpec(array.shape, lambda i, n=array.ndim: (0,) * n) for array in arrays]
    outs = left_starts.shape[0]
    return pl.pallas_call(
        lambda *refs: joint_kernel(*refs, plan=plan, sizes=sizes, outs=outs),
        grid=(1,),
        in_specs=[pl.BlockSpec(memory_space=pltpu.SMEM)] + whole,
        out_specs=[pl.BlockSpec((size, sum(sizes)), lambda i: (0, 0))] * outs,
        out_shape=[jax.ShapeDtypeStruct((size, sum(sizes)), BF)] * outs,
        compiler_params=pltpu.CompilerParams(vmem_limit_bytes=VMEM_BYTES),
        cost_estimate=pl.CostEstimate(flops=6 * 10**9, bytes_accessed=14 * 10**6, transcendentals=0),
        name="joint_terms",
    )(left_starts, *arrays)


def output_kernel(*refs, parts, adds, firsts):
    hids, downs, refs = refs[:parts], refs[parts : 2 * parts], refs[2 * parts :]
    adds, firsts, out_ref = refs[:adds], refs[adds:-1], refs[-1]
    total = nt(hids[0][...], downs[0][...])
    for hid, down in zip(hids[1:], downs[1:]):
        total = total + nt(hid[...], down[...])
    for add in adds:
        total = total + add[...].astype(F32)
    if not firsts:
        out_ref[...] = total.astype(BF)
    for i, first in enumerate(firsts):

        @pl.when(pl.program_id(0) == i)
        def _():
            out_ref[...] = (total + first[...]).astype(BF)


def output(hids, downs, adds, firsts, skip, tile):
    width = downs[0].shape[0]
    row = pl.BlockSpec((tile, width), lambda i: (i, 0))
    return pl.pallas_call(
        lambda *refs: output_kernel(*refs, parts=len(hids), adds=len(adds), firsts=len(firsts)),
        grid=(2,),
        in_specs=[pl.BlockSpec((tile, hid.shape[1]), lambda i: (skip + i, 0)) for hid in hids]
        + [pl.BlockSpec(down.shape, lambda i: (0, 0)) for down in downs]
        + [row] * len(adds)
        + [pl.BlockSpec((tile, width), lambda i: (0, 0))] * len(firsts),
        out_specs=row,
        out_shape=jax.ShapeDtypeStruct((2 * tile, width), BF),
        compiler_params=pltpu.CompilerParams(vmem_limit_bytes=VMEM_BYTES),
        cost_estimate=pl.CostEstimate(flops=5 * 10**9, bytes_accessed=16 * 10**6, transcendentals=0),
        name="output",
    )(*hids, *downs, *adds, *firsts)


def finish_kernel(x_ref, gain_ref, dmid_ref, dq_ref, dp_ref, query_ref, pair_ref, out_ref):
    source = x_ref[...].astype(F32)
    scale = lax.rsqrt(jnp.mean(source * source, axis=-1, keepdims=True) + EPS)
    unit = source * scale
    grad = (mm(query_ref[...], dq_ref[...]) + mm(pair_ref[...], dp_ref[...])).T
    weighted = grad * gain_ref[...]
    mean = jnp.mean(weighted * unit, axis=-1, keepdims=True)
    out_ref[...] = (dmid_ref[...].astype(F32) + scale * (weighted - unit * mean)).astype(BF)


def finish(x, m, gain, dmid, dq, dp, query, pair, tile=256):
    tokens, width = dmid.shape
    row = pl.BlockSpec((tile, width), lambda i: (i, 0))
    return pl.pallas_call(
        finish_kernel,
        grid=(tokens // tile,),
        in_specs=[
            pl.BlockSpec((tile, width), lambda i: (m * (tokens // tile) + i, 0)),
            pl.BlockSpec((1, width), lambda i: (0, 0)),
            row,
            pl.BlockSpec((dq.shape[0], tile), lambda i: (0, i)),
            pl.BlockSpec((dp.shape[0], tile), lambda i: (0, i)),
            pl.BlockSpec(query.shape, lambda i: (0, 0)),
            pl.BlockSpec(pair.shape, lambda i: (0, 0)),
        ],
        out_specs=row,
        out_shape=jax.ShapeDtypeStruct((tokens, width), BF),
        compiler_params=pltpu.CompilerParams(vmem_limit_bytes=VMEM_BYTES),
        cost_estimate=pl.CostEstimate(
            flops=2 * tokens * width * (dq.shape[0] + dp.shape[0]), bytes_accessed=12 * 10**6, transcendentals=0
        ),
        name="finish",
    )(x, gain, dmid, dq, dp, query, pair)


def widen_kernel(core_ref, *refs, parts, counts):
    mine, theirs, refs = refs[:parts], refs[parts : 2 * parts], refs[2 * parts :]
    gate_ref, up_ref, gate_grad, up_grad, down_grad, sums_ref = refs
    step = pl.program_id(0)
    tiles = sum(counts)
    at = step % tiles
    picked = None
    low = 0
    for part, other, count in zip(mine, theirs, counts):
        here = jnp.where(step < tiles, part[...], other[...])
        picked = here if picked is None else jnp.where(at < low, picked, here)
        low += count
    picked = picked.astype(F32)
    gate_grad[...] = picked[0]
    up_grad[...] = picked[1]
    down_grad[...] = picked[2]

    @pl.when(step == 0)
    def _():
        sums_ref[...] = jnp.zeros_like(sums_ref)

    terms = gate_ref[...].astype(F32) * picked[0] + up_ref[...].astype(F32) * picked[1]
    sums_ref[...] += jnp.sum(terms, axis=1, keepdims=True)


def widen(core, mine, theirs, gate, up, tile=256):
    rows, hidden = gate.shape
    counts = [part.shape[2] // tile for part in mine]
    tiles = sum(counts)
    lows = [sum(counts[:i]) for i in range(len(counts))]

    def place(step, core):
        return (core[0] ^ (step // tiles)) * tiles + step % tiles

    def inside(step, low, count):
        return jnp.minimum(jnp.maximum(step - low, 0), count - 1)

    mine_specs = [
        pl.BlockSpec((3, rows, tile), lambda i, core, low=low, count=count: (0, 0, inside(i, low, count)))
        for low, count in zip(lows, counts)
    ]
    their_specs = [
        pl.BlockSpec((3, rows, tile), lambda i, core, low=low, count=count: (0, 0, inside(i - tiles, low, count)))
        for low, count in zip(lows, counts)
    ]
    wide = pl.BlockSpec((rows, tile), lambda i, core: (0, place(i, core)))
    return pl.pallas_call(
        lambda *refs: widen_kernel(*refs, parts=len(mine), counts=counts),
        grid_spec=pltpu.PrefetchScalarGridSpec(
            num_scalar_prefetch=1,
            grid=(2 * tiles,),
            in_specs=mine_specs + their_specs + [wide, wide],
            out_specs=[wide, wide, wide, pl.BlockSpec((rows, 1), lambda i, core: (0, 0))],
        ),
        out_shape=[
            jax.ShapeDtypeStruct((rows, hidden), F32),
            jax.ShapeDtypeStruct((rows, hidden), F32),
            jax.ShapeDtypeStruct((rows, hidden), F32),
            jax.ShapeDtypeStruct((rows, 1), F32),
        ],
        compiler_params=pltpu.CompilerParams(vmem_limit_bytes=VMEM_BYTES),
        cost_estimate=pl.CostEstimate(flops=0, bytes_accessed=26 * 10**6, transcendentals=0),
        name="widen",
    )(core, *mine, *theirs, gate, up)


def partner(value, axis, size, bit):
    return lax.ppermute(value, axis, [(i, i ^ bit) for i in range(size)])


def after(value, *others):
    return lax.optimization_barrier((value,) + others)[0]


def pick(value, index, axis):
    return lax.dynamic_index_in_dim(value, index, axis, keepdims=False)


def pair_up(mine, other, index, axis):
    first = jnp.where(index == 0, mine, other)
    second = jnp.where(index == 0, other, mine)
    return jnp.stack([first, second], axis=axis)


class Fast:
    chip = 2

    def __init__(self, rows):
        self.rows = rows
        member, rep = lax.axis_index("shard"), lax.axis_index("rep")
        self.member, self.rep_index = member, rep
        self.c, self.y, self.z, self.far = member % 2, rep % 2, (rep // 2) % 2, rep // 4
        self.order = [member, member ^ 2, member ^ 1, member ^ 3]
        across = member // 2
        self.feed_starts = jnp.stack([across * 2 * rows, (1 - across) * 2 * rows]).astype(jnp.int32)
        self.feed_sizes = (2 * rows, 2 * rows)
        self.starts = jnp.stack([which * rows for which in self.order]).astype(jnp.int32)
        self.left_starts = self.feed_starts

    def x(self, value):
        return partner(value, "shard", 4, 2)

    def core(self, value):
        return partner(value, "shard", 4, 1)

    def rep(self, value, bit):
        return partner(value, "rep", 8, bit)

    def pieces(self, value, behind=None):
        across = self.x(value)
        return [value, across, self.core(value), self.core(across)]


    def feed_columns(self, columns):
        return self.c * (columns // 2), columns // 2

    def feed_core(self, shards, low, high, columns):
        half = columns // 2

        def cut(which):
            return jnp.stack([lax.dynamic_slice_in_dim(s, which * half + low, high - low, 1) for s in shards])

        mine, theirs = cut(self.c), cut(1 - self.c)
        both = pair_up(mine, self.core(theirs), self.c, 1)
        return both.reshape(3, 2 * self.rows, high - low)

    def feed_eighth(self, both):
        flat = both.reshape(-1, both.shape[2])
        eighth = flat.shape[0] // 8
        return self.x(lax.dynamic_slice_in_dim(flat, self.rep_index * eighth, eighth, 0))

    def feed_parts(self, both, eighth):
        return [both, self.spread(eighth).reshape(both.shape)]

    def gather_pairs(self, sent):
        both = jnp.stack([sent, self.x(sent)])
        return jnp.concatenate([both, self.core(both)], axis=0)

    def spread(self, eighth):
        return lax.all_gather(eighth, "rep", axis=0, tiled=True)

    def z_sum(self, value, order=(0, 1)):
        lines = [[at for at in range(8) if at % 2 == y] for y in order]
        return lax.psum(value, "rep", axis_index_groups=lines)

    def deal(self, held):
        first, second = [], []
        for at in range(32):
            rep, member = at // 4, at % 4
            y, c = rep % 2, member % 2
            here, there = rep * 4 + member - c + y, (rep ^ 1) * 4 + member - c + y
            if c == y:
                first.append((at, there))
            else:
                first.append((at, here))
                second.append((at, there))
        return [lax.ppermute(held, ("rep", "shard"), pairs) for pairs in (first, second)]

    def dealt(self, held, got):
        stay = self.c == self.y
        return jnp.where(stay, held, got[0]), jnp.where(stay, got[0], got[1])


class Chain:
    def __init__(self, net, kept, outward, count=1):
        self.net, self.stage, self.got = net, 0, None
        self.shape = (count, 2, kept.shape[0] // (2 * count), kept.shape[1])
        self.parts, self.out = [kept], outward

    def total(self):
        return sum(part.astype(F32) for part in self.parts + [self.got]).astype(BF)

    def ready(self):
        if self.stage == 1:
            parts = [part.reshape(self.shape) for part in self.parts + [self.got]]
            y = self.net.y
            self.out = sum(pick(part, 1 - y, 1).astype(F32) for part in parts).astype(BF)
            self.parts = [pick(part, y, 1) for part in parts]
        elif self.stage > 1:
            self.out = self.total()
            self.parts = [self.out]
        return self.out

    def move(self):
        if self.stage == 0:
            self.got = self.net.x(self.out)
        else:
            self.got = self.net.rep(self.out, (1, 2, 4)[self.stage - 1])
        self.stage += 1


def settle(chains, *others):
    values = lax.optimization_barrier(tuple(chain.got for chain in chains) + others)
    for chain, value in zip(chains, values):
        chain.got = value
    return values[len(chains) :]


def advance(chains, *others):
    outs = [chain.ready() for chain in chains]
    values = lax.optimization_barrier(tuple(outs) + others)
    for chain, value in zip(chains, values):
        chain.out = value
        chain.move()
    return values[len(chains) :]


class General:
    chip = 1

    def __init__(self, rows):
        shards = lax.axis_size("shard")
        self.rows, self.shards = rows, shards
        self.member = lax.axis_index("shard")
        self.order = [jnp.int32(i) for i in range(shards)]
        self.starts = jnp.arange(shards, dtype=jnp.int32) * rows
        self.feed_starts = self.starts
        self.left_starts = jnp.zeros((1,), jnp.int32)
        self.feed_sizes = (shards * rows,)

    def pieces(self, value):
        whole = lax.all_gather(value, "shard", axis=0)
        return [whole[i] for i in range(self.shards)]

    def feed_core(self, shards, low, high, columns):
        return jnp.stack([shard[:, low:high] for shard in shards])

    def gather_pairs(self, sent):
        return lax.all_gather(sent, "shard", axis=0)

    def sum_pairs(self, terms):
        return lax.psum_scatter(terms, "shard", scatter_dimension=0, tiled=False).astype(F32)

    def whole_sum(self, terms, axis):
        owned = lax.psum_scatter(terms, "shard", scatter_dimension=axis, tiled=True)
        return lax.psum(owned, "rep").astype(F32)


def on_device(
    tokens,
    cotangent,
    block_map,
    query_weight,
    key_weight,
    value_weight,
    output_weight,
    attention_gain,
    gate_weight,
    up_weight,
    down_weight,
    feed_gain,
):
    shards = lax.axis_size("shard")
    fast = shards == 4 and lax.axis_size("rep") == 8
    micro, rows, width = tokens.shape
    block = rows // 2
    total = micro * rows
    shard_rows = query_weight.shape[0]
    net = Fast(shard_rows) if fast else General(shard_rows)
    head_width = HEADS * HEAD_DIM
    pair_width = KV_HEADS * HEAD_DIM
    hidden_width = gate_weight.shape[1]
    batches = range(micro)

    gain_pieces = net.pieces(jnp.stack([attention_gain, feed_gain], axis=1))
    gains = jnp.zeros((width, 2), BF)
    for i, piece in enumerate(gain_pieces):
        gains = lax.dynamic_update_slice_in_dim(gains, piece, net.starts[i], 0)
    gain_one = gains[:, 0].astype(F32)[None, :]
    gain_two = gains[:, 1].astype(F32)[None, :]
    pair_pieces = net.pieces(jnp.concatenate([key_weight, value_weight], axis=1))
    feed_shards = [gate_weight, up_weight, down_weight.T]
    columns = hidden_width // net.chip
    cuts = [0, 512, 1280, columns] if fast else [0, columns]

    blocks_here = block_map[:, 0]
    own_block = lax.dynamic_index_in_dim(blocks_here, net.member, axis=1, keepdims=False)
    others = jnp.stack(
        [lax.dynamic_index_in_dim(blocks_here, which, axis=1, keepdims=False) for which in net.order],
        axis=1,
    )
    gap = ((own_block[:, None] - others) * block).astype(jnp.int32)
    inside = jnp.arange(block, dtype=jnp.int32)
    place = jnp.concatenate(
        [
            own_block[:, None] * block + inside[None, :],
            jnp.broadcast_to(block * shards + inside[None, :], (micro, block)),
        ],
        axis=1,
    ).reshape(total)
    half = HEAD_DIM // 2
    freq = jnp.exp(jnp.arange(half, dtype=F32) * (-2.0 * jnp.log(10000.0) / HEAD_DIM))
    angle = freq[:, None] * place.astype(F32)[None, :]
    cosine, sine = jnp.cos(angle), jnp.sin(angle)

    key_place = jnp.concatenate(
        [
            (others[:, :, None] * block + inside).reshape(micro, -1),
            jnp.broadcast_to(block * shards + inside[None, :], (micro, block)),
        ],
        axis=1,
    ).reshape(-1)
    key_angle = freq[:, None] * key_place.astype(F32)[None, :]
    key_cosine, key_sine = jnp.cos(key_angle), jnp.sin(key_angle)

    source = tokens.reshape(total, width)
    turned_one = prepare(source, gain_one)
    upstream = cotangent.reshape(total, width)
    if fast:
        bind = lax.optimization_barrier

        def core_of(part, *others):
            shards_after = [after(shard, *others) if others else shard for shard in feed_shards]
            return net.feed_core(shards_after, cuts[part], cuts[part + 1], hidden_width)

        feed_cores = [core_of(0)]
        query_across = net.x(after(query_weight, pair_pieces[1]))
        pair_across = after(pair_pieces[1], turned_one)
        pair_pieces = [pair_pieces[0], pair_across, pair_pieces[2], net.core(pair_across)]
        own_pairs, pair_full = project(net.starts, turned_one, cosine, sine, pair_pieces, 640, KV_HEADS, 1.0)
        sent = [own_pairs[:, m * rows : m * rows + block] for m in batches]
        across = [net.x(part) for part in sent]
        across[0], turned_q = bind((across[0], turned_one))
        query_across = after(query_across, sent[1])
        query_pieces = [query_weight, query_across, net.core(query_weight), net.core(query_across)]
        pairs = [[sent[0], across[0], net.core(sent[0]), net.core(across[0])]]
        query, query_full = project(net.starts, turned_q, cosine, sine, query_pieces, 640, HEADS, HEAD_DIM**-0.5)
        eighths = [net.feed_eighth(after(part, across[0])) for part in feed_cores]
        moved = net.core(after(upstream, across[0]))
        upstream_all = [(upstream, m) for m in batches] + [(moved, m) for m in batches]
        turned_other = net.core(after(turned_one, across[0]))
        output_across = net.x(after(output_weight, across[0]))
        mixed_0, log_0 = attend(gap, query, pairs[0], own_pairs, micro, 0)
        mixed_0, output_across, across[1], eighth_0 = bind((mixed_0, output_across, across[1], eighths[0]))
        feed_parts = [net.feed_parts(feed_cores[0], eighth_0)]
        pairs.append([sent[1], across[1], net.core(sent[1]), net.core(across[1])])
        feed_cores += [core_of(1, mixed_0), core_of(2, mixed_0)]
        eighth_1, eighth_2 = [net.feed_eighth(part) for part in feed_cores[1:]]
        output_pieces = [output_weight, output_across, net.core(output_weight), net.core(output_across)]
        mixed_1, log_1 = attend(after(gap, mixed_0), query, pairs[1], own_pairs, micro, 1)
        mixed_1, eighth_1, eighth_2 = bind((mixed_1, eighth_1, eighth_2))
        feed_parts += [net.feed_parts(feed_cores[1], eighth_1), net.feed_parts(feed_cores[2], eighth_2)]
        mixed, log_total = [mixed_0, mixed_1], [log_0, log_1]
        mixed_all = mixed + [net.core(value) for value in mixed]
        middle_0, normed_0, output_full = merge(
            net.starts, after(mixed_0, mixed_1), source, 0, gain_two, output_pieces
        )
        middle_1, normed_1 = merge(net.starts, mixed_1, source, 1, gain_two, [output_full])
        middle, normed_two = [middle_0, middle_1], [normed_0, normed_1]
        normed_all = [(value, 0) for value in normed_two] + [(net.core(value), 0) for value in normed_two]
    else:
        own_pairs, pair_full = project(net.starts, turned_one, cosine, sine, pair_pieces, 640, KV_HEADS, 1.0)
        pairs = [list(net.gather_pairs(own_pairs[:, m * rows : m * rows + block])) for m in batches]
        query_pieces = net.pieces(query_weight)
        query, query_full = project(net.starts, turned_one, cosine, sine, query_pieces, 640, HEADS, HEAD_DIM**-0.5)
        feed_parts = [net.pieces(jnp.stack(feed_shards))]
        output_pieces = net.pieces(output_weight)
        mixed, log_total, middle, normed_two = [], [], [], []
        for m in batches:
            mixed_m, log_m = attend(gap, query, pairs[m], own_pairs, micro, m)
            middle_m, normed_m, output_full = merge(net.starts, mixed_m, source, m, gain_two, output_pieces)
            mixed.append(mixed_m)
            log_total.append(log_m)
            middle.append(middle_m)
            normed_two.append(normed_m)
        normed_all = [(value, 0) for value in normed_two]
        upstream_all = [(upstream, m) for m in batches]

    backs = [[] for _ in batches]
    hids, downs, feed_terms, ones = [], [], [], []
    starts = net.feed_starts
    for k, parts in enumerate(feed_parts):
        split = ((0, 1), (2,)) if fast and k == 1 else ((0, 1, 2),)
        grads, backs_here, hid, down = feed(
            starts, net.left_starts, normed_all, upstream_all, parts, net.feed_sizes, rows, split
        )
        feed_terms.append(grads)
        if fast and k == 2:
            settled = settle(ones[:2], *backs_here, hid)
            backs_here, hid = settled[:-1], settled[-1]
        for m in batches:
            backs[m].append(backs_here[m])
            if fast:
                backs[m].append(net.core(backs_here[micro + m]))
        if fast:
            grads = [grad.reshape(-1, grad.shape[-1]) for grad in grads]
            ones += [Chain(net, grads[j], grads[len(split) + j], len(names)) for j, names in enumerate(split)]
        hids.append(hid)
        downs.append(down)
        starts = after(net.feed_starts, hid)
        if fast and k == 0:
            prompt = jnp.concatenate(
                [turned_one[:, m * rows : m * rows + block] for m in batches], axis=1
            )
            prompt_across = net.x(after(prompt, normed_two[-1]))
            starts, prompt_across = bind((starts, prompt_across))
            prompts = [prompt, prompt_across, net.core(prompt), net.core(prompt_across)]
            ones[0].move()
        elif fast and k == 1:
            (starts,) = settle(ones[:1], starts)
            (starts,) = advance(ones[:1], starts)
            ones[1].move()
    size = net.feed_sizes[0]

    def back_of(m, grad_mixed, low, high):
        return attend_back(
            gap, cosine, sine, key_cosine, key_sine, query, mixed[m], grad_mixed, log_total[m], pairs[m], own_pairs, micro, m, low, high
        )

    def pair_grads(summed, own_terms):
        return jnp.concatenate([summed.astype(BF), own_terms], axis=-1).reshape(2 * pair_width, rows)

    def finish_of(m, dmid, grad_query, grad_pairs):
        return finish(source, m, gain_one, dmid, grad_query, grad_pairs, query_full, pair_full)

    if fast:
        lefts_one = [(turned_one, 0), (turned_one, 1), (turned_other, 0), (turned_other, 1)]
        lefts_mixed = [(value, 0) for value in mixed_all]
        part_1, part_2, part_3, part_4 = ones

        def split(value, axis):
            size = value.shape[axis] // 2
            return [lax.dynamic_slice_in_dim(value, at * size, size, axis) for at in (net.c, 1 - net.c)]

        middle_0, first = advance([part_2, part_3], after(middle[0], backs[0][-1]), part_1.total())
        first = net.z_sum(first)
        def kind(value, which):
            return lax.dynamic_index_in_dim(value, which, value.ndim - 4, keepdims=False)

        def pairs_out(terms, own):
            extra = jnp.concatenate([kind(terms[:2], 1 - net.c), kind(own, 1 - net.c)[None]], axis=0)
            return net.core(terms[2:]), net.core(extra)

        def pairs_chip(terms, own, away, extra):
            mine = kind(terms, net.c).astype(F32)
            theirs = jnp.concatenate([kind(away, net.c), extra[:2]], axis=0).astype(F32)
            return (mine + theirs).astype(BF).reshape(4, pair_width, block), [
                value.reshape(pair_width, block) for value in (kind(own, net.c), extra[2])
            ]

        dmid_0, mixed_0 = unmerge(middle_0, upstream, 0, gain_two, output_full, backs[0])
        theirs = output(hids, [downs[0], downs[1], after(downs[2], mixed_0)], [], [], micro, rows)
        mixed_0, theirs = settle([part_2, part_3], mixed_0, theirs)
        theirs = net.core(theirs)
        (mixed_0,) = advance([part_3, part_4], mixed_0)
        query_0, terms_0, own_0 = back_of(0, mixed_0, 0, KV_HEADS)
        query_0, terms_0, theirs, first = settle([part_3], query_0, terms_0, theirs, first)
        away_0, extra_0 = pairs_out(terms_0, own_0)
        second = jnp.concatenate([part_2.total(), part_3.total()], axis=0)
        halves_0 = split(after(dmid_0, query_0), 1)
        second, middle_1 = bind((second, after(middle[1], query_0)))
        second = net.z_sum(second)
        dmid_1, mixed_1 = unmerge(middle_1, upstream, 1, gain_two, output_full, backs[1])
        halves_1 = split(dmid_1, 1)
        mixed_1, moved_0, moved_1, away_0, extra_0 = settle(
            [part_4], mixed_1, halves_0[1], halves_1[1], away_0, extra_0
        )
        kept_0 = (terms_0[:2].astype(F32) + away_0.astype(F32)).astype(BF)
        mixed_1, moved_0, moved_1, out_0 = advance([part_4], mixed_1, moved_0, moved_1, kept_0[1])
        got_0 = net.x(out_0)
        dmid_halves = [halves_0[0], halves_1[0], net.core(moved_0), net.core(moved_1)]
        query_1, terms_1, own_1 = back_of(1, mixed_1, 0, 3)
        output_terms = grad_terms(
            net.left_starts, lefts_mixed, [after(value, query_1) for value in dmid_halves], False, size, 640
        )

        query_1, got_0, *output_terms = settle([part_4], query_1, got_0, *output_terms)
        blocks_0, owns_0 = pairs_chip(terms_0, own_0, away_0, extra_0)
        chain_o = Chain(net, *output_terms)
        mixed_1, third, blocks_0 = advance([chain_o], after(mixed_1, query_1), part_4.total(), blocks_0)
        third = net.z_sum(third, (1, 0))
        got_1st = net.deal(after(first, mixed_1))
        query_1b, terms_1b, own_1b = back_of(1, mixed_1, 3, KV_HEADS)

        query_1b, second = settle([chain_o], query_1b, second)
        terms_1 = jnp.concatenate([terms_1, terms_1b], axis=2)
        own_1 = jnp.concatenate([own_1, own_1b], axis=1)
        grad_query = [query_0, jnp.concatenate([query_1, query_1b], axis=0)]
        halves = [split(value, 0) for value in grad_query]
        moved_0, moved_1, terms_1 = bind((halves[0][1], halves[1][1], terms_1))
        away_1, extra_1 = pairs_out(terms_1, own_1)
        query_halves = [halves[0][0], halves[1][0], net.core(moved_0), net.core(moved_1)]
        (out_o,) = bind((chain_o.ready(),))
        away_1, extra_1, out_o, *settled = bind((away_1, extra_1, out_o, *query_halves, *got_1st))
        query_halves, got_1st = settled[:4], settled[4:]
        kept_1 = (terms_1[:2].astype(F32) + away_1.astype(F32)).astype(BF)
        blocks_1, owns_1 = pairs_chip(terms_1, own_1, away_1, extra_1)
        out_1, blocks_1, chain_o.out = bind((kept_1[1], blocks_1, out_o))
        chain_o.move()
        got_1 = net.x(out_1)
        got_2 = net.deal(after(second, out_1))
        arrays = [turned_one, turned_other, *prompts, *query_halves, blocks_0, *owns_0, blocks_1, *owns_1]
        steps_query = [(m // 2, (m % 2) * rows, 6 + m, None) for m in range(4)]
        steps_pair = []
        for m in batches:
            steps_pair += [(2 + j, m * block, 10 + 3 * m, j) for j in range(4)]
            steps_pair += [(j, m * rows + block, 11 + 3 * m + j, None) for j in range(2)]
        query_terms = joint_terms(
            net.left_starts, arrays, [steps_query, steps_pair], [head_width // 2, pair_width], size
        )
        got_1, *query_terms = bind((got_1, *query_terms))
        chain_q = Chain(net, *query_terms)
        (query_0,) = advance([chain_q], query_0)
        grad_pairs = [
            pair_grads(kept[0].astype(F32) + got.astype(F32), own)
            for kept, got, own in ((kept_0, got_0, own_0), (kept_1, after(got_1, query_0), own_1))
        ]
        source_0 = finish_of(0, dmid_0, query_0, grad_pairs[0])
        source_0, third = bind((source_0, third))
        source_1 = finish_of(1, dmid_1, after(grad_query[1], source_0), grad_pairs[1])
        source_0, source_1, *got_2 = settle([chain_q, chain_o], source_0, source_1, *got_2)
        (theirs,) = advance([chain_q], theirs)
        chain_o.got = after(chain_o.got, theirs)
        (theirs,) = advance([chain_o], theirs)
        layer_out = output(hids, downs, [theirs], middle, 0, rows)
        (layer_out,) = settle([chain_q, chain_o], layer_out)
        (held_q,) = bind((chain_q.ready(),))
        held_q, first, second, third = bind((held_q, first, second, third))
        chain_o.got = after(chain_o.got, held_q)
        held_q = net.z_sum(held_q)
        chain_o.ready()
        chain_o.move()
        got_3 = net.deal(third)
        mine_1, theirs_1 = net.dealt(first, got_1st)
        mine_2, theirs_2 = net.dealt(second, got_2)
        mine_3, theirs_3 = net.dealt(third, got_3)
        gate_grad, up_grad, down_grad, sums = widen(
            net.c[None].astype(jnp.int32),
            [mine_1, mine_2, mine_3],
            [theirs_1, theirs_2, theirs_3],
            gate_weight,
            up_weight,
        )
        held_q, sums = settle([chain_o], held_q, sums)
        got_q = net.deal(held_q)
        held_o = chain_o.total()
        got_o = net.deal(held_o)
        output_rows = [value[0] for value in net.dealt(held_o, got_o)]
        query_rows = [value[0] for value in net.dealt(held_q, got_q)]
        pair_rows = [value[:, head_width // 2 :] for value in query_rows]
        query_rows = [value[:, : head_width // 2] for value in query_rows]

        def columns_of(rows_of):
            mine, theirs = (value.astype(F32) for value in rows_of)
            return jnp.where(net.c == 0, mine, theirs), jnp.where(net.c == 0, theirs, mine)

        output_grad = jnp.concatenate(columns_of(output_rows), axis=1)
        query_grad = jnp.concatenate(columns_of(query_rows), axis=1)
        key_grad, value_grad = columns_of(pair_rows)
        down_grad = down_grad.T
        feed_gain_grad = sums[:, 0] / feed_gain.astype(F32)
        grad_source = [source_0, source_1]
    else:
        grad_query, grad_pairs, dmids = [], [], []
        for m in batches:
            dmid, grad_mixed = unmerge(middle[m], upstream, m, gain_two, output_full, backs[m])
            query_m, terms, own = back_of(m, grad_mixed, 0, KV_HEADS)
            dmids.append(dmid)
            grad_query.append(query_m)
            grad_pairs.append(pair_grads(net.sum_pairs(terms), own))
        lefts_one = [(turned_one, m) for m in batches]
        lefts_mixed = [(value, 0) for value in mixed]
        terms = [
            grad_terms(net.left_starts, lefts_mixed, dmids, False, size, 640),
            grad_terms(net.left_starts, lefts_one, grad_query, True, size, 640),
            grad_terms(net.left_starts, lefts_one, grad_pairs, True, size, 640),
        ]
        output_grad, query_grad, pair_grad = [net.whole_sum(term[0], 0) for term in terms]
        key_grad, value_grad = pair_grad[:, :pair_width], pair_grad[:, pair_width:]
        feed_grads = net.whole_sum(feed_terms[0][0].reshape(3, width, hidden_width), 1)
        gate_grad, up_grad, down_grad = feed_grads[0], feed_grads[1], feed_grads[2].T
        layer_out = output(hids, downs, [], middle, 0, rows)
        grad_source = [finish_of(m, dmids[m], grad_query[m], grad_pairs[m]) for m in batches]

    def gain_grad(gain, *both):
        terms = sum(jnp.sum(weight.astype(F32) * grad, axis=1) for weight, grad in both)
        return terms / gain.astype(F32)

    attention_gain_grad = gain_grad(
        attention_gain, (query_weight, query_grad), (key_weight, key_grad), (value_weight, value_grad)
    )
    if not fast:
        feed_gain_grad = gain_grad(feed_gain, (gate_weight, gate_grad), (up_weight, up_grad))
    return (
        layer_out.reshape(tokens.shape),
        jnp.stack(grad_source),
        query_grad,
        key_grad,
        value_grad,
        output_grad,
        attention_gain_grad,
        gate_grad,
        up_grad,
        down_grad,
        feed_gain_grad,
    )


def solution(mesh):
    return jax.shard_map(
        on_device,
        mesh=mesh,
        in_specs=(
            P(None, ("rep", "shard"), None),
            P(None, ("rep", "shard"), None),
            P(None, "rep", None),
            P("shard", None),
            P("shard", None),
            P("shard", None),
            P("shard", None),
            P("shard"),
            P("shard", None),
            P("shard", None),
            P(None, "shard"),
            P("shard"),
        ),
        out_specs=(
            P(None, ("rep", "shard"), None),
            P(None, ("rep", "shard"), None),
            P("shard", None),
            P("shard", None),
            P("shard", None),
            P("shard", None),
            P("shard"),
            P("shard", None),
            P("shard", None),
            P(None, "shard"),
            P("shard"),
        ),
        check_vma=False,
    )
```

```python
import jax
import jax.numpy as jnp
from jax import lax
from jax.experimental import pallas as pl
from jax.experimental.pallas import tpu as pltpu
from jax.sharding import PartitionSpec as P

HEADS = 20
KV_HEADS = 5
HEAD_DIM = 64
GROUP = HEADS // KV_HEADS
EPS = 1e-05
NEG = -1e30
F32 = jnp.float32
BF = jnp.bfloat16
VMEM_BYTES = 62 * 1024 * 1024


def mm(left, right):
    return jnp.dot(left, right, preferred_element_type=F32)


def ein(spec, left, right):
    return jnp.einsum(spec, left, right, preferred_element_type=F32)

def attend_kernel(gap_ref, q_ref, *refs, m, blocks):
    k_ref, v_ref, refs = refs[:blocks], refs[blocks : 2 * blocks], refs[2 * blocks :]
    kl_ref, vl_ref, a_ref, lse_ref = refs
    dim, blk = kl_ref.shape
    keys = jnp.concatenate([k_ref[j][...].T for j in range(blocks)] + [kl_ref[...].T], axis=0)
    ones = jnp.ones((16, (blocks+1)*blk), BF)
    vals = jnp.concatenate([jnp.concatenate([v_ref[j][...] for j in range(blocks)] + [vl_ref[...]], axis=1), ones], axis=0)
    diff = lax.broadcasted_iota(jnp.int32,(blk,blk),0) - lax.broadcasted_iota(jnp.int32,(blk,blk),1)
    n = blocks*blk
    for g in range(GROUP):
        for half in (0,1):
            q = q_ref[g*dim:(g+1)*dim, half*blk:(half+1)*blk]
            if half == 0:
                s = mm(keys[:n], q)
                s = jnp.concatenate([jnp.where(diff <= gap_ref[m, j], s[j*blk:(j+1)*blk], NEG) for j in range(blocks)], axis=0)
                vv = vals[:, :n]
            else:
                s = mm(keys, q)
                s = jnp.concatenate([s[:n], jnp.where(diff <= 0, s[n:], NEG)], axis=0)
                vv = vals
            top = jnp.max(s, axis=0, keepdims=True)
            p = jnp.exp(s - top).astype(BF)
            o = mm(vv, p)
            total = o[dim:dim+1]
            a_ref[g*dim:(g+1)*dim, half*blk:(half+1)*blk] = (o[:dim] / total).astype(BF)
            lse_ref[0, g:g+1, half*blk:(half+1)*blk] = top + jnp.log(total)

def attend(gap, qT, pairs, ownT, micro, m):
    blocks, blk = len(pairs), pairs[0].shape[1]
    rows = qT.shape[1] // micro
    return pl.pallas_call(
        lambda *refs: attend_kernel(*refs, m=m, blocks=blocks),
        grid=(KV_HEADS,),
        in_specs=[
            pl.BlockSpec(memory_space=pltpu.SMEM),
            pl.BlockSpec((GROUP * HEAD_DIM, rows), lambda h: (h, m)),
        ]
        + [pl.BlockSpec((HEAD_DIM, blk), lambda h: (h, 0))] * blocks
        + [pl.BlockSpec((HEAD_DIM, blk), lambda h: (KV_HEADS + h, 0))] * blocks
        + [
            pl.BlockSpec((HEAD_DIM, blk), lambda h: (h, 2 * m + 1)),
            pl.BlockSpec((HEAD_DIM, blk), lambda h: (KV_HEADS + h, 2 * m + 1)),
        ],
        out_specs=[
            pl.BlockSpec((GROUP * HEAD_DIM, rows), lambda h: (h, 0)),
            pl.BlockSpec((1, GROUP, rows), lambda h: (h, 0, 0)),
        ],
        out_shape=[
            jax.ShapeDtypeStruct((qT.shape[0], rows), BF),
            jax.ShapeDtypeStruct((KV_HEADS, GROUP, rows), F32),
        ],
        compiler_params=pltpu.CompilerParams(vmem_limit_bytes=VMEM_BYTES),
        cost_estimate=pl.CostEstimate(flops=3 * 10**10, bytes_accessed=5 * 10**6, transcendentals=12 * 10**6),
        name="attend",
    )(gap, qT, *pairs, *pairs, ownT, ownT)


def back_kernel(gap_ref, cos_ref, sin_ref, kcos_ref, ksin_ref, q_ref, a_ref, da_ref, lse_ref, *refs, m, blocks):
    k_ref, v_ref, refs = refs[:blocks], refs[blocks : 2 * blocks], refs[2 * blocks :]
    kl_ref, vl_ref, dq_ref, terms_ref, own_ref, p_scr, ds_scr = refs
    dim, blk = kl_ref.shape
    n = blocks*blk
    keysT = jnp.concatenate([k_ref[j][...] for j in range(blocks)] + [kl_ref[...]], axis=1)
    keys = jnp.concatenate([k_ref[j][...].T for j in range(blocks)] + [kl_ref[...].T], axis=0)
    vals = jnp.concatenate([v_ref[j][...].T for j in range(blocks)] + [vl_ref[...].T], axis=0)
    diff = lax.broadcasted_iota(jnp.int32,(blk,blk),0) - lax.broadcasted_iota(jnp.int32,(blk,blk),1)
    dk = None; dv = None
    for half in (0,1):
        span = n if half == 0 else n + blk
        cols = slice(half*blk, (half+1)*blk)
        qn = []; dan = []
        for g in range(GROUP):
            rows = slice(g*dim, (g+1)*dim)
            q = q_ref[rows, cols]; da = da_ref[rows, cols]
            qn.append(q.T); dan.append(da.T)
            delta = jnp.sum(da.astype(F32) * a_ref[rows, cols].astype(F32), axis=0, keepdims=True)
            lse = lse_ref[0, g:g+1, cols]
            s = mm(keys[:span], q)
            if half == 0:
                s = jnp.concatenate([jnp.where(diff <= gap_ref[m, j], s[j*blk:(j+1)*blk], NEG) for j in range(blocks)], axis=0)
            else:
                s = jnp.concatenate([s[:n], jnp.where(diff <= 0, s[n:], NEG)], axis=0)
            p = jnp.exp(s - lse)
            dp = mm(vals[:span], da)
            ds = (p * (dp - delta)).astype(BF)
            p_scr[:span, g*blk:(g+1)*blk] = p.astype(BF)
            ds_scr[:span, g*blk:(g+1)*blk] = ds
            dq = mm(keysT[:, :span], ds) * (HEAD_DIM ** -0.5)
            c = cos_ref[:, cols]; sn = sin_ref[:, cols]
            first = dq[:dim//2]; second = dq[dim//2:]
            dq_ref[rows, cols] = jnp.concatenate([first*c + second*sn, second*c - first*sn], axis=0).astype(BF)
        qn = jnp.concatenate(qn, axis=0); dan = jnp.concatenate(dan, axis=0)
        dkh = mm(ds_scr[:span], qn); dvh = mm(p_scr[:span], dan)
        if half == 0:
            dk, dv = dkh, dvh
        else:
            dk = jnp.concatenate([dk + dkh[:n], dkh[n:]], axis=0)
            dv = jnp.concatenate([dv + dvh[:n], dvh[n:]], axis=0)
    half = dim // 2
    for j in range(blocks + 1):
        cols = slice(j * blk, (j + 1) * blk)
        turned = dk[cols].T
        first, second = turned[:half], turned[half:]
        c, sn = kcos_ref[:, cols], ksin_ref[:, cols]
        turned = jnp.concatenate([first * c + second * sn, second * c - first * sn], axis=0).astype(BF)
        value = dv[cols].T.astype(BF)
        if j < blocks:
            terms_ref[j, 0, 0], terms_ref[j, 1, 0] = turned, value
        else:
            own_ref[0, 0], own_ref[1, 0] = turned, value


def attend_back(gap, cosT, sinT, kcos, ksin, qT, aT, daT, lse, pairs, ownT, micro, m, low, high):
    blocks, blk = len(pairs), pairs[0].shape[1]
    rows = qT.shape[1] // micro
    count = high - low
    query = pl.BlockSpec((GROUP * HEAD_DIM, rows), lambda h: (low + h, m))
    part = pl.BlockSpec((GROUP * HEAD_DIM, rows), lambda h: (low + h, 0))
    table = pl.BlockSpec((HEAD_DIM // 2, rows), lambda h: (0, m))
    keys = pl.BlockSpec((HEAD_DIM // 2, (blocks + 1) * blk), lambda h: (0, m))
    return pl.pallas_call(
        lambda *refs: back_kernel(*refs, m=m, blocks=blocks),
        grid=(count,),
        in_specs=[
            pl.BlockSpec(memory_space=pltpu.SMEM),
            table,
            table,
            keys,
            keys,
            query,
            part,
            part,
            pl.BlockSpec((1, GROUP, rows), lambda h: (low + h, 0, 0)),
        ]
        + [pl.BlockSpec((HEAD_DIM, blk), lambda h: (low + h, 0))] * blocks
        + [pl.BlockSpec((HEAD_DIM, blk), lambda h: (KV_HEADS + low + h, 0))] * blocks
        + [
            pl.BlockSpec((HEAD_DIM, blk), lambda h: (low + h, 2 * m + 1)),
            pl.BlockSpec((HEAD_DIM, blk), lambda h: (KV_HEADS + low + h, 2 * m + 1)),
        ],
        out_specs=[
            pl.BlockSpec((GROUP * HEAD_DIM, rows), lambda h: (h, 0)),
            pl.BlockSpec((blocks, 2, 1, HEAD_DIM, blk), lambda h: (0, 0, h, 0, 0)),
            pl.BlockSpec((2, 1, HEAD_DIM, blk), lambda h: (0, h, 0, 0)),
        ],
        out_shape=[
            jax.ShapeDtypeStruct((count * GROUP * HEAD_DIM, rows), BF),
            jax.ShapeDtypeStruct((blocks, 2, count, HEAD_DIM, blk), BF),
            jax.ShapeDtypeStruct((2, count, HEAD_DIM, blk), BF),
        ],
        scratch_shapes=[pltpu.VMEM(((blocks + 1) * blk, GROUP * blk), BF)] * 2,
        compiler_params=pltpu.CompilerParams(vmem_limit_bytes=VMEM_BYTES),
        cost_estimate=pl.CostEstimate(flops=2 * 10**9 * count, bytes_accessed=10**6 * count, transcendentals=0),
        name="attend_back",
    )(gap, cosT, sinT, kcos, ksin, qT, aT, daT, lse, *pairs, *pairs, ownT, ownT)


def nt(left, right):
    return lax.dot_general(left, right, (((1,), (1,)), ((), ())), preferred_element_type=F32)


def tn(left, right):
    return lax.dot_general(left, right, (((0,), (0,)), ((), ())), preferred_element_type=F32)


def project_kernel(row_ref, ht_ref, cos_ref, sin_ref, *refs, pieces, turned, scale):
    parts, (out_ref, whole_ref) = refs[:pieces], refs[pieces:]
    for i, part in enumerate(parts):
        whole_ref[pl.ds(pl.multiple_of(row_ref[i], 16), part.shape[0]), :] = part[...]
    raw = tn(whole_ref[...], ht_ref[...])
    half = HEAD_DIM // 2
    for head in range(raw.shape[0] // HEAD_DIM):
        at = head * HEAD_DIM
        if head < turned:
            first, second = raw[at : at + half], raw[at + half : at + HEAD_DIM]
            cosine, sine = cos_ref[...], sin_ref[...]
            out_ref[at : at + half] = (first * cosine - second * sine).astype(BF) * BF(scale)
            out_ref[at + half : at + HEAD_DIM] = (second * cosine + first * sine).astype(BF) * BF(scale)
        else:
            out_ref[at : at + HEAD_DIM] = raw[at : at + HEAD_DIM].astype(BF)


def project(starts, ht, cosine, sine, pieces, tile, turned, scale):
    width, tokens = ht.shape
    count = pieces[0].shape[1]
    table = pl.BlockSpec(cosine.shape, lambda i: (0, 0))
    return pl.pallas_call(
        lambda *refs: project_kernel(*refs, pieces=len(pieces), turned=turned, scale=scale),
        grid=(count // tile,),
        in_specs=[
            pl.BlockSpec(memory_space=pltpu.SMEM),
            pl.BlockSpec((width, tokens), lambda i: (0, 0)),
            table,
            table,
        ]
        + [pl.BlockSpec((piece.shape[0], tile), lambda i: (0, i)) for piece in pieces],
        out_specs=[
            pl.BlockSpec((tile, tokens), lambda i: (i, 0)),
            pl.BlockSpec((width, tile), lambda i: (0, i)),
        ],
        out_shape=[
            jax.ShapeDtypeStruct((count, tokens), BF),
            jax.ShapeDtypeStruct((width, count), BF),
        ],
        compiler_params=pltpu.CompilerParams(vmem_limit_bytes=VMEM_BYTES),
        cost_estimate=pl.CostEstimate(
            flops=2 * tokens * width * count, bytes_accessed=6 * width * count, transcendentals=0
        ),
        name="project",
    )(starts, ht, cosine, sine, *pieces)


def feed_kernel(row_ref, left_ref, *refs, sets, pieces, groups, split, step):
    hs, cs, refs = refs[:sets], refs[sets : 2 * sets], refs[2 * sets :]
    parts, refs = refs[:pieces], refs[pieces:]
    count = groups * len(split)
    grads, refs = refs[:count], refs[count:]
    backs, refs = refs[:sets], refs[sets:]
    hid_ref, down_ref, ht_ref, ct_ref, gate_ref, up_ref, dg_ref, dw_ref, acc_ref = refs
    tokens, width = hs[0].shape
    at = pl.program_id(0)

    @pl.when(at == 0)
    def _():
        for i in range(sets):
            ht_ref[:, i * tokens : (i + 1) * tokens] = hs[i][...].T
            ct_ref[:, i * tokens : (i + 1) * tokens] = cs[i][...].T
        acc_ref[...] = jnp.zeros_like(acc_ref)

    for k, whole in enumerate((gate_ref, up_ref, down_ref)):
        for i, part in enumerate(parts):
            whole[pl.ds(pl.multiple_of(row_ref[i], 16), part.shape[1]), :] = part[k]
    for i in range(sets):
        for b in range(0, tokens, step):
            rows, to = pl.ds(b, step), pl.ds(i * tokens + b, step)
            gate = mm(hs[i][rows, :], gate_ref[...])
            upper = mm(hs[i][rows, :], up_ref[...])
            grad = mm(cs[i][rows, :], down_ref[...])
            sigma = jax.nn.sigmoid(gate)
            silu = gate * sigma
            hid_ref[to, :] = (silu * upper).astype(BF)
            dg_ref[to, :] = (grad * upper * (sigma + silu * (1.0 - sigma))).astype(BF)
            dw_ref[to, :] = (grad * silu).astype(BF)
    times = ((ht_ref, dg_ref), (ht_ref, dw_ref), (ct_ref, hid_ref))
    for i in range(groups):
        for j, names in enumerate(split):
            out = grads[i * len(split) + j]
            rows = pl.ds(pl.multiple_of(left_ref[i], 16), out.shape[1])
            for at_name, name in enumerate(names):
                left, right = times[name]
                out[at_name] = mm(left[rows, :], right[...]).astype(BF)
    for b in range(0, sets * tokens, step):
        rows = pl.ds(b, step)
        acc_ref[rows, :] += nt(dg_ref[rows, :], gate_ref[...]) + nt(dw_ref[rows, :], up_ref[...])

    @pl.when(at == pl.num_programs(0) - 1)
    def _():
        for i, back in enumerate(backs):
            back[...] = acc_ref[pl.ds(i * tokens, tokens), :].astype(BF)


def feed(starts, left_starts, hs, cs, parts, sizes, rows, split=((0, 1, 2),), tile=256, step=256):
    sets = len(hs)
    tokens, width = rows, hs[0][0].shape[1]
    hidden = parts[0].shape[2]
    one = pl.Buffered(1)
    back = pl.BlockSpec((tokens, width), lambda i: (0, 0), pipeline_mode=one)
    toks = [pl.BlockSpec((tokens, width), lambda i, at=at: (at, 0), pipeline_mode=one) for _, at in hs + cs]
    smem = pl.BlockSpec(memory_space=pltpu.SMEM)
    counts = [(len(names), size) for size in sizes for names in split]
    grad_specs = [pl.BlockSpec((count, size, tile), lambda i: (0, 0, i)) for count, size in counts]
    grad_shapes = [jax.ShapeDtypeStruct((count, size, hidden), BF) for count, size in counts]
    results = pl.pallas_call(
        lambda *refs: feed_kernel(*refs, sets=sets, pieces=len(parts), groups=len(sizes), split=split, step=step),
        grid=(hidden // tile,),
        in_specs=[smem, smem]
        + toks
        + [pl.BlockSpec((3, part.shape[1], tile), lambda i: (0, 0, i)) for part in parts],
        out_specs=grad_specs
        + [back] * sets
        + [pl.BlockSpec((sets * tokens, tile), lambda i: (0, i)), pl.BlockSpec((width, tile), lambda i: (0, i))],
        out_shape=grad_shapes
        + [jax.ShapeDtypeStruct((tokens, width), BF)] * sets
        + [jax.ShapeDtypeStruct((sets * tokens, hidden), BF), jax.ShapeDtypeStruct((width, hidden), BF)],
        scratch_shapes=[pltpu.VMEM((width, sets * tokens), BF)] * 2
        + [pltpu.VMEM((width, tile), BF)] * 2
        + [pltpu.VMEM((sets * tokens, tile), BF)] * 2
        + [pltpu.VMEM((sets * tokens, width), F32)],
        compiler_params=pltpu.CompilerParams(vmem_limit_bytes=VMEM_BYTES),
        cost_estimate=pl.CostEstimate(
            flops=16 * sets * tokens * width * hidden,
            bytes_accessed=14 * width * hidden + 12 * sets * tokens * width,
            transcendentals=sets * tokens * hidden,
        ),
        name="feed",
    )(starts, left_starts, *[h for h, _ in hs], *[c for c, _ in cs], *parts)
    count = len(grad_specs)
    return results[:count], results[count : count + sets], results[-2], results[-1]


def prepare_kernel(x_ref, gain_ref, ht_ref):
    source = x_ref[...].astype(F32)
    scale = lax.rsqrt(jnp.mean(source * source, axis=-1, keepdims=True) + EPS)
    ht_ref[...] = (source * scale * gain_ref[...]).astype(BF).T


def prepare(x, gain, tile=256):
    tokens, width = x.shape
    return pl.pallas_call(
        prepare_kernel,
        grid=(tokens // tile,),
        in_specs=[pl.BlockSpec((tile, width), lambda i: (i, 0)), pl.BlockSpec((1, width), lambda i: (0, 0))],
        out_specs=pl.BlockSpec((width, tile), lambda i: (0, i)),
        out_shape=jax.ShapeDtypeStruct((width, tokens), BF),
        compiler_params=pltpu.CompilerParams(vmem_limit_bytes=VMEM_BYTES),
        cost_estimate=pl.CostEstimate(flops=0, bytes_accessed=6 * 10**6, transcendentals=0),
        name="prepare",
    )(x, gain)


def merge_kernel(row_ref, at_ref, x_ref, gain_ref, *refs, pieces):
    if pieces == 1:
        whole_ref, mid_ref, h_ref = refs
    else:
        parts, (mid_ref, h_ref, whole_ref) = refs[:pieces], refs[pieces:]
        for i, part in enumerate(parts):
            whole_ref[pl.ds(pl.multiple_of(row_ref[i], 16), part.shape[0]), :] = part[...]
    middle = x_ref[...].astype(F32) + tn(at_ref[...], whole_ref[...])
    scale = lax.rsqrt(jnp.mean(middle * middle, axis=-1, keepdims=True) + EPS)
    mid_ref[...] = middle
    h_ref[...] = (middle * scale * gain_ref[...]).astype(BF)


def merge(starts, at, x, m, gain, pieces):
    head_width, tokens = at.shape
    width = x.shape[1]
    row = pl.BlockSpec((tokens, width), lambda i: (0, 0))
    outs = [row, row]
    shapes = [jax.ShapeDtypeStruct((tokens, width), F32), jax.ShapeDtypeStruct((tokens, width), BF)]
    if len(pieces) > 1:
        outs.append(pl.BlockSpec((head_width, width), lambda i: (0, 0)))
        shapes.append(jax.ShapeDtypeStruct((head_width, width), BF))
    return pl.pallas_call(
        lambda *refs: merge_kernel(*refs, pieces=len(pieces)),
        grid=(1,),
        in_specs=[
            pl.BlockSpec(memory_space=pltpu.SMEM),
            pl.BlockSpec((head_width, tokens), lambda i: (0, 0)),
            pl.BlockSpec((tokens, width), lambda i: (m, 0)),
            pl.BlockSpec((1, width), lambda i: (0, 0)),
        ]
        + [pl.BlockSpec(piece.shape, lambda i: (0, 0)) for piece in pieces],
        out_specs=outs,
        out_shape=shapes,
        compiler_params=pltpu.CompilerParams(vmem_limit_bytes=VMEM_BYTES),
        cost_estimate=pl.CostEstimate(
            flops=2 * tokens * width * head_width, bytes_accessed=16 * 10**6, transcendentals=0
        ),
        name="merge",
    )(starts, at, x, gain, *pieces)


def unmerge_kernel(mid_ref, c_ref, gain_ref, whole_ref, *refs):
    backs, (dmid_ref, da_ref) = refs[:-2], refs[-2:]
    middle = mid_ref[...]
    scale = lax.rsqrt(jnp.mean(middle * middle, axis=-1, keepdims=True) + EPS)
    unit = middle * scale
    grad = backs[0][...].astype(F32)
    for back in backs[1:]:
        grad = grad + back[...].astype(F32)
    weighted = grad * gain_ref[...]
    mean = jnp.mean(weighted * unit, axis=-1, keepdims=True)
    dmid = (c_ref[...].astype(F32) + scale * (weighted - unit * mean)).astype(BF)
    dmid_ref[...] = dmid
    da_ref[...] = nt(whole_ref[...], dmid).astype(BF)


def unmerge(mid, c, m, gain, whole, backs, tile=256):
    tokens, width = mid.shape
    head_width = whole.shape[0]
    row = pl.BlockSpec((tile, width), lambda i: (i, 0))
    return pl.pallas_call(
        unmerge_kernel,
        grid=(tokens // tile,),
        in_specs=[
            row,
            pl.BlockSpec((tile, width), lambda i: (m * (tokens // tile) + i, 0)),
            pl.BlockSpec((1, width), lambda i: (0, 0)),
            pl.BlockSpec((head_width, width), lambda i: (0, 0)),
        ]
        + [row] * len(backs),
        out_specs=[row, pl.BlockSpec((head_width, tile), lambda i: (0, i))],
        out_shape=[
            jax.ShapeDtypeStruct((tokens, width), BF),
            jax.ShapeDtypeStruct((head_width, tokens), BF),
        ],
        compiler_params=pltpu.CompilerParams(vmem_limit_bytes=VMEM_BYTES),
        cost_estimate=pl.CostEstimate(
            flops=2 * tokens * width * head_width, bytes_accessed=16 * 10**6, transcendentals=0
        ),
        name="unmerge",
    )(mid, c, gain, whole, *backs)


def terms_kernel(left_ref, *refs, count, turned):
    lefts, rights, outs = refs[:count], refs[count : 2 * count], refs[2 * count :]
    times = nt if turned else mm
    for i, out in enumerate(outs):
        rows = pl.ds(pl.multiple_of(left_ref[i], 16), out.shape[0])
        total = times(lefts[0][rows, :], rights[0][...])
        for left, right in zip(lefts[1:], rights[1:]):
            total = total + times(left[rows, :], right[...])
        out[...] = total.astype(BF)


def grad_terms(left_starts, lefts, rights, turned, size, tile):
    columns = rights[0].shape[0 if turned else 1]
    span = rights[0].shape[1 if turned else 0]
    count = left_starts.shape[0]
    if turned:
        right_specs = [pl.BlockSpec((tile, span), lambda i: (i, 0)) for _ in rights]
    else:
        right_specs = [pl.BlockSpec((span, tile), lambda i: (0, i)) for _ in rights]
    left_specs = [pl.BlockSpec((left.shape[0], span), lambda i, at=at: (0, at)) for left, at in lefts]
    return pl.pallas_call(
        lambda *refs: terms_kernel(*refs, count=len(lefts), turned=turned),
        grid=(columns // tile,),
        in_specs=[pl.BlockSpec(memory_space=pltpu.SMEM)] + left_specs + right_specs,
        out_specs=[pl.BlockSpec((size, tile), lambda i: (0, i))] * count,
        out_shape=[jax.ShapeDtypeStruct((size, columns), BF)] * count,
        compiler_params=pltpu.CompilerParams(vmem_limit_bytes=VMEM_BYTES),
        cost_estimate=pl.CostEstimate(
            flops=2 * len(lefts) * span * columns * size * count, bytes_accessed=8 * 10**6, transcendentals=0
        ),
        name="grad_terms",
    )(left_starts, *[left for left, _ in lefts], *rights)


def joint_kernel(left_ref, *refs, plan, sizes, outs):
    refs, outs = refs[:-outs], refs[-outs:]
    for i, out in enumerate(outs):
        rows = pl.ds(pl.multiple_of(left_ref[i], 16), out.shape[0])
        column = 0
        for steps, count in zip(plan, sizes):
            total = 0.0
            for left, at, right, index in steps:
                value = refs[right][...] if index is None else refs[right][index]
                total = total + nt(refs[left][rows, at : at + value.shape[1]], value)
            out[:, column : column + count] = total.astype(BF)
            column += count


def joint_terms(left_starts, arrays, plan, sizes, size):
    whole = [pl.BlockSpec(array.shape, lambda i, n=array.ndim: (0,) * n) for array in arrays]
    outs = left_starts.shape[0]
    return pl.pallas_call(
        lambda *refs: joint_kernel(*refs, plan=plan, sizes=sizes, outs=outs),
        grid=(1,),
        in_specs=[pl.BlockSpec(memory_space=pltpu.SMEM)] + whole,
        out_specs=[pl.BlockSpec((size, sum(sizes)), lambda i: (0, 0))] * outs,
        out_shape=[jax.ShapeDtypeStruct((size, sum(sizes)), BF)] * outs,
        compiler_params=pltpu.CompilerParams(vmem_limit_bytes=VMEM_BYTES),
        cost_estimate=pl.CostEstimate(flops=6 * 10**9, bytes_accessed=14 * 10**6, transcendentals=0),
        name="joint_terms",
    )(left_starts, *arrays)


def output_kernel(*refs, parts, adds, firsts):
    hids, downs, refs = refs[:parts], refs[parts : 2 * parts], refs[2 * parts :]
    adds, firsts, out_ref = refs[:adds], refs[adds:-1], refs[-1]
    total = nt(hids[0][...], downs[0][...])
    for hid, down in zip(hids[1:], downs[1:]):
        total = total + nt(hid[...], down[...])
    for add in adds:
        total = total + add[...].astype(F32)
    if not firsts:
        out_ref[...] = total.astype(BF)
    for i, first in enumerate(firsts):

        @pl.when(pl.program_id(0) == i)
        def _():
            out_ref[...] = (total + first[...]).astype(BF)


def output(hids, downs, adds, firsts, skip, tile):
    width = downs[0].shape[0]
    row = pl.BlockSpec((tile, width), lambda i: (i, 0))
    return pl.pallas_call(
        lambda *refs: output_kernel(*refs, parts=len(hids), adds=len(adds), firsts=len(firsts)),
        grid=(2,),
        in_specs=[pl.BlockSpec((tile, hid.shape[1]), lambda i: (skip + i, 0)) for hid in hids]
        + [pl.BlockSpec(down.shape, lambda i: (0, 0)) for down in downs]
        + [row] * len(adds)
        + [pl.BlockSpec((tile, width), lambda i: (0, 0))] * len(firsts),
        out_specs=row,
        out_shape=jax.ShapeDtypeStruct((2 * tile, width), BF),
        compiler_params=pltpu.CompilerParams(vmem_limit_bytes=VMEM_BYTES),
        cost_estimate=pl.CostEstimate(flops=5 * 10**9, bytes_accessed=16 * 10**6, transcendentals=0),
        name="output",
    )(*hids, *downs, *adds, *firsts)


def finish_kernel(x_ref, gain_ref, dmid_ref, dq_ref, dp_ref, query_ref, pair_ref, out_ref):
    source = x_ref[...].astype(F32)
    scale = lax.rsqrt(jnp.mean(source * source, axis=-1, keepdims=True) + EPS)
    unit = source * scale
    grad = (mm(query_ref[...], dq_ref[...]) + mm(pair_ref[...], dp_ref[...])).T
    weighted = grad * gain_ref[...]
    mean = jnp.mean(weighted * unit, axis=-1, keepdims=True)
    out_ref[...] = (dmid_ref[...].astype(F32) + scale * (weighted - unit * mean)).astype(BF)


def finish(x, m, gain, dmid, dq, dp, query, pair, tile=256):
    tokens, width = dmid.shape
    row = pl.BlockSpec((tile, width), lambda i: (i, 0))
    return pl.pallas_call(
        finish_kernel,
        grid=(tokens // tile,),
        in_specs=[
            pl.BlockSpec((tile, width), lambda i: (m * (tokens // tile) + i, 0)),
            pl.BlockSpec((1, width), lambda i: (0, 0)),
            row,
            pl.BlockSpec((dq.shape[0], tile), lambda i: (0, i)),
            pl.BlockSpec((dp.shape[0], tile), lambda i: (0, i)),
            pl.BlockSpec(query.shape, lambda i: (0, 0)),
            pl.BlockSpec(pair.shape, lambda i: (0, 0)),
        ],
        out_specs=row,
        out_shape=jax.ShapeDtypeStruct((tokens, width), BF),
        compiler_params=pltpu.CompilerParams(vmem_limit_bytes=VMEM_BYTES),
        cost_estimate=pl.CostEstimate(
            flops=2 * tokens * width * (dq.shape[0] + dp.shape[0]), bytes_accessed=12 * 10**6, transcendentals=0
        ),
        name="finish",
    )(x, gain, dmid, dq, dp, query, pair)


def widen_kernel(core_ref, *refs, parts, counts):
    mine, theirs, refs = refs[:parts], refs[parts : 2 * parts], refs[2 * parts :]
    gate_ref, up_ref, gate_grad, up_grad, down_grad, sums_ref = refs
    step = pl.program_id(0)
    tiles = sum(counts)
    at = step % tiles
    picked = None
    low = 0
    for part, other, count in zip(mine, theirs, counts):
        here = jnp.where(step < tiles, part[...], other[...])
        picked = here if picked is None else jnp.where(at < low, picked, here)
        low += count
    picked = picked.astype(F32)
    gate_grad[...] = picked[0]
    up_grad[...] = picked[1]
    down_grad[...] = picked[2]

    @pl.when(step == 0)
    def _():
        sums_ref[...] = jnp.zeros_like(sums_ref)

    terms = gate_ref[...].astype(F32) * picked[0] + up_ref[...].astype(F32) * picked[1]
    sums_ref[...] += jnp.sum(terms, axis=1, keepdims=True)


def widen(core, mine, theirs, gate, up, tile=256):
    rows, hidden = gate.shape
    counts = [part.shape[2] // tile for part in mine]
    tiles = sum(counts)
    lows = [sum(counts[:i]) for i in range(len(counts))]

    def place(step, core):
        return (core[0] ^ (step // tiles)) * tiles + step % tiles

    def inside(step, low, count):
        return jnp.minimum(jnp.maximum(step - low, 0), count - 1)

    mine_specs = [
        pl.BlockSpec((3, rows, tile), lambda i, core, low=low, count=count: (0, 0, inside(i, low, count)))
        for low, count in zip(lows, counts)
    ]
    their_specs = [
        pl.BlockSpec((3, rows, tile), lambda i, core, low=low, count=count: (0, 0, inside(i - tiles, low, count)))
        for low, count in zip(lows, counts)
    ]
    wide = pl.BlockSpec((rows, tile), lambda i, core: (0, place(i, core)))
    return pl.pallas_call(
        lambda *refs: widen_kernel(*refs, parts=len(mine), counts=counts),
        grid_spec=pltpu.PrefetchScalarGridSpec(
            num_scalar_prefetch=1,
            grid=(2 * tiles,),
            in_specs=mine_specs + their_specs + [wide, wide],
            out_specs=[wide, wide, wide, pl.BlockSpec((rows, 1), lambda i, core: (0, 0))],
        ),
        out_shape=[
            jax.ShapeDtypeStruct((rows, hidden), F32),
            jax.ShapeDtypeStruct((rows, hidden), F32),
            jax.ShapeDtypeStruct((rows, hidden), F32),
            jax.ShapeDtypeStruct((rows, 1), F32),
        ],
        compiler_params=pltpu.CompilerParams(vmem_limit_bytes=VMEM_BYTES),
        cost_estimate=pl.CostEstimate(flops=0, bytes_accessed=26 * 10**6, transcendentals=0),
        name="widen",
    )(core, *mine, *theirs, gate, up)


def partner(value, axis, size, bit):
    return lax.ppermute(value, axis, [(i, i ^ bit) for i in range(size)])


def after(value, *others):
    return lax.optimization_barrier((value,) + others)[0]


def pick(value, index, axis):
    return lax.dynamic_index_in_dim(value, index, axis, keepdims=False)


def pair_up(mine, other, index, axis):
    first = jnp.where(index == 0, mine, other)
    second = jnp.where(index == 0, other, mine)
    return jnp.stack([first, second], axis=axis)


class Fast:
    chip = 2

    def __init__(self, rows):
        self.rows = rows
        member, rep = lax.axis_index("shard"), lax.axis_index("rep")
        self.member, self.rep_index = member, rep
        self.c, self.y, self.z, self.far = member % 2, rep % 2, (rep // 2) % 2, rep // 4
        self.order = [member, member ^ 2, member ^ 1, member ^ 3]
        across = member // 2
        self.feed_starts = jnp.stack([across * 2 * rows, (1 - across) * 2 * rows]).astype(jnp.int32)
        self.feed_sizes = (2 * rows, 2 * rows)
        self.starts = jnp.stack([which * rows for which in self.order]).astype(jnp.int32)
        self.left_starts = self.feed_starts

    def x(self, value):
        return partner(value, "shard", 4, 2)

    def core(self, value):
        return partner(value, "shard", 4, 1)

    def rep(self, value, bit):
        return partner(value, "rep", 8, bit)

    def pieces(self, value, behind=None):
        across = self.x(value)
        return [value, across, self.core(value), self.core(across)]


    def feed_columns(self, columns):
        return self.c * (columns // 2), columns // 2

    def feed_core(self, shards, low, high, columns):
        half = columns // 2

        def cut(which):
            return jnp.stack([lax.dynamic_slice_in_dim(s, which * half + low, high - low, 1) for s in shards])

        mine, theirs = cut(self.c), cut(1 - self.c)
        both = pair_up(mine, self.core(theirs), self.c, 1)
        return both.reshape(3, 2 * self.rows, high - low)

    def feed_eighth(self, both):
        flat = both.reshape(-1, both.shape[2])
        eighth = flat.shape[0] // 8
        return self.x(lax.dynamic_slice_in_dim(flat, self.rep_index * eighth, eighth, 0))

    def feed_parts(self, both, eighth):
        return [both, self.spread(eighth).reshape(both.shape)]

    def gather_pairs(self, sent):
        both = jnp.stack([sent, self.x(sent)])
        return jnp.concatenate([both, self.core(both)], axis=0)

    def spread(self, eighth):
        return lax.all_gather(eighth, "rep", axis=0, tiled=True)

    def z_sum(self, value, order=(0, 1)):
        lines = [[at for at in range(8) if at % 2 == y] for y in order]
        return lax.psum(value, "rep", axis_index_groups=lines)

    def deal(self, held):
        first, second = [], []
        for at in range(32):
            rep, member = at // 4, at % 4
            y, c = rep % 2, member % 2
            here, there = rep * 4 + member - c + y, (rep ^ 1) * 4 + member - c + y
            if c == y:
                first.append((at, there))
            else:
                first.append((at, here))
                second.append((at, there))
        return [lax.ppermute(held, ("rep", "shard"), pairs) for pairs in (first, second)]

    def dealt(self, held, got):
        stay = self.c == self.y
        return jnp.where(stay, held, got[0]), jnp.where(stay, got[0], got[1])


class Chain:
    def __init__(self, net, kept, outward, count=1):
        self.net, self.stage, self.got = net, 0, None
        self.shape = (count, 2, kept.shape[0] // (2 * count), kept.shape[1])
        self.parts, self.out = [kept], outward

    def total(self):
        return sum(part.astype(F32) for part in self.parts + [self.got]).astype(BF)

    def ready(self):
        if self.stage == 1:
            parts = [part.reshape(self.shape) for part in self.parts + [self.got]]
            y = self.net.y
            self.out = sum(pick(part, 1 - y, 1).astype(F32) for part in parts).astype(BF)
            self.parts = [pick(part, y, 1) for part in parts]
        elif self.stage > 1:
            self.out = self.total()
            self.parts = [self.out]
        return self.out

    def move(self):
        if self.stage == 0:
            self.got = self.net.x(self.out)
        else:
            self.got = self.net.rep(self.out, (1, 2, 4)[self.stage - 1])
        self.stage += 1


def settle(chains, *others):
    values = lax.optimization_barrier(tuple(chain.got for chain in chains) + others)
    for chain, value in zip(chains, values):
        chain.got = value
    return values[len(chains) :]


def advance(chains, *others):
    outs = [chain.ready() for chain in chains]
    values = lax.optimization_barrier(tuple(outs) + others)
    for chain, value in zip(chains, values):
        chain.out = value
        chain.move()
    return values[len(chains) :]


class General:
    chip = 1

    def __init__(self, rows):
        shards = lax.axis_size("shard")
        self.rows, self.shards = rows, shards
        self.member = lax.axis_index("shard")
        self.order = [jnp.int32(i) for i in range(shards)]
        self.starts = jnp.arange(shards, dtype=jnp.int32) * rows
        self.feed_starts = self.starts
        self.left_starts = jnp.zeros((1,), jnp.int32)
        self.feed_sizes = (shards * rows,)

    def pieces(self, value):
        whole = lax.all_gather(value, "shard", axis=0)
        return [whole[i] for i in range(self.shards)]

    def feed_core(self, shards, low, high, columns):
        return jnp.stack([shard[:, low:high] for shard in shards])

    def gather_pairs(self, sent):
        return lax.all_gather(sent, "shard", axis=0)

    def sum_pairs(self, terms):
        return lax.psum_scatter(terms, "shard", scatter_dimension=0, tiled=False).astype(F32)

    def whole_sum(self, terms, axis):
        owned = lax.psum_scatter(terms, "shard", scatter_dimension=axis, tiled=True)
        return lax.psum(owned, "rep").astype(F32)


def on_device(
    tokens,
    cotangent,
    block_map,
    query_weight,
    key_weight,
    value_weight,
    output_weight,
    attention_gain,
    gate_weight,
    up_weight,
    down_weight,
    feed_gain,
):
    shards = lax.axis_size("shard")
    fast = shards == 4 and lax.axis_size("rep") == 8
    micro, rows, width = tokens.shape
    block = rows // 2
    total = micro * rows
    shard_rows = query_weight.shape[0]
    net = Fast(shard_rows) if fast else General(shard_rows)
    head_width = HEADS * HEAD_DIM
    pair_width = KV_HEADS * HEAD_DIM
    hidden_width = gate_weight.shape[1]
    batches = range(micro)

    gain_pieces = net.pieces(jnp.stack([attention_gain, feed_gain], axis=1))
    gains = jnp.zeros((width, 2), BF)
    for i, piece in enumerate(gain_pieces):
        gains = lax.dynamic_update_slice_in_dim(gains, piece, net.starts[i], 0)
    gain_one = gains[:, 0].astype(F32)[None, :]
    gain_two = gains[:, 1].astype(F32)[None, :]
    pair_pieces = net.pieces(jnp.concatenate([key_weight, value_weight], axis=1))
    feed_shards = [gate_weight, up_weight, down_weight.T]
    columns = hidden_width // net.chip
    cuts = [0, 512, 1280, columns] if fast else [0, columns]

    blocks_here = block_map[:, 0]
    own_block = lax.dynamic_index_in_dim(blocks_here, net.member, axis=1, keepdims=False)
    others = jnp.stack(
        [lax.dynamic_index_in_dim(blocks_here, which, axis=1, keepdims=False) for which in net.order],
        axis=1,
    )
    gap = ((own_block[:, None] - others) * block).astype(jnp.int32)
    inside = jnp.arange(block, dtype=jnp.int32)
    place = jnp.concatenate(
        [
            own_block[:, None] * block + inside[None, :],
            jnp.broadcast_to(block * shards + inside[None, :], (micro, block)),
        ],
        axis=1,
    ).reshape(total)
    half = HEAD_DIM // 2
    freq = jnp.exp(jnp.arange(half, dtype=F32) * (-2.0 * jnp.log(10000.0) / HEAD_DIM))
    angle = freq[:, None] * place.astype(F32)[None, :]
    cosine, sine = jnp.cos(angle), jnp.sin(angle)

    key_place = jnp.concatenate(
        [
            (others[:, :, None] * block + inside).reshape(micro, -1),
            jnp.broadcast_to(block * shards + inside[None, :], (micro, block)),
        ],
        axis=1,
    ).reshape(-1)
    key_angle = freq[:, None] * key_place.astype(F32)[None, :]
    key_cosine, key_sine = jnp.cos(key_angle), jnp.sin(key_angle)

    source = tokens.reshape(total, width)
    turned_one = prepare(source, gain_one)
    upstream = cotangent.reshape(total, width)
    if fast:
        bind = lax.optimization_barrier

        def core_of(part, *others):
            shards_after = [after(shard, *others) if others else shard for shard in feed_shards]
            return net.feed_core(shards_after, cuts[part], cuts[part + 1], hidden_width)

        feed_cores = [core_of(0)]
        query_across = net.x(after(query_weight, pair_pieces[1]))
        pair_across = after(pair_pieces[1], turned_one)
        pair_pieces = [pair_pieces[0], pair_across, pair_pieces[2], net.core(pair_across)]
        own_pairs, pair_full = project(net.starts, turned_one, cosine, sine, pair_pieces, 640, KV_HEADS, 1.0)
        sent = [own_pairs[:, m * rows : m * rows + block] for m in batches]
        across = [net.x(part) for part in sent]
        across[0], turned_q = bind((across[0], turned_one))
        query_across = after(query_across, sent[1])
        query_pieces = [query_weight, query_across, net.core(query_weight), net.core(query_across)]
        pairs = [[sent[0], across[0], net.core(sent[0]), net.core(across[0])]]
        query, query_full = project(net.starts, turned_q, cosine, sine, query_pieces, 640, HEADS, HEAD_DIM**-0.5)
        eighths = [net.feed_eighth(after(part, across[0])) for part in feed_cores]
        moved = net.core(after(upstream, across[0]))
        upstream_all = [(upstream, m) for m in batches] + [(moved, m) for m in batches]
        turned_other = net.core(after(turned_one, across[0]))
        output_across = net.x(after(output_weight, across[0]))
        mixed_0, log_0 = attend(gap, query, pairs[0], own_pairs, micro, 0)
        mixed_0, output_across, across[1], eighth_0 = bind((mixed_0, output_across, across[1], eighths[0]))
        feed_parts = [net.feed_parts(feed_cores[0], eighth_0)]
        pairs.append([sent[1], across[1], net.core(sent[1]), net.core(across[1])])
        feed_cores += [core_of(1, mixed_0), core_of(2, mixed_0)]
        eighth_1, eighth_2 = [net.feed_eighth(part) for part in feed_cores[1:]]
        output_pieces = [output_weight, output_across, net.core(output_weight), net.core(output_across)]
        mixed_1, log_1 = attend(after(gap, mixed_0), query, pairs[1], own_pairs, micro, 1)
        mixed_1, eighth_1, eighth_2, *output_pieces[2:] = bind((mixed_1, eighth_1, eighth_2, *output_pieces[2:]))
        feed_parts += [net.feed_parts(feed_cores[1], eighth_1), net.feed_parts(feed_cores[2], eighth_2)]
        mixed, log_total = [mixed_0, mixed_1], [log_0, log_1]
        mixed_all = mixed + [net.core(value) for value in mixed]
        middle_0, normed_0, output_full = merge(
            net.starts, after(mixed_0, mixed_1), source, 0, gain_two, output_pieces
        )
        middle_1, normed_1 = merge(net.starts, mixed_1, source, 1, gain_two, [output_full])
        middle, normed_two = [middle_0, middle_1], [normed_0, normed_1]
        normed_all = [(value, 0) for value in normed_two] + [(net.core(value), 0) for value in normed_two]
    else:
        own_pairs, pair_full = project(net.starts, turned_one, cosine, sine, pair_pieces, 640, KV_HEADS, 1.0)
        pairs = [list(net.gather_pairs(own_pairs[:, m * rows : m * rows + block])) for m in batches]
        query_pieces = net.pieces(query_weight)
        query, query_full = project(net.starts, turned_one, cosine, sine, query_pieces, 640, HEADS, HEAD_DIM**-0.5)
        feed_parts = [net.pieces(jnp.stack(feed_shards))]
        output_pieces = net.pieces(output_weight)
        mixed, log_total, middle, normed_two = [], [], [], []
        for m in batches:
            mixed_m, log_m = attend(gap, query, pairs[m], own_pairs, micro, m)
            middle_m, normed_m, output_full = merge(net.starts, mixed_m, source, m, gain_two, output_pieces)
            mixed.append(mixed_m)
            log_total.append(log_m)
            middle.append(middle_m)
            normed_two.append(normed_m)
        normed_all = [(value, 0) for value in normed_two]
        upstream_all = [(upstream, m) for m in batches]

    backs = [[] for _ in batches]
    hids, downs, feed_terms, ones = [], [], [], []
    starts = net.feed_starts
    for k, parts in enumerate(feed_parts):
        split = ((0, 1), (2,)) if fast and k == 1 else ((0, 1, 2),)
        grads, backs_here, hid, down = feed(
            starts, net.left_starts, normed_all, upstream_all, parts, net.feed_sizes, rows, split
        )
        feed_terms.append(grads)
        if fast and k == 2:
            settled = settle(ones[:2], *backs_here, hid)
            backs_here, hid = settled[:-1], settled[-1]
        for m in batches:
            backs[m].append(backs_here[m])
            if fast:
                backs[m].append(net.core(backs_here[micro + m]))
        if fast:
            grads = [grad.reshape(-1, grad.shape[-1]) for grad in grads]
            ones += [Chain(net, grads[j], grads[len(split) + j], len(names)) for j, names in enumerate(split)]
        hids.append(hid)
        downs.append(down)
        starts = after(net.feed_starts, hid)
        if fast and k == 0:
            prompt = jnp.concatenate(
                [turned_one[:, m * rows : m * rows + block] for m in batches], axis=1
            )
            prompt_across = net.x(after(prompt, normed_two[-1]))
            starts, prompt_across = bind((starts, prompt_across))
            prompts = [prompt, prompt_across, net.core(prompt), net.core(prompt_across)]
            ones[0].move()
        elif fast and k == 1:
            (starts,) = settle(ones[:1], starts)
            (starts,) = advance(ones[:1], starts)
            ones[1].move()
    size = net.feed_sizes[0]

    def back_of(m, grad_mixed, low, high):
        return attend_back(
            gap, cosine, sine, key_cosine, key_sine, query, mixed[m], grad_mixed, log_total[m], pairs[m], own_pairs, micro, m, low, high
        )

    def pair_grads(summed, own_terms):
        return jnp.concatenate([summed.astype(BF), own_terms], axis=-1).reshape(2 * pair_width, rows)

    def finish_of(m, dmid, grad_query, grad_pairs):
        return finish(source, m, gain_one, dmid, grad_query, grad_pairs, query_full, pair_full)

    if fast:
        lefts_one = [(turned_one, 0), (turned_one, 1), (turned_other, 0), (turned_other, 1)]
        lefts_mixed = [(value, 0) for value in mixed_all]
        part_1, part_2, part_3, part_4 = ones

        def split(value, axis):
            size = value.shape[axis] // 2
            return [lax.dynamic_slice_in_dim(value, at * size, size, axis) for at in (net.c, 1 - net.c)]

        middle_0, first = advance([part_2, part_3], after(middle[0], backs[0][-1]), part_1.total())
        first = net.z_sum(first)
        def kind(value, which):
            return lax.dynamic_index_in_dim(value, which, value.ndim - 4, keepdims=False)

        def pairs_out(terms, own):
            extra = jnp.concatenate([kind(terms[:2], 1 - net.c), kind(own, 1 - net.c)[None]], axis=0)
            return net.core(terms[2:]), net.core(extra)

        def pairs_chip(terms, own, away, extra):
            mine = kind(terms, net.c).astype(F32)
            theirs = jnp.concatenate([kind(away, net.c), extra[:2]], axis=0).astype(F32)
            return (mine + theirs).astype(BF).reshape(4, pair_width, block), [
                value.reshape(pair_width, block) for value in (kind(own, net.c), extra[2])
            ]

        dmid_0, mixed_0 = unmerge(middle_0, upstream, 0, gain_two, output_full, backs[0])
        theirs = output(hids, [downs[0], downs[1], after(downs[2], mixed_0)], [], [], micro, rows)
        mixed_0, theirs = settle([part_2, part_3], mixed_0, theirs)
        theirs = net.core(theirs)
        (mixed_0,) = advance([part_3, part_4], mixed_0)
        query_0, terms_0, own_0 = back_of(0, mixed_0, 0, KV_HEADS)
        query_0, terms_0, theirs, first = settle([part_3], query_0, terms_0, theirs, first)
        away_0, extra_0 = pairs_out(terms_0, own_0)
        second = jnp.concatenate([part_2.total(), part_3.total()], axis=0)
        halves_0 = split(after(dmid_0, query_0), 1)
        second, middle_1 = bind((second, after(middle[1], query_0)))
        second = net.z_sum(second)
        dmid_1, mixed_1 = unmerge(middle_1, upstream, 1, gain_two, output_full, backs[1])
        halves_1 = split(dmid_1, 1)
        mixed_1, moved_0, moved_1, away_0, extra_0 = settle(
            [part_4], mixed_1, halves_0[1], halves_1[1], away_0, extra_0
        )
        kept_0 = (terms_0[:2].astype(F32) + away_0.astype(F32)).astype(BF)
        mixed_1, moved_0, moved_1, out_0 = advance([part_4], mixed_1, moved_0, moved_1, kept_0[1])
        got_0 = net.x(out_0)
        dmid_halves = [halves_0[0], halves_1[0], net.core(moved_0), net.core(moved_1)]
        output_terms = grad_terms(net.left_starts, lefts_mixed, dmid_halves, False, size, 640)
        chain_o = Chain(net, *output_terms)
        (mixed_1,) = advance([chain_o], mixed_1)
        got_1st = net.deal(after(first, mixed_1))
        query_1, terms_1, own_1 = back_of(1, mixed_1, 0, KV_HEADS)

        query_1, got_0, second = settle([part_4, chain_o], query_1, got_0, second)
        grad_query = [query_0, query_1]
        halves = [split(value, 0) for value in grad_query]
        moved_0, moved_1, terms_1 = bind((halves[0][1], halves[1][1], terms_1))
        away_1, extra_1 = pairs_out(terms_1, own_1)
        query_halves = [halves[0][0], halves[1][0], net.core(moved_0), net.core(moved_1)]
        blocks_0, owns_0 = pairs_chip(terms_0, own_0, away_0, extra_0)
        third = net.z_sum(part_4.total(), (1, 0))
        (out_o,) = bind((chain_o.ready(),))
        away_1, extra_1, out_o, *settled = bind((away_1, extra_1, out_o, *query_halves, *got_1st))
        query_halves, got_1st = settled[:4], settled[4:]
        kept_1 = (terms_1[:2].astype(F32) + away_1.astype(F32)).astype(BF)
        blocks_1, owns_1 = pairs_chip(terms_1, own_1, away_1, extra_1)
        out_1, blocks_1, chain_o.out = bind((kept_1[1], blocks_1, out_o))
        chain_o.move()
        got_1 = net.x(out_1)
        got_2 = net.deal(after(second, out_1))
        arrays = [turned_one, turned_other, *prompts, *query_halves, blocks_0, *owns_0, blocks_1, *owns_1]
        steps_query = [(m // 2, (m % 2) * rows, 6 + m, None) for m in range(4)]
        steps_pair = []
        for m in batches:
            steps_pair += [(2 + j, m * block, 10 + 3 * m, j) for j in range(4)]
            steps_pair += [(j, m * rows + block, 11 + 3 * m + j, None) for j in range(2)]
        query_terms = joint_terms(
            net.left_starts, arrays, [steps_query, steps_pair], [head_width // 2, pair_width], size
        )
        got_1, *query_terms = bind((got_1, *query_terms))
        chain_q = Chain(net, *query_terms)
        (query_0,) = advance([chain_q], query_0)
        grad_pairs = [
            pair_grads(kept[0].astype(F32) + got.astype(F32), own)
            for kept, got, own in ((kept_0, got_0, own_0), (kept_1, after(got_1, query_0), own_1))
        ]
        source_0 = finish_of(0, dmid_0, query_0, grad_pairs[0])
        source_0, third = bind((source_0, third))
        source_1 = finish_of(1, dmid_1, after(grad_query[1], source_0), grad_pairs[1])
        source_0, source_1, *got_2 = settle([chain_q, chain_o], source_0, source_1, *got_2)
        (theirs,) = advance([chain_q], theirs)
        chain_o.got = after(chain_o.got, theirs)
        (theirs,) = advance([chain_o], theirs)
        layer_out = output(hids, downs, [theirs], middle, 0, rows)
        (layer_out,) = settle([chain_q, chain_o], layer_out)
        (held_q,) = bind((chain_q.ready(),))
        held_q, first, second, third = bind((held_q, first, second, third))
        chain_o.got = after(chain_o.got, held_q)
        held_q = net.z_sum(held_q)
        chain_o.ready()
        chain_o.move()
        got_3 = net.deal(third)
        mine_1, theirs_1 = net.dealt(first, got_1st)
        mine_2, theirs_2 = net.dealt(second, got_2)
        mine_3, theirs_3 = net.dealt(third, got_3)
        gate_grad, up_grad, down_grad, sums = widen(
            net.c[None].astype(jnp.int32),
            [mine_1, mine_2, mine_3],
            [theirs_1, theirs_2, theirs_3],
            gate_weight,
            up_weight,
        )
        grad_source = jnp.stack([source_0, source_1])
        sums, grad_source = settle([chain_o], sums, grad_source)
        held_o = chain_o.total()
        got_o = net.deal(held_o)
        held_q, *got_o = bind((held_q, *got_o))
        got_q = net.deal(held_q)
        output_rows = [value[0] for value in net.dealt(held_o, got_o)]
        query_rows = [value[0] for value in net.dealt(held_q, got_q)]
        pair_rows = [value[:, head_width // 2 :] for value in query_rows]
        query_rows = [value[:, : head_width // 2] for value in query_rows]

        def columns_of(rows_of):
            mine, theirs = (value.astype(F32) for value in rows_of)
            return jnp.where(net.c == 0, mine, theirs), jnp.where(net.c == 0, theirs, mine)

        output_grad = jnp.concatenate(columns_of(output_rows), axis=1)
        query_grad = jnp.concatenate(columns_of(query_rows), axis=1)
        key_grad, value_grad = columns_of(pair_rows)
        down_grad = down_grad.T
        feed_gain_grad = sums[:, 0] / feed_gain.astype(F32)
    else:
        grad_query, grad_pairs, dmids = [], [], []
        for m in batches:
            dmid, grad_mixed = unmerge(middle[m], upstream, m, gain_two, output_full, backs[m])
            query_m, terms, own = back_of(m, grad_mixed, 0, KV_HEADS)
            dmids.append(dmid)
            grad_query.append(query_m)
            grad_pairs.append(pair_grads(net.sum_pairs(terms), own))
        lefts_one = [(turned_one, m) for m in batches]
        lefts_mixed = [(value, 0) for value in mixed]
        terms = [
            grad_terms(net.left_starts, lefts_mixed, dmids, False, size, 640),
            grad_terms(net.left_starts, lefts_one, grad_query, True, size, 640),
            grad_terms(net.left_starts, lefts_one, grad_pairs, True, size, 640),
        ]
        output_grad, query_grad, pair_grad = [net.whole_sum(term[0], 0) for term in terms]
        key_grad, value_grad = pair_grad[:, :pair_width], pair_grad[:, pair_width:]
        feed_grads = net.whole_sum(feed_terms[0][0].reshape(3, width, hidden_width), 1)
        gate_grad, up_grad, down_grad = feed_grads[0], feed_grads[1], feed_grads[2].T
        layer_out = output(hids, downs, [], middle, 0, rows)
        grad_source = jnp.stack([finish_of(m, dmids[m], grad_query[m], grad_pairs[m]) for m in batches])

    def gain_grad(gain, *both):
        terms = sum(jnp.sum(weight.astype(F32) * grad, axis=1) for weight, grad in both)
        return terms / gain.astype(F32)

    attention_gain_grad = gain_grad(
        attention_gain, (query_weight, query_grad), (key_weight, key_grad), (value_weight, value_grad)
    )
    if not fast:
        feed_gain_grad = gain_grad(feed_gain, (gate_weight, gate_grad), (up_weight, up_grad))
    return (
        layer_out.reshape(tokens.shape),
        grad_source,
        query_grad,
        key_grad,
        value_grad,
        output_grad,
        attention_gain_grad,
        gate_grad,
        up_grad,
        down_grad,
        feed_gain_grad,
    )


def solution(mesh):
    return jax.shard_map(
        on_device,
        mesh=mesh,
        in_specs=(
            P(None, ("rep", "shard"), None),
            P(None, ("rep", "shard"), None),
            P(None, "rep", None),
            P("shard", None),
            P("shard", None),
            P("shard", None),
            P("shard", None),
            P("shard"),
            P("shard", None),
            P("shard", None),
            P(None, "shard"),
            P("shard"),
        ),
        out_specs=(
            P(None, ("rep", "shard"), None),
            P(None, ("rep", "shard"), None),
            P("shard", None),
            P("shard", None),
            P("shard", None),
            P("shard", None),
            P("shard"),
            P("shard", None),
            P("shard", None),
            P(None, "shard"),
            P("shard"),
        ),
        check_vma=False,
    )
```

```python
import jax
import jax.numpy as jnp
from jax import lax
from jax.experimental import pallas as pl
from jax.experimental.pallas import tpu as pltpu
from jax.sharding import PartitionSpec as P

HEADS = 20
KV_HEADS = 5
HEAD_DIM = 64
GROUP = HEADS // KV_HEADS
EPS = 1e-05
NEG = -1e30
F32 = jnp.float32
BF = jnp.bfloat16
VMEM_BYTES = 62 * 1024 * 1024


def mm(left, right):
    return jnp.dot(left, right, preferred_element_type=F32)


def ein(spec, left, right):
    return jnp.einsum(spec, left, right, preferred_element_type=F32)

def attend_kernel(gap_ref, q_ref, *refs, m, blocks):
    k_ref, v_ref, refs = refs[:blocks], refs[blocks : 2 * blocks], refs[2 * blocks :]
    kl_ref, vl_ref, a_ref, lse_ref = refs
    dim, blk = kl_ref.shape
    keys = jnp.concatenate([k_ref[j][...].T for j in range(blocks)] + [kl_ref[...].T], axis=0)
    ones = jnp.ones((16, (blocks+1)*blk), BF)
    vals = jnp.concatenate([jnp.concatenate([v_ref[j][...] for j in range(blocks)] + [vl_ref[...]], axis=1), ones], axis=0)
    diff = lax.broadcasted_iota(jnp.int32,(blk,blk),0) - lax.broadcasted_iota(jnp.int32,(blk,blk),1)
    n = blocks*blk
    for g in range(GROUP):
        for half in (0,1):
            q = q_ref[g*dim:(g+1)*dim, half*blk:(half+1)*blk]
            if half == 0:
                s = mm(keys[:n], q)
                s = jnp.concatenate([jnp.where(diff <= gap_ref[m, j], s[j*blk:(j+1)*blk], NEG) for j in range(blocks)], axis=0)
                vv = vals[:, :n]
            else:
                s = mm(keys, q)
                s = jnp.concatenate([s[:n], jnp.where(diff <= 0, s[n:], NEG)], axis=0)
                vv = vals
            top = jnp.max(s, axis=0, keepdims=True)
            p = jnp.exp(s - top).astype(BF)
            o = mm(vv, p)
            total = o[dim:dim+1]
            a_ref[g*dim:(g+1)*dim, half*blk:(half+1)*blk] = (o[:dim] / total).astype(BF)
            lse_ref[0, g:g+1, half*blk:(half+1)*blk] = top + jnp.log(total)

def attend(gap, qT, pairs, ownT, micro, m):
    blocks, blk = len(pairs), pairs[0].shape[1]
    rows = qT.shape[1] // micro
    return pl.pallas_call(
        lambda *refs: attend_kernel(*refs, m=m, blocks=blocks),
        grid=(KV_HEADS,),
        in_specs=[
            pl.BlockSpec(memory_space=pltpu.SMEM),
            pl.BlockSpec((GROUP * HEAD_DIM, rows), lambda h: (h, m)),
        ]
        + [pl.BlockSpec((HEAD_DIM, blk), lambda h: (h, 0))] * blocks
        + [pl.BlockSpec((HEAD_DIM, blk), lambda h: (KV_HEADS + h, 0))] * blocks
        + [
            pl.BlockSpec((HEAD_DIM, blk), lambda h: (h, 2 * m + 1)),
            pl.BlockSpec((HEAD_DIM, blk), lambda h: (KV_HEADS + h, 2 * m + 1)),
        ],
        out_specs=[
            pl.BlockSpec((GROUP * HEAD_DIM, rows), lambda h: (h, 0)),
            pl.BlockSpec((1, GROUP, rows), lambda h: (h, 0, 0)),
        ],
        out_shape=[
            jax.ShapeDtypeStruct((qT.shape[0], rows), BF),
            jax.ShapeDtypeStruct((KV_HEADS, GROUP, rows), F32),
        ],
        compiler_params=pltpu.CompilerParams(vmem_limit_bytes=VMEM_BYTES),
        cost_estimate=pl.CostEstimate(flops=3 * 10**10, bytes_accessed=5 * 10**6, transcendentals=12 * 10**6),
        name="attend",
    )(gap, qT, *pairs, *pairs, ownT, ownT)


def back_kernel(gap_ref, cos_ref, sin_ref, kcos_ref, ksin_ref, q_ref, a_ref, da_ref, lse_ref, *refs, m, blocks):
    k_ref, v_ref, refs = refs[:blocks], refs[blocks : 2 * blocks], refs[2 * blocks :]
    kl_ref, vl_ref, dq_ref, terms_ref, own_ref, p_scr, ds_scr = refs
    dim, blk = kl_ref.shape
    n = blocks*blk
    keysT = jnp.concatenate([k_ref[j][...] for j in range(blocks)] + [kl_ref[...]], axis=1)
    keys = jnp.concatenate([k_ref[j][...].T for j in range(blocks)] + [kl_ref[...].T], axis=0)
    vals = jnp.concatenate([v_ref[j][...].T for j in range(blocks)] + [vl_ref[...].T], axis=0)
    diff = lax.broadcasted_iota(jnp.int32,(blk,blk),0) - lax.broadcasted_iota(jnp.int32,(blk,blk),1)
    dk = None; dv = None
    for half in (0,1):
        span = n if half == 0 else n + blk
        cols = slice(half*blk, (half+1)*blk)
        qn = []; dan = []
        for g in range(GROUP):
            rows = slice(g*dim, (g+1)*dim)
            q = q_ref[rows, cols]; da = da_ref[rows, cols]
            qn.append(q.T); dan.append(da.T)
            delta = jnp.sum(da.astype(F32) * a_ref[rows, cols].astype(F32), axis=0, keepdims=True)
            lse = lse_ref[0, g:g+1, cols]
            s = mm(keys[:span], q)
            if half == 0:
                s = jnp.concatenate([jnp.where(diff <= gap_ref[m, j], s[j*blk:(j+1)*blk], NEG) for j in range(blocks)], axis=0)
            else:
                s = jnp.concatenate([s[:n], jnp.where(diff <= 0, s[n:], NEG)], axis=0)
            p = jnp.exp(s - lse)
            dp = mm(vals[:span], da)
            ds = (p * (dp - delta)).astype(BF)
            p_scr[:span, g*blk:(g+1)*blk] = p.astype(BF)
            ds_scr[:span, g*blk:(g+1)*blk] = ds
            dq = mm(keysT[:, :span], ds) * (HEAD_DIM ** -0.5)
            c = cos_ref[:, cols]; sn = sin_ref[:, cols]
            first = dq[:dim//2]; second = dq[dim//2:]
            dq_ref[rows, cols] = jnp.concatenate([first*c + second*sn, second*c - first*sn], axis=0).astype(BF)
        qn = jnp.concatenate(qn, axis=0); dan = jnp.concatenate(dan, axis=0)
        dkh = mm(ds_scr[:span], qn); dvh = mm(p_scr[:span], dan)
        if half == 0:
            dk, dv = dkh, dvh
        else:
            dk = jnp.concatenate([dk + dkh[:n], dkh[n:]], axis=0)
            dv = jnp.concatenate([dv + dvh[:n], dvh[n:]], axis=0)
    half = dim // 2
    for j in range(blocks + 1):
        cols = slice(j * blk, (j + 1) * blk)
        turned = dk[cols].T
        first, second = turned[:half], turned[half:]
        c, sn = kcos_ref[:, cols], ksin_ref[:, cols]
        turned = jnp.concatenate([first * c + second * sn, second * c - first * sn], axis=0).astype(BF)
        value = dv[cols].T.astype(BF)
        if j < blocks:
            terms_ref[j, 0, 0], terms_ref[j, 1, 0] = turned, value
        else:
            own_ref[0, 0], own_ref[1, 0] = turned, value


def attend_back(gap, cosT, sinT, kcos, ksin, qT, aT, daT, lse, pairs, ownT, micro, m, low, high):
    blocks, blk = len(pairs), pairs[0].shape[1]
    rows = qT.shape[1] // micro
    count = high - low
    query = pl.BlockSpec((GROUP * HEAD_DIM, rows), lambda h: (low + h, m))
    part = pl.BlockSpec((GROUP * HEAD_DIM, rows), lambda h: (low + h, 0))
    table = pl.BlockSpec((HEAD_DIM // 2, rows), lambda h: (0, m))
    keys = pl.BlockSpec((HEAD_DIM // 2, (blocks + 1) * blk), lambda h: (0, m))
    return pl.pallas_call(
        lambda *refs: back_kernel(*refs, m=m, blocks=blocks),
        grid=(count,),
        in_specs=[
            pl.BlockSpec(memory_space=pltpu.SMEM),
            table,
            table,
            keys,
            keys,
            query,
            part,
            part,
            pl.BlockSpec((1, GROUP, rows), lambda h: (low + h, 0, 0)),
        ]
        + [pl.BlockSpec((HEAD_DIM, blk), lambda h: (low + h, 0))] * blocks
        + [pl.BlockSpec((HEAD_DIM, blk), lambda h: (KV_HEADS + low + h, 0))] * blocks
        + [
            pl.BlockSpec((HEAD_DIM, blk), lambda h: (low + h, 2 * m + 1)),
            pl.BlockSpec((HEAD_DIM, blk), lambda h: (KV_HEADS + low + h, 2 * m + 1)),
        ],
        out_specs=[
            pl.BlockSpec((GROUP * HEAD_DIM, rows), lambda h: (h, 0)),
            pl.BlockSpec((blocks, 2, 1, HEAD_DIM, blk), lambda h: (0, 0, h, 0, 0)),
            pl.BlockSpec((2, 1, HEAD_DIM, blk), lambda h: (0, h, 0, 0)),
        ],
        out_shape=[
            jax.ShapeDtypeStruct((count * GROUP * HEAD_DIM, rows), BF),
            jax.ShapeDtypeStruct((blocks, 2, count, HEAD_DIM, blk), BF),
            jax.ShapeDtypeStruct((2, count, HEAD_DIM, blk), BF),
        ],
        scratch_shapes=[pltpu.VMEM(((blocks + 1) * blk, GROUP * blk), BF)] * 2,
        compiler_params=pltpu.CompilerParams(vmem_limit_bytes=VMEM_BYTES),
        cost_estimate=pl.CostEstimate(flops=8 * 10**9 * count, bytes_accessed=10**6 * count, transcendentals=0),
        name="attend_back",
    )(gap, cosT, sinT, kcos, ksin, qT, aT, daT, lse, *pairs, *pairs, ownT, ownT)


def nt(left, right):
    return lax.dot_general(left, right, (((1,), (1,)), ((), ())), preferred_element_type=F32)


def tn(left, right):
    return lax.dot_general(left, right, (((0,), (0,)), ((), ())), preferred_element_type=F32)


def project_kernel(row_ref, ht_ref, cos_ref, sin_ref, *refs, pieces, turned, scale):
    parts, (out_ref, whole_ref) = refs[:pieces], refs[pieces:]
    for i, part in enumerate(parts):
        whole_ref[pl.ds(pl.multiple_of(row_ref[i], 16), part.shape[0]), :] = part[...]
    raw = tn(whole_ref[...], ht_ref[...])
    half = HEAD_DIM // 2
    for head in range(raw.shape[0] // HEAD_DIM):
        at = head * HEAD_DIM
        if head < turned:
            first, second = raw[at : at + half], raw[at + half : at + HEAD_DIM]
            cosine, sine = cos_ref[...], sin_ref[...]
            out_ref[at : at + half] = (first * cosine - second * sine).astype(BF) * BF(scale)
            out_ref[at + half : at + HEAD_DIM] = (second * cosine + first * sine).astype(BF) * BF(scale)
        else:
            out_ref[at : at + HEAD_DIM] = raw[at : at + HEAD_DIM].astype(BF)


def project(starts, ht, cosine, sine, pieces, tile, turned, scale):
    width, tokens = ht.shape
    count = pieces[0].shape[1]
    table = pl.BlockSpec(cosine.shape, lambda i: (0, 0))
    return pl.pallas_call(
        lambda *refs: project_kernel(*refs, pieces=len(pieces), turned=turned, scale=scale),
        grid=(count // tile,),
        in_specs=[
            pl.BlockSpec(memory_space=pltpu.SMEM),
            pl.BlockSpec((width, tokens), lambda i: (0, 0)),
            table,
            table,
        ]
        + [pl.BlockSpec((piece.shape[0], tile), lambda i: (0, i)) for piece in pieces],
        out_specs=[
            pl.BlockSpec((tile, tokens), lambda i: (i, 0)),
            pl.BlockSpec((width, tile), lambda i: (0, i)),
        ],
        out_shape=[
            jax.ShapeDtypeStruct((count, tokens), BF),
            jax.ShapeDtypeStruct((width, count), BF),
        ],
        compiler_params=pltpu.CompilerParams(vmem_limit_bytes=VMEM_BYTES),
        cost_estimate=pl.CostEstimate(
            flops=2 * tokens * width * count, bytes_accessed=6 * width * count, transcendentals=0
        ),
        name="project",
    )(starts, ht, cosine, sine, *pieces)


def feed_kernel(row_ref, left_ref, *refs, sets, pieces, groups, split, step):
    hs, cs, refs = refs[:sets], refs[sets : 2 * sets], refs[2 * sets :]
    parts, refs = refs[:pieces], refs[pieces:]
    count = groups * len(split)
    grads, refs = refs[:count], refs[count:]
    backs, refs = refs[:sets], refs[sets:]
    hid_ref, down_ref, ht_ref, ct_ref, gate_ref, up_ref, dg_ref, dw_ref, acc_ref = refs
    tokens, width = hs[0].shape
    at = pl.program_id(0)

    @pl.when(at == 0)
    def _():
        for i in range(sets):
            ht_ref[:, i * tokens : (i + 1) * tokens] = hs[i][...].T
            ct_ref[:, i * tokens : (i + 1) * tokens] = cs[i][...].T
        acc_ref[...] = jnp.zeros_like(acc_ref)

    for k, whole in enumerate((gate_ref, up_ref, down_ref)):
        for i, part in enumerate(parts):
            whole[pl.ds(pl.multiple_of(row_ref[i], 16), part.shape[1]), :] = part[k]
    for i in range(sets):
        for b in range(0, tokens, step):
            rows, to = pl.ds(b, step), pl.ds(i * tokens + b, step)
            gate = mm(hs[i][rows, :], gate_ref[...])
            upper = mm(hs[i][rows, :], up_ref[...])
            grad = mm(cs[i][rows, :], down_ref[...])
            sigma = jax.nn.sigmoid(gate)
            silu = gate * sigma
            hid_ref[to, :] = (silu * upper).astype(BF)
            dg_ref[to, :] = (grad * upper * (sigma + silu * (1.0 - sigma))).astype(BF)
            dw_ref[to, :] = (grad * silu).astype(BF)
    times = ((ht_ref, dg_ref), (ht_ref, dw_ref), (ct_ref, hid_ref))
    for i in range(groups):
        for j, names in enumerate(split):
            out = grads[i * len(split) + j]
            rows = pl.ds(pl.multiple_of(left_ref[i], 16), out.shape[1])
            for at_name, name in enumerate(names):
                left, right = times[name]
                out[at_name] = mm(left[rows, :], right[...]).astype(BF)
    for b in range(0, sets * tokens, step):
        rows = pl.ds(b, step)
        acc_ref[rows, :] += nt(dg_ref[rows, :], gate_ref[...]) + nt(dw_ref[rows, :], up_ref[...])

    @pl.when(at == pl.num_programs(0) - 1)
    def _():
        for i, back in enumerate(backs):
            back[...] = acc_ref[pl.ds(i * tokens, tokens), :].astype(BF)


def feed(starts, left_starts, hs, cs, parts, sizes, rows, split=((0, 1, 2),), tile=256, step=256):
    sets = len(hs)
    tokens, width = rows, hs[0][0].shape[1]
    hidden = parts[0].shape[2]
    one = pl.Buffered(1)
    back = pl.BlockSpec((tokens, width), lambda i: (0, 0), pipeline_mode=one)
    toks = [pl.BlockSpec((tokens, width), lambda i, at=at: (at, 0), pipeline_mode=one) for _, at in hs + cs]
    smem = pl.BlockSpec(memory_space=pltpu.SMEM)
    counts = [(len(names), size) for size in sizes for names in split]
    grad_specs = [pl.BlockSpec((count, size, tile), lambda i: (0, 0, i)) for count, size in counts]
    grad_shapes = [jax.ShapeDtypeStruct((count, size, hidden), BF) for count, size in counts]
    results = pl.pallas_call(
        lambda *refs: feed_kernel(*refs, sets=sets, pieces=len(parts), groups=len(sizes), split=split, step=step),
        grid=(hidden // tile,),
        in_specs=[smem, smem]
        + toks
        + [pl.BlockSpec((3, part.shape[1], tile), lambda i: (0, 0, i)) for part in parts],
        out_specs=grad_specs
        + [back] * sets
        + [pl.BlockSpec((sets * tokens, tile), lambda i: (0, i)), pl.BlockSpec((width, tile), lambda i: (0, i))],
        out_shape=grad_shapes
        + [jax.ShapeDtypeStruct((tokens, width), BF)] * sets
        + [jax.ShapeDtypeStruct((sets * tokens, hidden), BF), jax.ShapeDtypeStruct((width, hidden), BF)],
        scratch_shapes=[pltpu.VMEM((width, sets * tokens), BF)] * 2
        + [pltpu.VMEM((width, tile), BF)] * 2
        + [pltpu.VMEM((sets * tokens, tile), BF)] * 2
        + [pltpu.VMEM((sets * tokens, width), F32)],
        compiler_params=pltpu.CompilerParams(vmem_limit_bytes=VMEM_BYTES),
        cost_estimate=pl.CostEstimate(
            flops=16 * sets * tokens * width * hidden,
            bytes_accessed=14 * width * hidden + 12 * sets * tokens * width,
            transcendentals=sets * tokens * hidden,
        ),
        name="feed",
    )(starts, left_starts, *[h for h, _ in hs], *[c for c, _ in cs], *parts)
    count = len(grad_specs)
    return results[:count], results[count : count + sets], results[-2], results[-1]


def prepare_kernel(x_ref, gain_ref, ht_ref):
    source = x_ref[...].astype(F32)
    scale = lax.rsqrt(jnp.mean(source * source, axis=-1, keepdims=True) + EPS)
    ht_ref[...] = (source * scale * gain_ref[...]).astype(BF).T


def prepare(x, gain, tile=256):
    tokens, width = x.shape
    return pl.pallas_call(
        prepare_kernel,
        grid=(tokens // tile,),
        in_specs=[pl.BlockSpec((tile, width), lambda i: (i, 0)), pl.BlockSpec((1, width), lambda i: (0, 0))],
        out_specs=pl.BlockSpec((width, tile), lambda i: (0, i)),
        out_shape=jax.ShapeDtypeStruct((width, tokens), BF),
        compiler_params=pltpu.CompilerParams(vmem_limit_bytes=VMEM_BYTES),
        cost_estimate=pl.CostEstimate(flops=0, bytes_accessed=6 * 10**6, transcendentals=0),
        name="prepare",
    )(x, gain)


def merge_kernel(row_ref, at_ref, x_ref, gain_ref, *refs, pieces):
    if pieces == 1:
        whole_ref, mid_ref, h_ref = refs
    else:
        parts, (mid_ref, h_ref, whole_ref) = refs[:pieces], refs[pieces:]
        for i, part in enumerate(parts):
            whole_ref[pl.ds(pl.multiple_of(row_ref[i], 16), part.shape[0]), :] = part[...]
    middle = x_ref[...].astype(F32) + tn(at_ref[...], whole_ref[...])
    scale = lax.rsqrt(jnp.mean(middle * middle, axis=-1, keepdims=True) + EPS)
    mid_ref[...] = middle
    h_ref[...] = (middle * scale * gain_ref[...]).astype(BF)


def merge(starts, at, x, m, gain, pieces):
    head_width, tokens = at.shape
    width = x.shape[1]
    row = pl.BlockSpec((tokens, width), lambda i: (0, 0))
    outs = [row, row]
    shapes = [jax.ShapeDtypeStruct((tokens, width), F32), jax.ShapeDtypeStruct((tokens, width), BF)]
    if len(pieces) > 1:
        outs.append(pl.BlockSpec((head_width, width), lambda i: (0, 0)))
        shapes.append(jax.ShapeDtypeStruct((head_width, width), BF))
    return pl.pallas_call(
        lambda *refs: merge_kernel(*refs, pieces=len(pieces)),
        grid=(1,),
        in_specs=[
            pl.BlockSpec(memory_space=pltpu.SMEM),
            pl.BlockSpec((head_width, tokens), lambda i: (0, 0)),
            pl.BlockSpec((tokens, width), lambda i: (m, 0)),
            pl.BlockSpec((1, width), lambda i: (0, 0)),
        ]
        + [pl.BlockSpec(piece.shape, lambda i: (0, 0)) for piece in pieces],
        out_specs=outs,
        out_shape=shapes,
        compiler_params=pltpu.CompilerParams(vmem_limit_bytes=VMEM_BYTES),
        cost_estimate=pl.CostEstimate(
            flops=2 * tokens * width * head_width, bytes_accessed=16 * 10**6, transcendentals=0
        ),
        name="merge",
    )(starts, at, x, gain, *pieces)


def unmerge_kernel(mid_ref, c_ref, gain_ref, whole_ref, *refs):
    backs, (dmid_ref, da_ref) = refs[:-2], refs[-2:]
    middle = mid_ref[...]
    scale = lax.rsqrt(jnp.mean(middle * middle, axis=-1, keepdims=True) + EPS)
    unit = middle * scale
    grad = backs[0][...].astype(F32)
    for back in backs[1:]:
        grad = grad + back[...].astype(F32)
    weighted = grad * gain_ref[...]
    mean = jnp.mean(weighted * unit, axis=-1, keepdims=True)
    dmid = (c_ref[...].astype(F32) + scale * (weighted - unit * mean)).astype(BF)
    dmid_ref[...] = dmid
    da_ref[...] = nt(whole_ref[...], dmid).astype(BF)


def unmerge(mid, c, m, gain, whole, backs, tile=256):
    tokens, width = mid.shape
    head_width = whole.shape[0]
    row = pl.BlockSpec((tile, width), lambda i: (i, 0))
    return pl.pallas_call(
        unmerge_kernel,
        grid=(tokens // tile,),
        in_specs=[
            row,
            pl.BlockSpec((tile, width), lambda i: (m * (tokens // tile) + i, 0)),
            pl.BlockSpec((1, width), lambda i: (0, 0)),
            pl.BlockSpec((head_width, width), lambda i: (0, 0)),
        ]
        + [row] * len(backs),
        out_specs=[row, pl.BlockSpec((head_width, tile), lambda i: (0, i))],
        out_shape=[
            jax.ShapeDtypeStruct((tokens, width), BF),
            jax.ShapeDtypeStruct((head_width, tokens), BF),
        ],
        compiler_params=pltpu.CompilerParams(vmem_limit_bytes=VMEM_BYTES),
        cost_estimate=pl.CostEstimate(
            flops=2 * tokens * width * head_width, bytes_accessed=16 * 10**6, transcendentals=0
        ),
        name="unmerge",
    )(mid, c, gain, whole, *backs)


def terms_kernel(left_ref, *refs, count, turned):
    lefts, rights, outs = refs[:count], refs[count : 2 * count], refs[2 * count :]
    times = nt if turned else mm
    for i, out in enumerate(outs):
        rows = pl.ds(pl.multiple_of(left_ref[i], 16), out.shape[0])
        total = times(lefts[0][rows, :], rights[0][...])
        for left, right in zip(lefts[1:], rights[1:]):
            total = total + times(left[rows, :], right[...])
        out[...] = total.astype(BF)


def grad_terms(left_starts, lefts, rights, turned, size, tile):
    columns = rights[0].shape[0 if turned else 1]
    span = rights[0].shape[1 if turned else 0]
    count = left_starts.shape[0]
    if turned:
        right_specs = [pl.BlockSpec((tile, span), lambda i: (i, 0)) for _ in rights]
    else:
        right_specs = [pl.BlockSpec((span, tile), lambda i: (0, i)) for _ in rights]
    left_specs = [pl.BlockSpec((left.shape[0], span), lambda i, at=at: (0, at)) for left, at in lefts]
    return pl.pallas_call(
        lambda *refs: terms_kernel(*refs, count=len(lefts), turned=turned),
        grid=(columns // tile,),
        in_specs=[pl.BlockSpec(memory_space=pltpu.SMEM)] + left_specs + right_specs,
        out_specs=[pl.BlockSpec((size, tile), lambda i: (0, i))] * count,
        out_shape=[jax.ShapeDtypeStruct((size, columns), BF)] * count,
        compiler_params=pltpu.CompilerParams(vmem_limit_bytes=VMEM_BYTES),
        cost_estimate=pl.CostEstimate(
            flops=2 * len(lefts) * span * columns * size * count, bytes_accessed=8 * 10**6, transcendentals=0
        ),
        name="grad_terms",
    )(left_starts, *[left for left, _ in lefts], *rights)


def joint_kernel(left_ref, *refs, plan, sizes, outs):
    refs, outs = refs[:-outs], refs[-outs:]
    for i, out in enumerate(outs):
        rows = pl.ds(pl.multiple_of(left_ref[i], 16), out.shape[0])
        column = 0
        for steps, count in zip(plan, sizes):
            total = 0.0
            for left, at, right, index in steps:
                value = refs[right][...] if index is None else refs[right][index]
                total = total + nt(refs[left][rows, at : at + value.shape[1]], value)
            out[:, column : column + count] = total.astype(BF)
            column += count


def joint_terms(left_starts, arrays, plan, sizes, size):
    whole = [pl.BlockSpec(array.shape, lambda i, n=array.ndim: (0,) * n) for array in arrays]
    outs = left_starts.shape[0]
    return pl.pallas_call(
        lambda *refs: joint_kernel(*refs, plan=plan, sizes=sizes, outs=outs),
        grid=(1,),
        in_specs=[pl.BlockSpec(memory_space=pltpu.SMEM)] + whole,
        out_specs=[pl.BlockSpec((size, sum(sizes)), lambda i: (0, 0))] * outs,
        out_shape=[jax.ShapeDtypeStruct((size, sum(sizes)), BF)] * outs,
        compiler_params=pltpu.CompilerParams(vmem_limit_bytes=VMEM_BYTES),
        cost_estimate=pl.CostEstimate(flops=6 * 10**9, bytes_accessed=14 * 10**6, transcendentals=0),
        name="joint_terms",
    )(left_starts, *arrays)


def output_kernel(*refs, parts, adds, firsts):
    hids, downs, refs = refs[:parts], refs[parts : 2 * parts], refs[2 * parts :]
    adds, firsts, out_ref = refs[:adds], refs[adds:-1], refs[-1]
    total = nt(hids[0][...], downs[0][...])
    for hid, down in zip(hids[1:], downs[1:]):
        total = total + nt(hid[...], down[...])
    for add in adds:
        total = total + add[...].astype(F32)
    if not firsts:
        out_ref[...] = total.astype(BF)
    for i, first in enumerate(firsts):

        @pl.when(pl.program_id(0) == i)
        def _():
            out_ref[...] = (total + first[...]).astype(BF)


def output(hids, downs, adds, firsts, skip, tile):
    width = downs[0].shape[0]
    row = pl.BlockSpec((tile, width), lambda i: (i, 0))
    return pl.pallas_call(
        lambda *refs: output_kernel(*refs, parts=len(hids), adds=len(adds), firsts=len(firsts)),
        grid=(2,),
        in_specs=[pl.BlockSpec((tile, hid.shape[1]), lambda i: (skip + i, 0)) for hid in hids]
        + [pl.BlockSpec(down.shape, lambda i: (0, 0)) for down in downs]
        + [row] * len(adds)
        + [pl.BlockSpec((tile, width), lambda i: (0, 0))] * len(firsts),
        out_specs=row,
        out_shape=jax.ShapeDtypeStruct((2 * tile, width), BF),
        compiler_params=pltpu.CompilerParams(vmem_limit_bytes=VMEM_BYTES),
        cost_estimate=pl.CostEstimate(flops=5 * 10**9, bytes_accessed=16 * 10**6, transcendentals=0),
        name="output",
    )(*hids, *downs, *adds, *firsts)


def finish_kernel(x_ref, gain_ref, dmid_ref, dq_ref, dp_ref, query_ref, pair_ref, out_ref):
    source = x_ref[...].astype(F32)
    scale = lax.rsqrt(jnp.mean(source * source, axis=-1, keepdims=True) + EPS)
    unit = source * scale
    grad = (mm(query_ref[...], dq_ref[...]) + mm(pair_ref[...], dp_ref[...])).T
    weighted = grad * gain_ref[...]
    mean = jnp.mean(weighted * unit, axis=-1, keepdims=True)
    out_ref[...] = (dmid_ref[...].astype(F32) + scale * (weighted - unit * mean)).astype(BF)


def finish(x, m, gain, dmid, dq, dp, query, pair, tile=256):
    tokens, width = dmid.shape
    row = pl.BlockSpec((tile, width), lambda i: (i, 0))
    return pl.pallas_call(
        finish_kernel,
        grid=(tokens // tile,),
        in_specs=[
            pl.BlockSpec((tile, width), lambda i: (m * (tokens // tile) + i, 0)),
            pl.BlockSpec((1, width), lambda i: (0, 0)),
            row,
            pl.BlockSpec((dq.shape[0], tile), lambda i: (0, i)),
            pl.BlockSpec((dp.shape[0], tile), lambda i: (0, i)),
            pl.BlockSpec(query.shape, lambda i: (0, 0)),
            pl.BlockSpec(pair.shape, lambda i: (0, 0)),
        ],
        out_specs=row,
        out_shape=jax.ShapeDtypeStruct((tokens, width), BF),
        compiler_params=pltpu.CompilerParams(vmem_limit_bytes=VMEM_BYTES),
        cost_estimate=pl.CostEstimate(
            flops=2 * tokens * width * (dq.shape[0] + dp.shape[0]), bytes_accessed=12 * 10**6, transcendentals=0
        ),
        name="finish",
    )(x, gain, dmid, dq, dp, query, pair)


def widen_kernel(core_ref, *refs, parts, counts):
    mine, theirs, refs = refs[:parts], refs[parts : 2 * parts], refs[2 * parts :]
    gate_ref, up_ref, gate_grad, up_grad, down_grad, sums_ref = refs
    step = pl.program_id(0)
    tiles = sum(counts)
    at = step % tiles
    picked = None
    low = 0
    for part, other, count in zip(mine, theirs, counts):
        here = jnp.where(step < tiles, part[...], other[...])
        picked = here if picked is None else jnp.where(at < low, picked, here)
        low += count
    picked = picked.astype(F32)
    gate_grad[...] = picked[0]
    up_grad[...] = picked[1]
    down_grad[...] = picked[2]

    @pl.when(step == 0)
    def _():
        sums_ref[...] = jnp.zeros_like(sums_ref)

    terms = gate_ref[...].astype(F32) * picked[0] + up_ref[...].astype(F32) * picked[1]
    sums_ref[...] += jnp.sum(terms, axis=1, keepdims=True)


def widen(core, mine, theirs, gate, up, tile=256):
    rows, hidden = gate.shape
    counts = [part.shape[2] // tile for part in mine]
    tiles = sum(counts)
    lows = [sum(counts[:i]) for i in range(len(counts))]

    def place(step, core):
        return (core[0] ^ (step // tiles)) * tiles + step % tiles

    def inside(step, low, count):
        return jnp.minimum(jnp.maximum(step - low, 0), count - 1)

    mine_specs = [
        pl.BlockSpec((3, rows, tile), lambda i, core, low=low, count=count: (0, 0, inside(i, low, count)))
        for low, count in zip(lows, counts)
    ]
    their_specs = [
        pl.BlockSpec((3, rows, tile), lambda i, core, low=low, count=count: (0, 0, inside(i - tiles, low, count)))
        for low, count in zip(lows, counts)
    ]
    wide = pl.BlockSpec((rows, tile), lambda i, core: (0, place(i, core)))
    return pl.pallas_call(
        lambda *refs: widen_kernel(*refs, parts=len(mine), counts=counts),
        grid_spec=pltpu.PrefetchScalarGridSpec(
            num_scalar_prefetch=1,
            grid=(2 * tiles,),
            in_specs=mine_specs + their_specs + [wide, wide],
            out_specs=[wide, wide, wide, pl.BlockSpec((rows, 1), lambda i, core: (0, 0))],
        ),
        out_shape=[
            jax.ShapeDtypeStruct((rows, hidden), F32),
            jax.ShapeDtypeStruct((rows, hidden), F32),
            jax.ShapeDtypeStruct((rows, hidden), F32),
            jax.ShapeDtypeStruct((rows, 1), F32),
        ],
        compiler_params=pltpu.CompilerParams(vmem_limit_bytes=VMEM_BYTES),
        cost_estimate=pl.CostEstimate(flops=0, bytes_accessed=26 * 10**6, transcendentals=0),
        name="widen",
    )(core, *mine, *theirs, gate, up)


def partner(value, axis, size, bit):
    return lax.ppermute(value, axis, [(i, i ^ bit) for i in range(size)])


def after(value, *others):
    return lax.optimization_barrier((value,) + others)[0]


def pick(value, index, axis):
    return lax.dynamic_index_in_dim(value, index, axis, keepdims=False)


def pair_up(mine, other, index, axis):
    first = jnp.where(index == 0, mine, other)
    second = jnp.where(index == 0, other, mine)
    return jnp.stack([first, second], axis=axis)


class Fast:
    chip = 2

    def __init__(self, rows):
        self.rows = rows
        member, rep = lax.axis_index("shard"), lax.axis_index("rep")
        self.member, self.rep_index = member, rep
        self.c, self.y, self.z, self.far = member % 2, rep % 2, (rep // 2) % 2, rep // 4
        self.order = [member, member ^ 2, member ^ 1, member ^ 3]
        across = member // 2
        self.feed_starts = jnp.stack([across * 2 * rows, (1 - across) * 2 * rows]).astype(jnp.int32)
        self.feed_sizes = (2 * rows, 2 * rows)
        self.starts = jnp.stack([which * rows for which in self.order]).astype(jnp.int32)
        self.left_starts = self.feed_starts

    def x(self, value):
        return partner(value, "shard", 4, 2)

    def core(self, value):
        return partner(value, "shard", 4, 1)

    def rep(self, value, bit):
        return partner(value, "rep", 8, bit)

    def pieces(self, value, behind=None):
        across = self.x(value)
        return [value, across, self.core(value), self.core(across)]


    def feed_columns(self, columns):
        return self.c * (columns // 2), columns // 2

    def feed_core(self, shards, low, high, columns):
        half = columns // 2

        def cut(which):
            return jnp.stack([lax.dynamic_slice_in_dim(s, which * half + low, high - low, 1) for s in shards])

        mine, theirs = cut(self.c), cut(1 - self.c)
        both = pair_up(mine, self.core(theirs), self.c, 1)
        return both.reshape(3, 2 * self.rows, high - low)

    def feed_eighth(self, both):
        flat = both.reshape(-1, both.shape[2])
        eighth = flat.shape[0] // 8
        return self.x(lax.dynamic_slice_in_dim(flat, self.rep_index * eighth, eighth, 0))

    def feed_parts(self, both, eighth):
        return [both, self.spread(eighth).reshape(both.shape)]

    def gather_pairs(self, sent):
        both = jnp.stack([sent, self.x(sent)])
        return jnp.concatenate([both, self.core(both)], axis=0)

    def spread(self, eighth):
        return lax.all_gather(eighth, "rep", axis=0, tiled=True)

    def z_sum(self, value, order=(0, 1)):
        lines = [[at for at in range(8) if at % 2 == y] for y in order]
        return lax.psum(value, "rep", axis_index_groups=lines)

    def deal(self, held):
        first, second = [], []
        for at in range(32):
            rep, member = at // 4, at % 4
            y, c = rep % 2, member % 2
            here, there = rep * 4 + member - c + y, (rep ^ 1) * 4 + member - c + y
            if c == y:
                first.append((at, there))
            else:
                first.append((at, here))
                second.append((at, there))
        return [lax.ppermute(held, ("rep", "shard"), pairs) for pairs in (first, second)]

    def dealt(self, held, got):
        stay = self.c == self.y
        return jnp.where(stay, held, got[0]), jnp.where(stay, got[0], got[1])


class Chain:
    def __init__(self, net, kept, outward, count=1):
        self.net, self.stage, self.got = net, 0, None
        self.shape = (count, 2, kept.shape[0] // (2 * count), kept.shape[1])
        self.parts, self.out = [kept], outward

    def total(self):
        return sum(part.astype(F32) for part in self.parts + [self.got]).astype(BF)

    def ready(self):
        if self.stage == 1:
            parts = [part.reshape(self.shape) for part in self.parts + [self.got]]
            y = self.net.y
            self.out = sum(pick(part, 1 - y, 1).astype(F32) for part in parts).astype(BF)
            self.parts = [pick(part, y, 1) for part in parts]
        elif self.stage > 1:
            self.out = self.total()
            self.parts = [self.out]
        return self.out

    def move(self):
        if self.stage == 0:
            self.got = self.net.x(self.out)
        else:
            self.got = self.net.rep(self.out, (1, 2, 4)[self.stage - 1])
        self.stage += 1


def settle(chains, *others):
    values = lax.optimization_barrier(tuple(chain.got for chain in chains) + others)
    for chain, value in zip(chains, values):
        chain.got = value
    return values[len(chains) :]


def advance(chains, *others):
    outs = [chain.ready() for chain in chains]
    values = lax.optimization_barrier(tuple(outs) + others)
    for chain, value in zip(chains, values):
        chain.out = value
        chain.move()
    return values[len(chains) :]


class General:
    chip = 1

    def __init__(self, rows):
        shards = lax.axis_size("shard")
        self.rows, self.shards = rows, shards
        self.member = lax.axis_index("shard")
        self.order = [jnp.int32(i) for i in range(shards)]
        self.starts = jnp.arange(shards, dtype=jnp.int32) * rows
        self.feed_starts = self.starts
        self.left_starts = jnp.zeros((1,), jnp.int32)
        self.feed_sizes = (shards * rows,)

    def pieces(self, value):
        whole = lax.all_gather(value, "shard", axis=0)
        return [whole[i] for i in range(self.shards)]

    def feed_core(self, shards, low, high, columns):
        return jnp.stack([shard[:, low:high] for shard in shards])

    def gather_pairs(self, sent):
        return lax.all_gather(sent, "shard", axis=0)

    def sum_pairs(self, terms):
        return lax.psum_scatter(terms, "shard", scatter_dimension=0, tiled=False).astype(F32)

    def whole_sum(self, terms, axis):
        owned = lax.psum_scatter(terms, "shard", scatter_dimension=axis, tiled=True)
        return lax.psum(owned, "rep").astype(F32)


def on_device(
    tokens,
    cotangent,
    block_map,
    query_weight,
    key_weight,
    value_weight,
    output_weight,
    attention_gain,
    gate_weight,
    up_weight,
    down_weight,
    feed_gain,
):
    shards = lax.axis_size("shard")
    fast = shards == 4 and lax.axis_size("rep") == 8
    micro, rows, width = tokens.shape
    block = rows // 2
    total = micro * rows
    shard_rows = query_weight.shape[0]
    net = Fast(shard_rows) if fast else General(shard_rows)
    head_width = HEADS * HEAD_DIM
    pair_width = KV_HEADS * HEAD_DIM
    hidden_width = gate_weight.shape[1]
    batches = range(micro)

    gain_pieces = net.pieces(jnp.stack([attention_gain, feed_gain], axis=1))
    gains = jnp.zeros((width, 2), BF)
    for i, piece in enumerate(gain_pieces):
        gains = lax.dynamic_update_slice_in_dim(gains, piece, net.starts[i], 0)
    gain_one = gains[:, 0].astype(F32)[None, :]
    gain_two = gains[:, 1].astype(F32)[None, :]
    pair_pieces = net.pieces(jnp.concatenate([key_weight, value_weight], axis=1))
    feed_shards = [gate_weight, up_weight, down_weight.T]
    columns = hidden_width // net.chip
    cuts = [0, 512, 1280, columns] if fast else [0, columns]

    blocks_here = block_map[:, 0]
    own_block = lax.dynamic_index_in_dim(blocks_here, net.member, axis=1, keepdims=False)
    others = jnp.stack(
        [lax.dynamic_index_in_dim(blocks_here, which, axis=1, keepdims=False) for which in net.order],
        axis=1,
    )
    gap = ((own_block[:, None] - others) * block).astype(jnp.int32)
    inside = jnp.arange(block, dtype=jnp.int32)
    place = jnp.concatenate(
        [
            own_block[:, None] * block + inside[None, :],
            jnp.broadcast_to(block * shards + inside[None, :], (micro, block)),
        ],
        axis=1,
    ).reshape(total)
    half = HEAD_DIM // 2
    freq = jnp.exp(jnp.arange(half, dtype=F32) * (-2.0 * jnp.log(10000.0) / HEAD_DIM))
    angle = freq[:, None] * place.astype(F32)[None, :]
    cosine, sine = jnp.cos(angle), jnp.sin(angle)

    key_place = jnp.concatenate(
        [
            (others[:, :, None] * block + inside).reshape(micro, -1),
            jnp.broadcast_to(block * shards + inside[None, :], (micro, block)),
        ],
        axis=1,
    ).reshape(-1)
    key_angle = freq[:, None] * key_place.astype(F32)[None, :]
    key_cosine, key_sine = jnp.cos(key_angle), jnp.sin(key_angle)

    source = tokens.reshape(total, width)
    turned_one = prepare(source, gain_one)
    upstream = cotangent.reshape(total, width)
    if fast:
        bind = lax.optimization_barrier

        def core_of(part, *others):
            shards_after = [after(shard, *others) if others else shard for shard in feed_shards]
            return net.feed_core(shards_after, cuts[part], cuts[part + 1], hidden_width)

        feed_cores = [core_of(0)]
        query_across = net.x(after(query_weight, pair_pieces[1]))
        pair_across = after(pair_pieces[1], turned_one)
        pair_pieces = [pair_pieces[0], pair_across, pair_pieces[2], net.core(pair_across)]
        own_pairs, pair_full = project(net.starts, turned_one, cosine, sine, pair_pieces, 640, KV_HEADS, 1.0)
        sent = [own_pairs[:, m * rows : m * rows + block] for m in batches]
        across = [net.x(part) for part in sent]
        across[0], turned_q = bind((across[0], turned_one))
        query_across = after(query_across, sent[1])
        query_pieces = [query_weight, query_across, net.core(query_weight), net.core(query_across)]
        pairs = [[sent[0], across[0], net.core(sent[0]), net.core(across[0])]]
        query, query_full = project(net.starts, turned_q, cosine, sine, query_pieces, 640, HEADS, HEAD_DIM**-0.5)
        eighths = [net.feed_eighth(after(part, across[0])) for part in feed_cores]
        moved = net.core(after(upstream, across[0]))
        upstream_all = [(upstream, m) for m in batches] + [(moved, m) for m in batches]
        turned_other = net.core(after(turned_one, across[0]))
        output_across = net.x(after(output_weight, across[0]))
        mixed_0, log_0 = attend(gap, query, pairs[0], own_pairs, micro, 0)
        mixed_0, output_across, across[1], eighth_0 = bind((mixed_0, output_across, across[1], eighths[0]))
        feed_parts = [net.feed_parts(feed_cores[0], eighth_0)]
        pairs.append([sent[1], across[1], net.core(sent[1]), net.core(across[1])])
        feed_cores += [core_of(1, mixed_0), core_of(2, mixed_0)]
        eighth_1, eighth_2 = [net.feed_eighth(part) for part in feed_cores[1:]]
        output_pieces = [output_weight, output_across, net.core(output_weight), net.core(output_across)]
        mixed_1, log_1 = attend(after(gap, mixed_0), query, pairs[1], own_pairs, micro, 1)
        mixed_1, eighth_1, eighth_2, *output_pieces[2:] = bind((mixed_1, eighth_1, eighth_2, *output_pieces[2:]))
        feed_parts += [net.feed_parts(feed_cores[1], eighth_1), net.feed_parts(feed_cores[2], eighth_2)]
        mixed, log_total = [mixed_0, mixed_1], [log_0, log_1]
        mixed_all = mixed + [net.core(value) for value in mixed]
        middle_0, normed_0, output_full = merge(
            net.starts, after(mixed_0, mixed_1), source, 0, gain_two, output_pieces
        )
        middle_1, normed_1 = merge(net.starts, mixed_1, source, 1, gain_two, [output_full])
        middle, normed_two = [middle_0, middle_1], [normed_0, normed_1]
        normed_all = [(value, 0) for value in normed_two] + [(net.core(value), 0) for value in normed_two]
    else:
        own_pairs, pair_full = project(net.starts, turned_one, cosine, sine, pair_pieces, 640, KV_HEADS, 1.0)
        pairs = [list(net.gather_pairs(own_pairs[:, m * rows : m * rows + block])) for m in batches]
        query_pieces = net.pieces(query_weight)
        query, query_full = project(net.starts, turned_one, cosine, sine, query_pieces, 640, HEADS, HEAD_DIM**-0.5)
        feed_parts = [net.pieces(jnp.stack(feed_shards))]
        output_pieces = net.pieces(output_weight)
        mixed, log_total, middle, normed_two = [], [], [], []
        for m in batches:
            mixed_m, log_m = attend(gap, query, pairs[m], own_pairs, micro, m)
            middle_m, normed_m, output_full = merge(net.starts, mixed_m, source, m, gain_two, output_pieces)
            mixed.append(mixed_m)
            log_total.append(log_m)
            middle.append(middle_m)
            normed_two.append(normed_m)
        normed_all = [(value, 0) for value in normed_two]
        upstream_all = [(upstream, m) for m in batches]

    backs = [[] for _ in batches]
    hids, downs, feed_terms, ones = [], [], [], []
    starts = net.feed_starts
    for k, parts in enumerate(feed_parts):
        split = ((0, 1), (2,)) if fast and k == 1 else ((0, 1, 2),)
        grads, backs_here, hid, down = feed(
            starts, net.left_starts, normed_all, upstream_all, parts, net.feed_sizes, rows, split
        )
        feed_terms.append(grads)
        if fast and k == 2:
            settled = settle(ones[:2], *backs_here, hid)
            backs_here, hid = settled[:-1], settled[-1]
        for m in batches:
            backs[m].append(backs_here[m])
            if fast:
                backs[m].append(net.core(backs_here[micro + m]))
        if fast:
            grads = [grad.reshape(-1, grad.shape[-1]) for grad in grads]
            ones += [Chain(net, grads[j], grads[len(split) + j], len(names)) for j, names in enumerate(split)]
        hids.append(hid)
        downs.append(down)
        starts = after(net.feed_starts, hid)
        if fast and k == 0:
            prompt = jnp.concatenate(
                [turned_one[:, m * rows : m * rows + block] for m in batches], axis=1
            )
            prompt_across = net.x(after(prompt, normed_two[-1]))
            starts, prompt_across = bind((starts, prompt_across))
            prompts = [prompt, prompt_across, net.core(prompt), net.core(prompt_across)]
            ones[0].move()
        elif fast and k == 1:
            (starts,) = settle(ones[:1], starts)
            (starts,) = advance(ones[:1], starts)
            ones[1].move()
    size = net.feed_sizes[0]

    def back_of(m, grad_mixed, low, high):
        return attend_back(
            gap, cosine, sine, key_cosine, key_sine, query, mixed[m], grad_mixed, log_total[m], pairs[m], own_pairs, micro, m, low, high
        )

    def pair_grads(summed, own_terms):
        return jnp.concatenate([summed.astype(BF), own_terms], axis=-1).reshape(2 * pair_width, rows)

    def finish_of(m, dmid, grad_query, grad_pairs):
        return finish(source, m, gain_one, dmid, grad_query, grad_pairs, query_full, pair_full)

    if fast:
        lefts_one = [(turned_one, 0), (turned_one, 1), (turned_other, 0), (turned_other, 1)]
        lefts_mixed = [(value, 0) for value in mixed_all]
        part_1, part_2, part_3, part_4 = ones

        def split(value, axis):
            size = value.shape[axis] // 2
            return [lax.dynamic_slice_in_dim(value, at * size, size, axis) for at in (net.c, 1 - net.c)]

        middle_0, first = advance([part_2, part_3], after(middle[0], backs[0][-1]), part_1.total())
        first = net.z_sum(first)
        def kind(value, which):
            return lax.dynamic_index_in_dim(value, which, value.ndim - 4, keepdims=False)

        def pairs_out(terms, own):
            extra = jnp.concatenate([kind(terms[:2], 1 - net.c), kind(own, 1 - net.c)[None]], axis=0)
            return net.core(terms[2:]), net.core(extra)

        def pairs_chip(terms, own, away, extra):
            mine = kind(terms, net.c).astype(F32)
            theirs = jnp.concatenate([kind(away, net.c), extra[:2]], axis=0).astype(F32)
            return (mine + theirs).astype(BF).reshape(4, pair_width, block), [
                value.reshape(pair_width, block) for value in (kind(own, net.c), extra[2])
            ]

        dmid_0, mixed_0 = unmerge(middle_0, upstream, 0, gain_two, output_full, backs[0])
        theirs = output(hids, [downs[0], downs[1], after(downs[2], mixed_0)], [], [], micro, rows)
        mixed_0, theirs = settle([part_2, part_3], mixed_0, theirs)
        theirs = net.core(theirs)
        (mixed_0,) = advance([part_3, part_4], mixed_0)
        query_0, terms_0, own_0 = back_of(0, mixed_0, 0, KV_HEADS)
        query_0, terms_0, theirs, first = settle([part_3], query_0, terms_0, theirs, first)
        away_0, extra_0 = pairs_out(terms_0, own_0)
        second = jnp.concatenate([part_2.total(), part_3.total()], axis=0)
        halves_0 = split(after(dmid_0, query_0), 1)
        second, middle_1 = bind((second, after(middle[1], query_0)))
        second = net.z_sum(second)
        dmid_1, mixed_1 = unmerge(middle_1, upstream, 1, gain_two, output_full, backs[1])
        halves_1 = split(dmid_1, 1)
        mixed_1, moved_0, moved_1, away_0, extra_0 = settle(
            [part_4], mixed_1, halves_0[1], halves_1[1], away_0, extra_0
        )
        kept_0 = (terms_0[:2].astype(F32) + away_0.astype(F32)).astype(BF)
        mixed_1, moved_0, moved_1, out_0 = advance([part_4], mixed_1, moved_0, moved_1, kept_0[1])
        got_0 = net.x(out_0)
        dmid_halves = [halves_0[0], halves_1[0], net.core(moved_0), net.core(moved_1)]
        query_1, terms_1, own_1 = back_of(1, mixed_1, 0, 3)
        output_terms = grad_terms(
            net.left_starts, lefts_mixed, [after(value, query_1) for value in dmid_halves], False, size, 640
        )

        query_1, got_0, *output_terms = settle([part_4], query_1, got_0, *output_terms)
        blocks_0, owns_0 = pairs_chip(terms_0, own_0, away_0, extra_0)
        chain_o = Chain(net, *output_terms)
        mixed_1, third, blocks_0 = advance([chain_o], after(mixed_1, query_1), part_4.total(), blocks_0)
        third = net.z_sum(third, (1, 0))
        got_1st = net.deal(after(first, mixed_1))
        query_1b, terms_1b, own_1b = back_of(1, mixed_1, 3, KV_HEADS)

        query_1b, second = settle([chain_o], query_1b, second)
        terms_1 = jnp.concatenate([terms_1, terms_1b], axis=2)
        own_1 = jnp.concatenate([own_1, own_1b], axis=1)
        grad_query = [query_0, jnp.concatenate([query_1, query_1b], axis=0)]
        halves = [split(value, 0) for value in grad_query]
        moved_0, moved_1, terms_1 = bind((halves[0][1], halves[1][1], terms_1))
        away_1, extra_1 = pairs_out(terms_1, own_1)
        query_halves = [halves[0][0], halves[1][0], net.core(moved_0), net.core(moved_1)]
        (out_o,) = bind((chain_o.ready(),))
        away_1, extra_1, out_o, *settled = bind((away_1, extra_1, out_o, *query_halves, *got_1st))
        query_halves, got_1st = settled[:4], settled[4:]
        kept_1 = (terms_1[:2].astype(F32) + away_1.astype(F32)).astype(BF)
        blocks_1, owns_1 = pairs_chip(terms_1, own_1, away_1, extra_1)
        out_1, blocks_1, chain_o.out = bind((kept_1[1], blocks_1, out_o))
        chain_o.move()
        got_1 = net.x(out_1)
        got_2 = net.deal(after(second, out_1))
        arrays = [turned_one, turned_other, *prompts, *query_halves, blocks_0, *owns_0, blocks_1, *owns_1]
        steps_query = [(m // 2, (m % 2) * rows, 6 + m, None) for m in range(4)]
        steps_pair = []
        for m in batches:
            steps_pair += [(2 + j, m * block, 10 + 3 * m, j) for j in range(4)]
            steps_pair += [(j, m * rows + block, 11 + 3 * m + j, None) for j in range(2)]
        query_terms = joint_terms(
            net.left_starts, arrays, [steps_query, steps_pair], [head_width // 2, pair_width], size
        )
        got_1, *query_terms = bind((got_1, *query_terms))
        chain_q = Chain(net, *query_terms)
        (query_0,) = advance([chain_q], query_0)
        grad_pairs = [
            pair_grads(kept[0].astype(F32) + got.astype(F32), own)
            for kept, got, own in ((kept_0, got_0, own_0), (kept_1, after(got_1, query_0), own_1))
        ]
        source_0 = finish_of(0, dmid_0, query_0, grad_pairs[0])
        source_0, third = bind((source_0, third))
        source_1 = finish_of(1, dmid_1, after(grad_query[1], source_0), grad_pairs[1])
        source_0, source_1, *got_2 = settle([chain_q, chain_o], source_0, source_1, *got_2)
        (theirs,) = advance([chain_q], theirs)
        chain_o.got = after(chain_o.got, theirs)
        (theirs,) = advance([chain_o], theirs)
        layer_out = output(hids, downs, [theirs], middle, 0, rows)
        (layer_out,) = settle([chain_q, chain_o], layer_out)
        (held_q,) = bind((chain_q.ready(),))
        held_q, first, second, third = bind((held_q, first, second, third))
        chain_o.got = after(chain_o.got, held_q)
        held_q = net.z_sum(held_q)
        chain_o.ready()
        chain_o.move()
        got_3 = net.deal(third)
        mine_1, theirs_1 = net.dealt(first, got_1st)
        mine_2, theirs_2 = net.dealt(second, got_2)
        mine_3, theirs_3 = net.dealt(third, got_3)
        gate_grad, up_grad, down_grad, sums = widen(
            net.c[None].astype(jnp.int32),
            [mine_1, mine_2, mine_3],
            [theirs_1, theirs_2, theirs_3],
            gate_weight,
            up_weight,
        )
        grad_source = jnp.stack([source_0, source_1])
        sums, grad_source = settle([chain_o], sums, grad_source)
        held_o = chain_o.total()
        got_o = net.deal(held_o)
        held_q, *got_o = bind((held_q, *got_o))
        got_q = net.deal(held_q)
        output_rows = [value[0] for value in net.dealt(held_o, got_o)]
        query_rows = [value[0] for value in net.dealt(held_q, got_q)]
        pair_rows = [value[:, head_width // 2 :] for value in query_rows]
        query_rows = [value[:, : head_width // 2] for value in query_rows]

        def columns_of(rows_of):
            mine, theirs = (value.astype(F32) for value in rows_of)
            return jnp.where(net.c == 0, mine, theirs), jnp.where(net.c == 0, theirs, mine)

        output_grad = jnp.concatenate(columns_of(output_rows), axis=1)
        query_grad = jnp.concatenate(columns_of(query_rows), axis=1)
        key_grad, value_grad = columns_of(pair_rows)
        down_grad = down_grad.T
        feed_gain_grad = sums[:, 0] / feed_gain.astype(F32)
    else:
        grad_query, grad_pairs, dmids = [], [], []
        for m in batches:
            dmid, grad_mixed = unmerge(middle[m], upstream, m, gain_two, output_full, backs[m])
            query_m, terms, own = back_of(m, grad_mixed, 0, KV_HEADS)
            dmids.append(dmid)
            grad_query.append(query_m)
            grad_pairs.append(pair_grads(net.sum_pairs(terms), own))
        lefts_one = [(turned_one, m) for m in batches]
        lefts_mixed = [(value, 0) for value in mixed]
        terms = [
            grad_terms(net.left_starts, lefts_mixed, dmids, False, size, 640),
            grad_terms(net.left_starts, lefts_one, grad_query, True, size, 640),
            grad_terms(net.left_starts, lefts_one, grad_pairs, True, size, 640),
        ]
        output_grad, query_grad, pair_grad = [net.whole_sum(term[0], 0) for term in terms]
        key_grad, value_grad = pair_grad[:, :pair_width], pair_grad[:, pair_width:]
        feed_grads = net.whole_sum(feed_terms[0][0].reshape(3, width, hidden_width), 1)
        gate_grad, up_grad, down_grad = feed_grads[0], feed_grads[1], feed_grads[2].T
        layer_out = output(hids, downs, [], middle, 0, rows)
        grad_source = jnp.stack([finish_of(m, dmids[m], grad_query[m], grad_pairs[m]) for m in batches])

    def gain_grad(gain, *both):
        terms = sum(jnp.sum(weight.astype(F32) * grad, axis=1) for weight, grad in both)
        return terms / gain.astype(F32)

    attention_gain_grad = gain_grad(
        attention_gain, (query_weight, query_grad), (key_weight, key_grad), (value_weight, value_grad)
    )
    if not fast:
        feed_gain_grad = gain_grad(feed_gain, (gate_weight, gate_grad), (up_weight, up_grad))
    return (
        layer_out.reshape(tokens.shape),
        grad_source,
        query_grad,
        key_grad,
        value_grad,
        output_grad,
        attention_gain_grad,
        gate_grad,
        up_grad,
        down_grad,
        feed_gain_grad,
    )


def solution(mesh):
    return jax.shard_map(
        on_device,
        mesh=mesh,
        in_specs=(
            P(None, ("rep", "shard"), None),
            P(None, ("rep", "shard"), None),
            P(None, "rep", None),
            P("shard", None),
            P("shard", None),
            P("shard", None),
            P("shard", None),
            P("shard"),
            P("shard", None),
            P("shard", None),
            P(None, "shard"),
            P("shard"),
        ),
        out_specs=(
            P(None, ("rep", "shard"), None),
            P(None, ("rep", "shard"), None),
            P("shard", None),
            P("shard", None),
            P("shard", None),
            P("shard", None),
            P("shard"),
            P("shard", None),
            P("shard", None),
            P(None, "shard"),
            P("shard"),
        ),
        check_vma=False,
    )
```
